32 devices in a mesh: seg: 8 (over y, x, core), fft: 4 (over z).
Axes of the slice: x: 2, y: 2, z: 4, core: 2. Of those that a mesh axis runs over, the one named last changes fastest.
Arguments:
- voltage: float32 [8, 2, 256, 4096], P('seg', None, None, 'fft'), may hold values from -6 to 6
- chirp_phase: float32 [2, 512, 4096], P(None, 'fft'), may hold values from -3.140625 to 3.140625
Outputs:
- dedispersed: float32 [8, 2, 256, 4096], P('seg', None, None, 'fft')
The draws below stay inside these ranges and needn't reach their ends.
All inputs are finite; a program needn't handle non-finite values.
Results may differ from the reference program's by a relative error of at most 0.0001.
Values sent between devices are 32-bit elements; how exact they have to be, the bound alone decides.
No kernel may reach another device: no remote copies, remote signals or barrier semaphores. Data moves between devices by JAX's collectives and lax.ppermute only.
A program may use at most 128 MiB of HBM per device.

```python
import jax
import jax.numpy as jnp
from jax import lax

M = 8388608
A = 1024
B = 4096
L = 2097152
SEGS = 8


def block_scale(key, extent, cuts, least, top_value):
    def one(position, blocks):
        heights = jax.random.uniform(jax.random.fold_in(jax.random.fold_in(key, 6), position), (blocks,), jnp.float32, least / len(cuts), top_value / len(cuts))
        return jnp.repeat(jnp.exp(heights), extent[position] // blocks).reshape((-1,) + (1,) * (len(extent) - position - 1))

    loudness = one(*cuts[0])
    for cut in cuts[1:]:
        loudness = loudness * one(*cut)
    return loudness


def scatter_about(own_key, shape, width, reach, pieces=(), held_as=jnp.bfloat16):
    gain = block_scale(own_key, shape, pieces, -0.22, 0.18) if pieces else 1.0
    result = jax.random.normal(own_key, shape, jnp.float32) * width * gain
    return jnp.minimum(jnp.maximum(result, -reach), reach).astype(held_as)


def setup_inputs(seed: int = 0) -> dict:
    streams_of = jax.random.split(jax.random.key(seed), 3)
    voltage = scatter_about(streams_of[0], (SEGS, 2, A // 4, B), 1.0, 6.0, ((0, 8), (3, 4)), jnp.float32)
    chirp_phase = jnp.clip(jax.random.uniform(streams_of[1], (2, A // 2, B), jnp.float32, -3.140625, 3.140625), -3.140625, 3.140625)
    return {"voltage": voltage, "chirp_phase": chirp_phase}


def unfold_chirp(chirp_phase):
    natural = jnp.concatenate([chirp_phase[0], chirp_phase[1, :1], jnp.flip(chirp_phase[1, 1:], axis=0)], axis=0)
    return jnp.transpose(natural).reshape(-1)


def reference(voltage, chirp_phase):
    phase_flat = unfold_chirp(chirp_phase)
    chirp_real = jnp.cos(phase_flat)
    chirp_imag = jnp.sin(phase_flat)
    keep_bins = jnp.arange(M // 2) > 0

    def advance(pending, samples):
        series = jnp.transpose(samples, (1, 2, 0)).reshape(L)
        padded = jnp.concatenate([series, jnp.zeros((M - L,), series.dtype)])
        spectrum = jnp.fft.rfft(padded)[: M // 2]
        spec_real = jnp.real(spectrum)
        spec_imag = jnp.imag(spectrum)
        filt_real = jnp.where(keep_bins, spec_real * chirp_real - spec_imag * chirp_imag, 0.0)
        filt_imag = jnp.where(keep_bins, spec_real * chirp_imag + spec_imag * chirp_real, 0.0)
        closing = jnp.zeros((1,), filt_real.dtype)
        filtered = lax.complex(jnp.concatenate([filt_real, closing]), jnp.concatenate([filt_imag, closing]))
        blocks = jnp.fft.irfft(filtered, n=M).reshape(4, L)
        emitted = blocks[0] + pending[0]
        carried = jnp.stack([pending[1] + blocks[1], pending[2] + blocks[2], blocks[3]])
        return carried, emitted

    start = jnp.zeros((3, L), jnp.float32)
    leftover, emitted = lax.scan(advance, start, voltage)
    shaped = emitted.reshape(SEGS, A // 4, B, 2)
    return jnp.transpose(shaped, (0, 3, 1, 2)).astype(jnp.float32)
```

```python
import functools
import math

import jax
import jax.numpy as jnp
import ml_dtypes
import numpy as np
from jax import lax
from jax.experimental import pallas as pl
from jax.experimental.pallas import tpu as pltpu
from jax.sharding import PartitionSpec as P

LANES = 128
SUB = 8
VMEM = 50 * 1024 * 1024


def passed_along(shard, axis, by):
    length = lax.axis_size(axis)
    pairs = [(i, i + by) for i in range(length) if 0 <= i + by < length]
    return lax.ppermute(shard, axis, pairs)


def turn(products, period):
    angles = np.mod(products, period).astype(np.float64) * (-2.0 * math.pi / period)
    return np.cos(angles), np.sin(angles)


def halves(table):
    high = table.astype(ml_dtypes.bfloat16)
    low = (table - high.astype(np.float64)).astype(ml_dtypes.bfloat16)
    return high, low


def split(values):
    high = values.astype(jnp.bfloat16)
    low = (values - high.astype(jnp.float32)).astype(jnp.bfloat16)
    return high, low


def dot(left, right):
    return jnp.dot(left, right, preferred_element_type=jnp.float32)


def dot3(left_high, left_low, right_high, right_low):
    return dot(left_high, right_high) + (dot(left_high, right_low) + dot(left_low, right_high))


def scale_by(value, cos, sin):
    re, im = value
    near = 1e-12
    if abs(sin) < near:
        return value if cos > 0 else (-re, -im)
    if abs(cos) < near:
        return (-im, re) if sin > 0 else (im, -re)
    if abs(abs(cos) - abs(sin)) < near:
        size = abs(cos)
        first = re if cos > 0 else -re
        second = im if cos > 0 else -im
        third = im if sin > 0 else -im
        fourth = re if sin > 0 else -re
        return (first - third) * size, (second + fourth) * size
    return re * cos - im * sin, re * sin + im * cos


def plus(left, right):
    return left[0] + right[0], left[1] + right[1]


def minus(left, right):
    return left[0] - right[0], left[1] - right[1]


def small_dft(values, sign):
    count = len(values)
    if count == 1:
        return values
    if count == 2:
        return [plus(values[0], values[1]), minus(values[0], values[1])]
    if count == 4:
        even_sum, even_gap = plus(values[0], values[2]), minus(values[0], values[2])
        odd_sum, odd_gap = plus(values[1], values[3]), minus(values[1], values[3])
        turned = scale_by(odd_gap, 0.0, float(sign))
        return [plus(even_sum, odd_sum), plus(even_gap, turned), minus(even_sum, odd_sum), minus(even_gap, turned)]
    radix = 4 if count == 32 else 2
    part = count // radix
    pieces = [small_dft(values[i::radix], sign) for i in range(radix)]
    result = [None] * count
    for k in range(part):
        column = []
        for i in range(radix):
            angle = sign * 2.0 * math.pi * i * k / count
            column.append(scale_by(pieces[i][k], math.cos(angle), math.sin(angle)))
        for q, value in enumerate(small_dft(column, sign)):
            result[k + part * q] = value
    return result


def spread_kernel(x0, x3, x2, x1, table_high, table_low, turns, phases, out, high, low):
    quarter, width = x0.shape[2], x0.shape[3]

    @pl.when(pl.program_id(0) == 0)
    def _():
        for block, ref in enumerate((x0, x3, x2, x1)):
            for parity in range(2):
                first, second = split(ref[0, parity])
                rows = pl.ds(block * quarter, quarter)
                high[rows, pl.ds(parity * width, width)] = first
                low[rows, pl.ds(parity * width, width)] = second

    sums = dot3(table_high[0], table_low[0], high[...], low[...])
    slots = sums.shape[0] // 2
    turn_re, turn_im = turns[0, 0], turns[0, 1]
    for parity in range(2):
        ph_re, ph_im = phases[0, 2 * parity], phases[0, 2 * parity + 1]
        re = sums[:slots, parity * width : (parity + 1) * width]
        im = sums[slots:, parity * width : (parity + 1) * width]
        w_re = turn_re * ph_re - turn_im * ph_im
        w_im = turn_re * ph_im + turn_im * ph_re
        out[0, parity, 0] = re * w_re - im * w_im
        out[0, parity, 1] = re * w_im + im * w_re


def middle_kernel(chunks, with_extra, device, *refs):
    pieces = refs[:chunks]
    chirp, twist, tab_high, tab_low, extra_turn, out = refs[chunks : chunks + 6]
    data, grid_a, kept = refs[chunks + 6 :]
    groups = pieces[0].shape[0]
    tiles = pieces[0].shape[4] // LANES
    per_group = tiles * chunks
    points = groups * per_group
    step = pl.program_id(0)
    is_first = device[0] == 0
    if with_extra:
        on_extra = jnp.logical_and(is_first, step == 0)
        on_zero = jnp.logical_and(is_first, step == 1)
        active = jnp.logical_or(is_first, step > 0)
    rows = points * SUB

    def place(j):
        group, rest = divmod(j, per_group)
        chunk, tile = divmod(rest, tiles)
        return pieces[chunk], group, pl.ds(tile * LANES, LANES)

    def outlet(j):
        group, tile = divmod(j, per_group)
        return group, pl.ds(tile * LANES, LANES)

    def load_plain():
        for j in range(points):
            ref, group, lanes = place(j)
            for parity in range(2):
                for part in range(2):
                    data[parity, part, j] = ref[group, parity, part, :, lanes]

    def load_extra():
        for j in range(points):
            ref, group, lanes = place(j)
            for parity in range(2):
                value = ref[group, parity, 1, :, lanes]
                for part in range(2):
                    data[parity, part, j] = value * extra_turn[parity, part, pl.ds(j, 1)]

    def run():
        spectra = []
        for parity in range(2):
            values = [(data[parity, 0, j], data[parity, 1, j]) for j in range(points)]
            for k, (re, im) in enumerate(small_dft(values, -1)):
                w_re, w_im = twist[parity, 0, pl.ds(k, 1)], twist[parity, 1, pl.ds(k, 1)]
                grid_a[pl.ds(k * SUB, SUB), pl.ds(0, LANES)] = re * w_re - im * w_im
                grid_a[pl.ds(k * SUB, SUB), pl.ds(LANES, LANES)] = re * w_im + im * w_re
            high, low = split(grid_a[...])
            spectra.append(dot3(high, low, tab_high[parity], tab_low[parity]))
        even, odd = spectra
        upper, lower = even + odd, even - odd
        u_re, u_im = upper[:, :LANES], upper[:, LANES:]
        l_re, l_im = lower[:, :LANES], lower[:, LANES:]
        c1r, c1i, c2r, c2i = (chirp[0, n].reshape(rows, LANES) for n in range(4))
        f_re, f_im = u_re * c1r - u_im * c1i, u_re * c1i + u_im * c1r
        g_re, g_im = l_re * c2r + l_im * c2i, l_im * c2r - l_re * c2i
        sides = ((f_re + g_re, f_im + g_im), (f_re - g_re, f_im - g_im))
        for parity in range(2):
            high, low = split(jnp.concatenate(sides[parity], axis=1))
            grid_a[...] = dot3(high, low, tab_high[2 + parity], tab_low[2 + parity])
            values = []
            for k in range(points):
                re = grid_a[pl.ds(k * SUB, SUB), pl.ds(0, LANES)]
                im = grid_a[pl.ds(k * SUB, SUB), pl.ds(LANES, LANES)]
                w_re, w_im = twist[parity, 0, pl.ds(k, 1)], twist[parity, 1, pl.ds(k, 1)]
                values.append((re * w_re + im * w_im, im * w_re - re * w_im))
            for j, (re, im) in enumerate(small_dft(values, 1)):
                group, lanes = outlet(j)
                out[group, parity, 0, :, lanes] = re
                out[group, parity, 1, :, lanes] = im

    if not with_extra:
        load_plain()
        run()
        return

    @pl.when(on_extra)
    def _():
        load_extra()

    @pl.when(step > 0)
    def _():
        load_plain()

    keep = lax.broadcasted_iota(jnp.int32, (SUB, LANES), 0) > 0

    @pl.when(on_zero)
    def _():
        for parity in range(2):
            for j in range(points):
                data[parity, 1, j] = jnp.where(keep, data[parity, 1, j], 0.0)

    @pl.when(active)
    def _():
        run()

    @pl.when(on_extra)
    def _():
        for parity in range(2):
            for j in range(points):
                group, lanes = outlet(j)
                w_re, w_im = extra_turn[parity, 0, pl.ds(j, 1)], extra_turn[parity, 1, pl.ds(j, 1)]
                kept[parity, j] = out[group, parity, 0, :, lanes] * w_re + out[group, parity, 1, :, lanes] * w_im

    @pl.when(on_zero)
    def _():
        for parity in range(2):
            for j in range(points):
                group, lanes = outlet(j)
                out[group, parity, 1, :, lanes] = jnp.where(keep, out[group, parity, 1, :, lanes], kept[parity, j])


def gather_kernel(chunks, *refs):
    pieces = refs[:chunks]
    turns, phases, table_high, table_low, out, high, low = refs[chunks:]
    groups, slots, width = pieces[0].shape[0], pieces[0].shape[3], pieces[0].shape[4]
    row = 0
    for chunk, ref in enumerate(pieces):
        own = pl.ds(chunk * slots, slots)
        for group in range(groups):
            t_re, t_im = turns[group, 0, own], turns[group, 1, own]
            for parity in range(2):
                ph_re, ph_im = phases[group, 2 * parity, own], phases[group, 2 * parity + 1, own]
                w_re = t_re * ph_re - t_im * ph_im
                w_im = t_re * ph_im + t_im * ph_re
                re, im = ref[group, parity, 0], ref[group, parity, 1]
                lanes = pl.ds(parity * width, width)
                for part, value in enumerate((re * w_re + im * w_im, im * w_re - re * w_im)):
                    first, second = split(value)
                    high[pl.ds(row + part * slots, slots), lanes] = first
                    low[pl.ds(row + part * slots, slots), lanes] = second
            row += 2 * slots
    sums = dot3(table_high[...], table_low[...], high[...], low[...])
    for parity in range(2):
        out[0, parity] = sums[:, parity * width : (parity + 1) * width]


def whole(shape):
    return pl.BlockSpec(shape, lambda i: (0,) * len(shape))


def params():
    return pltpu.CompilerParams(vmem_limit_bytes=VMEM, dimension_semantics=("arbitrary",))


def estimate(flops, size):
    return pl.CostEstimate(flops=int(flops), bytes_accessed=int(size), transcendentals=0)


def per_device(col_chunks, row_chunks, voltage, chirp_phase):
    groups = lax.axis_size("fft")
    device = lax.axis_index("fft")
    quarter, width = voltage.shape[2], voltage.shape[3]
    row_count = 4 * quarter
    half = row_count // 2
    columns = width * groups
    slots = half // groups
    total = row_count * columns
    first_len = columns // LANES
    col_width = width // col_chunks
    row_slots = slots // row_chunks
    blocks = slots // SUB
    step_blocks = blocks // row_chunks

    rows = np.arange(half)
    times = np.arange(row_count)
    cos, sin = turn(rows[:, None] * times[None, :], row_count)
    sin[0] = np.where(times % 2 == 0, 1.0, -1.0)
    spread_table = np.stack([cos, sin]).reshape(2, groups, slots, row_count)
    spread_high, spread_low = halves(spread_table.transpose(1, 0, 2, 3).reshape(groups, 2 * slots, row_count))

    cos, sin = turn(rows[:, None] * np.arange(width)[None, :], total)
    turns = np.stack([cos, sin]).reshape(2, groups, slots, width).transpose(1, 0, 2, 3).astype(np.float32)

    zs = np.arange(groups)[:, None]
    even_phase = np.stack(turn(rows[None, :] * (zs * width), total), axis=1)
    odd_phase = np.stack(turn(rows[None, :] * (2 * zs * width + 1), 2 * total), axis=1)
    phase_table = np.concatenate([even_phase, odd_phase], axis=1).reshape(groups, 4, groups, slots)
    phase_table = phase_table.transpose(0, 2, 1, 3)[..., None].astype(np.float32)
    phases = lax.dynamic_index_in_dim(jnp.asarray(phase_table), device, 0, keepdims=False)

    keys = np.arange(first_len)
    lanes = np.arange(LANES)
    twist = np.stack(
        [
            np.stack(turn(keys[:, None] * lanes[None, :], columns)),
            np.stack(turn(keys[:, None] * (2 * lanes[None, :] + 1), 2 * columns)),
        ]
    ).astype(np.float32)
    tables = []
    for cos, sin in (
        turn(lanes[:, None] * lanes[None, :], LANES),
        turn((2 * lanes[:, None] + 1) * lanes[None, :], 2 * LANES),
    ):
        tables.append(np.block([[cos, sin], [-sin, cos]]))
    tables = np.stack(tables + [table.T for table in tables])
    tab_high, tab_low = halves(tables)
    every = (LANES * keys[:, None] + lanes[None, :])
    extra_turn = np.stack(
        [np.stack(turn(half * every, total)), np.stack(turn(half * (2 * every + 1), 2 * total))]
    ).astype(np.float32)

    cos, sin = turn(rows[None, :] * np.arange(quarter)[:, None], row_count)
    cos[:, 0] = 0.5
    sin[:, 0] = np.where(np.arange(quarter) % 2 == 0, 0.5, -0.5)
    gather_table = np.stack([cos, sin], axis=1) / total
    gather_table = gather_table.reshape(quarter, 2, groups, row_chunks, row_slots)
    gather_table = gather_table.transpose(0, 3, 2, 1, 4).reshape(quarter, 2 * half)
    gather_high, gather_low = halves(gather_table)

    spread_call = [
        pl.pallas_call(
            spread_kernel,
            grid=(groups,),
            in_specs=[pl.BlockSpec((1, 2, quarter, col_width), lambda d: (0, 0, 0, 0))] * 4
            + [pl.BlockSpec((1, 2 * slots, row_count), lambda d: (d, 0, 0))] * 2
            + [
                pl.BlockSpec((1, 2, slots, col_width), lambda d, c=chunk: (d, 0, 0, c)),
                pl.BlockSpec((1, 4, slots, 1), lambda d: (d, 0, 0, 0)),
            ],
            out_specs=pl.BlockSpec((1, 2, 2, slots, col_width), lambda d: (d, 0, 0, 0, 0)),
            out_shape=jax.ShapeDtypeStruct((groups, 2, 2, slots, col_width), jnp.float32),
            scratch_shapes=[pltpu.VMEM((row_count, 2 * col_width), jnp.bfloat16)] * 2,
            compiler_params=params(),
            cost_estimate=estimate(12 * row_count * row_count * col_width, 16 * row_count * col_width),
            name="spread",
        )
        for chunk in range(col_chunks)
    ]

    received = []
    for chunk in range(col_chunks):
        own = voltage[..., chunk * col_width : (chunk + 1) * col_width]
        one = passed_along(own, "seg", 1)
        two = passed_along(one, "seg", 1)
        three = passed_along(two, "seg", 1)
        sent = spread_call[chunk](own, three, two, one, spread_high, spread_low, turns, phases)
        received.append(lax.all_to_all(sent, "fft", split_axis=0, concat_axis=0, tiled=True))

    is_first = device == 0
    digits = chirp_phase.reshape(2, slots, LANES, first_len)
    near, far = digits[0], digits[1, :, ::-1, ::-1]
    zero_row = jnp.roll(jnp.flip(chirp_phase[0, 0]), 1).reshape(LANES, first_len)
    at_zero = jnp.logical_and(is_first, jnp.arange(slots) == 0)[:, None, None]
    extra = jnp.pad(jnp.stack([digits[1, 0], far[0]])[:, None], ((0, 0), (0, SUB - 1), (0, 0), (0, 0)))
    far = jnp.where(at_zero, zero_row[None], far)
    angles = jnp.concatenate([extra, jnp.stack([near, far])], axis=1)
    angles = angles.reshape(2, blocks + 1, SUB, LANES, first_len).transpose(1, 0, 4, 2, 3)
    dead = (
        (lax.broadcasted_iota(jnp.int32, angles.shape, 0) == 1)
        & (lax.broadcasted_iota(jnp.int32, angles.shape, 2) == 0)
        & (lax.broadcasted_iota(jnp.int32, angles.shape, 3) == 0)
        & (lax.broadcasted_iota(jnp.int32, angles.shape, 4) == 0)
        & is_first
    )
    chirp = jnp.stack([jnp.where(dead, 0.0, jnp.cos(angles)), jnp.where(dead, 0.0, jnp.sin(angles))], axis=2)
    chirp = chirp.reshape(blocks + 1, 4, first_len, SUB, LANES)

    device_word = device.astype(jnp.int32).reshape(1)
    returned = []
    for chunk in range(row_chunks):
        with_extra = chunk == 0
        base = chunk * step_blocks
        lag = 1 if with_extra else 0

        def inlet(i, base=base, lag=lag):
            return (0, 0, 0, base + jnp.maximum(i - lag, 0), 0)

        def outlet(i, lag=lag):
            return (0, 0, 0, jnp.maximum(i - lag, 0), 0)

        def chirp_at(i, base=base, lag=lag):
            return (base + 1 - lag + i, 0, 0, 0, 0)

        sent = pl.pallas_call(
            functools.partial(middle_kernel, col_chunks, with_extra),
            grid=(step_blocks + lag,),
            in_specs=[pl.BlockSpec(memory_space=pltpu.SMEM)]
            + [pl.BlockSpec((groups, 2, 2, SUB, col_width), inlet)] * col_chunks
            + [
                pl.BlockSpec((1, 4, first_len, SUB, LANES), chirp_at),
                whole(twist.shape),
                whole(tab_high.shape),
                whole(tab_low.shape),
                whole(extra_turn.shape),
            ],
            out_specs=pl.BlockSpec((groups, 2, 2, SUB, width), outlet),
            out_shape=jax.ShapeDtypeStruct((groups, 2, 2, row_slots, width), jnp.float32),
            scratch_shapes=[
                pltpu.VMEM((2, 2, first_len, SUB, LANES), jnp.float32),
                pltpu.VMEM((first_len * SUB, 2 * LANES), jnp.float32),
                pltpu.VMEM((2, first_len, SUB, LANES), jnp.float32),
            ],
            compiler_params=params(),
            cost_estimate=estimate(2e9 / row_chunks, 25e6 / row_chunks),
            name="middle",
        )(device_word, *received, chirp, twist, tab_high, tab_low, extra_turn)
        returned.append(lax.all_to_all(sent, "fft", split_axis=0, concat_axis=0, tiled=True))

    tile = min(width, 2 * LANES)
    return pl.pallas_call(
        functools.partial(gather_kernel, row_chunks),
        grid=(width // tile,),
        in_specs=[pl.BlockSpec((groups, 2, 2, row_slots, tile), lambda c: (0, 0, 0, 0, c))] * row_chunks
        + [
            pl.BlockSpec((groups, 2, slots, tile), lambda c: (0, 0, 0, c)),
            whole((groups, 4, slots, 1)),
            whole(gather_high.shape),
            whole(gather_low.shape),
        ],
        out_specs=pl.BlockSpec((1, 2, quarter, tile), lambda c: (0, 0, 0, c)),
        out_shape=jax.ShapeDtypeStruct((1, 2, quarter, width), jnp.float32),
        scratch_shapes=[pltpu.VMEM((2 * half, 2 * tile), jnp.bfloat16)] * 2,
        compiler_params=params(),
        cost_estimate=estimate(12 * quarter * row_count * width, 20e6),
        name="gather",
    )(*returned, turns, phases, gather_high, gather_low)


def solution(mesh):
    in_specs = (P("seg", None, None, "fft"), P(None, "fft", None))
    out_specs = P("seg", None, None, "fft")
    return jax.shard_map(
        functools.partial(per_device, 4, 4),
        mesh=mesh,
        in_specs=in_specs,
        out_specs=out_specs,
        check_vma=False,
    )
```

```python
import math

import jax
import jax.numpy as jnp
import ml_dtypes
import numpy as np
from jax import lax
from jax.experimental import pallas as pl
from jax.experimental.pallas import tpu as pltpu
from jax.sharding import PartitionSpec as P

LANES = 128
SUB = 8
VMEM = 50 * 1024 * 1024


def turn(products, period):
    angles = np.mod(products, period).astype(np.float64) * (-2.0 * math.pi / period)
    return np.cos(angles), np.sin(angles)


def halves(table):
    high = table.astype(ml_dtypes.bfloat16)
    low = (table - high.astype(np.float64)).astype(ml_dtypes.bfloat16)
    return high, low


def split(values):
    high = values.astype(jnp.bfloat16)
    low = (values - high.astype(jnp.float32)).astype(jnp.bfloat16)
    return high, low


def dot(left, right):
    return jnp.dot(left, right, preferred_element_type=jnp.float32)


def dot3(left_high, left_low, right_high, right_low):
    return dot(left_high, right_high) + (dot(left_high, right_low) + dot(left_low, right_high))


def scale_by(value, cos, sin):
    re, im = value
    near = 1e-12
    if abs(sin) < near:
        return value if cos > 0 else (-re, -im)
    if abs(cos) < near:
        return (-im, re) if sin > 0 else (im, -re)
    if abs(abs(cos) - abs(sin)) < near:
        size = abs(cos)
        first = re if cos > 0 else -re
        second = im if cos > 0 else -im
        third = im if sin > 0 else -im
        fourth = re if sin > 0 else -re
        return (first - third) * size, (second + fourth) * size
    return re * cos - im * sin, re * sin + im * cos


def plus(left, right):
    return left[0] + right[0], left[1] + right[1]


def minus(left, right):
    return left[0] - right[0], left[1] - right[1]


def small_dft(values, sign):
    count = len(values)
    if count == 1:
        return values
    if count == 2:
        return [plus(values[0], values[1]), minus(values[0], values[1])]
    if count == 4:
        even_sum, even_gap = plus(values[0], values[2]), minus(values[0], values[2])
        odd_sum, odd_gap = plus(values[1], values[3]), minus(values[1], values[3])
        turned = scale_by(odd_gap, 0.0, float(sign))
        return [plus(even_sum, odd_sum), plus(even_gap, turned), minus(even_sum, odd_sum), minus(even_gap, turned)]
    radix = 4 if count == 32 else 2
    part = count // radix
    pieces = [small_dft(values[i::radix], sign) for i in range(radix)]
    result = [None] * count
    for k in range(part):
        column = []
        for i in range(radix):
            angle = sign * 2.0 * math.pi * i * k / count
            column.append(scale_by(pieces[i][k], math.cos(angle), math.sin(angle)))
        for q, value in enumerate(small_dft(column, sign)):
            result[k + part * q] = value
    return result


def forward(value_at, twist, tab_high, tab_low, grid):
    spectra = []
    for parity in range(2):
        values = [value_at(parity, j) for j in range(twist.shape[2])]
        for k, (re, im) in enumerate(small_dft(values, -1)):
            w_re, w_im = twist[parity, 0, pl.ds(k, 1)], twist[parity, 1, pl.ds(k, 1)]
            grid[pl.ds(k * SUB, SUB), pl.ds(0, LANES)] = re * w_re - im * w_im
            grid[pl.ds(k * SUB, SUB), pl.ds(LANES, LANES)] = re * w_im + im * w_re
        high, low = split(grid[...])
        spectra.append(dot3(high, low, tab_high[parity], tab_low[parity]))
    even, odd = spectra
    return even + odd, even - odd


def backward(side_ref, parity, twist, tab_high, tab_low, grid, put):
    high, low = split(side_ref[parity])
    grid[...] = dot3(high, low, tab_high[2 + parity], tab_low[2 + parity])
    values = []
    for k in range(twist.shape[2]):
        re = grid[pl.ds(k * SUB, SUB), pl.ds(0, LANES)]
        im = grid[pl.ds(k * SUB, SUB), pl.ds(LANES, LANES)]
        w_re, w_im = twist[parity, 0, pl.ds(k, 1)], twist[parity, 1, pl.ds(k, 1)]
        values.append((re * w_re + im * w_im, im * w_re - re * w_im))
    for j, (re, im) in enumerate(small_dft(values, 1)):
        put(j, re, im)


def spread_kernel(x, table_high, table_low, turns, phases, out):
    count, slots, width = out.shape[0], out.shape[3], out.shape[4]
    first, second = zip(*(split(x[0, parity]) for parity in range(2)))
    high, low = jnp.concatenate(first, axis=1), jnp.concatenate(second, axis=1)
    sums = dot3(table_high[...], table_low[...], high, low).reshape(count, 2, slots, 2 * width)
    turn_re, turn_im = turns[:, 0], turns[:, 1]
    for parity in range(2):
        lanes = slice(parity * width, (parity + 1) * width)
        ph_re, ph_im = phases[:, 2 * parity], phases[:, 2 * parity + 1]
        re, im = sums[:, 0, :, lanes], sums[:, 1, :, lanes]
        w_re = turn_re * ph_re - turn_im * ph_im
        w_im = turn_re * ph_im + turn_im * ph_re
        out[:, parity, 0] = re * w_re - im * w_im
        out[:, parity, 1] = re * w_im + im * w_re


def chirp_kernel(position, chirp, twist, tab_high, tab_low, extra_turn, out, sides, grid, kept):
    step = pl.program_id(0)
    is_first = position[0] == 0
    on_extra = jnp.logical_and(is_first, step == 0)
    on_zero = jnp.logical_and(is_first, step == 1)
    points = twist.shape[2]

    @pl.when(jnp.logical_or(is_first, step > 0))
    def _():
        near_re, near_im, far_re, far_im = (chirp[0, n].reshape(points * SUB, LANES) for n in range(4))
        sides[0, :, pl.ds(0, LANES)] = near_re + far_re
        sides[0, :, pl.ds(LANES, LANES)] = near_im - far_im
        sides[1, :, pl.ds(0, LANES)] = near_re - far_re
        sides[1, :, pl.ds(LANES, LANES)] = near_im + far_im
        for parity in range(2):

            def put(j, re, im, parity=parity):
                out[j, parity, 0] = re
                out[j, parity, 1] = im

            backward(sides, parity, twist, tab_high, tab_low, grid, put)

    @pl.when(on_extra)
    def _():
        for parity in range(2):
            for j in range(points):
                w_re, w_im = extra_turn[parity, 0, pl.ds(j, 1)], extra_turn[parity, 1, pl.ds(j, 1)]
                kept[parity, j] = out[j, parity, 0] * w_re + out[j, parity, 1] * w_im

    @pl.when(on_zero)
    def _():
        keep = lax.broadcasted_iota(jnp.int32, (SUB, LANES), 0) > 0
        for parity in range(2):
            for j in range(points):
                out[j, parity, 1] = jnp.where(keep, out[j, parity, 1], kept[parity, j])


def response_kernel(
    parts, turns_in, phases_in, back_high, back_low, table_high, table_low, turns, phases, out, packed
):
    sources, slots = parts.shape[0], parts.shape[3]
    count, out_slots = out.shape[0], out.shape[4]
    for source in range(sources):
        t_re, t_im = turns_in[source, 0], turns_in[source, 1]
        for parity in range(2):
            ph_re, ph_im = phases_in[source, 2 * parity], phases_in[source, 2 * parity + 1]
            w_re = t_re * ph_re - t_im * ph_im
            w_im = t_re * ph_im + t_im * ph_re
            re, im = parts[source, parity, 0], parts[source, parity, 1]
            lanes = pl.ds(parity * LANES, LANES)
            for part, value in enumerate((re * w_re + im * w_im, im * w_re - re * w_im)):
                rows = pl.ds((2 * source + part) * slots, slots)
                packed[rows, lanes] = value
    first, second = split(packed[...])
    quarter = table_high.shape[1]
    for block in range(4):
        rows = pl.ds(block * quarter, quarter)
        taps = dot3(back_high[rows], back_low[rows], first, second)
        taps_high, taps_low = split(taps)
        sums = dot3(table_high[...], table_low[...], taps_high, taps_low)
        sums = sums.reshape(count, 2, out_slots, 2 * LANES)
        turn_re, turn_im = turns[:, 0], turns[:, 1]
        for parity in range(2):
            lanes = slice(parity * LANES, (parity + 1) * LANES)
            ph_re, ph_im = phases[:, 2 * parity], phases[:, 2 * parity + 1]
            re, im = sums[:, 0, :, lanes], sums[:, 1, :, lanes]
            w_re = turn_re * ph_re - turn_im * ph_im
            w_im = turn_re * ph_im + turn_im * ph_re
            out[:, block, parity, 0] = re * w_re - im * w_im
            out[:, block, parity, 1] = re * w_im + im * w_re


def forward_kernel(x, twist, tab_high, tab_low, out, grid):
    tiles = x.shape[5] // LANES

    def value_at(parity, j):
        group, tile = divmod(j, tiles)
        lanes = pl.ds(tile * LANES, LANES)
        return x[0, group, parity, 0, :, lanes], x[0, group, parity, 1, :, lanes]

    upper, lower = forward(value_at, twist, tab_high, tab_low, grid)
    out[0, 0] = upper
    out[0, 1] = lower


def apply_kernel(taps, spectrum, twist, tab_high, tab_low, out, response, ring, sides, grid):
    step = pl.program_id(0)
    points = twist.shape[2]
    tiles = out.shape[5] // LANES

    @pl.when(step < 4)
    def _():
        def value_at(parity, j):
            return taps[j, 0, parity, 0], taps[j, 0, parity, 1]

        upper, lower = forward(value_at, twist, tab_high, tab_low, grid)
        ring[step, 0] = upper
        ring[step, 1] = lower

    @pl.when(step == 3)
    def _():
        sign = 1.0 - 2.0 * (lax.broadcasted_iota(jnp.int32, (SUB, LANES), 0) % 2).astype(jnp.float32)
        re_lanes, im_lanes = pl.ds(0, LANES), pl.ds(LANES, LANES)
        for side in range(2):
            for k in range(points):
                rows = pl.ds(k * SUB, SUB)
                res = [ring[j, side, rows, re_lanes] for j in range(4)]
                ims = [ring[j, side, rows, im_lanes] for j in range(4)]
                for j in range(4):
                    response[j, side, rows, re_lanes] = res[j] - sign * ims[j - 1]
                    response[j, side, rows, im_lanes] = ims[j] + sign * res[j - 1]
        ring[...] = jnp.zeros_like(ring)

    @pl.when(step >= 4)
    def _():
        ring[lax.rem(step, 4)] = spectrum[0]
        slots = [lax.rem(step - j, 4) for j in range(4)]
        re_lanes, im_lanes = pl.ds(0, LANES), pl.ds(LANES, LANES)
        for k in range(points):
            rows = pl.ds(k * SUB, SUB)
            sums = []
            for side in range(2):
                total_re, total_im = 0.0, 0.0
                for j in range(4):
                    h_re, h_im = response[j, side, rows, re_lanes], response[j, side, rows, im_lanes]
                    x_re, x_im = ring[slots[j], side, rows, re_lanes], ring[slots[j], side, rows, im_lanes]
                    total_re += h_re * x_re - h_im * x_im
                    total_im += h_re * x_im + h_im * x_re
                sums.append((total_re, total_im))
            for parity, side in enumerate((plus(*sums), minus(*sums))):
                sides[parity, rows, re_lanes] = side[0]
                sides[parity, rows, im_lanes] = side[1]
        for parity in range(2):

            def put(j, re, im, parity=parity):
                group, tile = divmod(j, tiles)
                lanes = pl.ds(tile * LANES, LANES)
                out[0, group, parity, 0, :, lanes] = re
                out[0, group, parity, 1, :, lanes] = im

            backward(sides, parity, twist, tab_high, tab_low, grid, put)


def gather_kernel(parts, turns, phases, table_high, table_low, out):
    count, slots, width = parts.shape[0], parts.shape[3], parts.shape[4]
    turn_re, turn_im = turns[:, 0], turns[:, 1]
    columns = []
    for parity in range(2):
        ph_re, ph_im = phases[:, 2 * parity], phases[:, 2 * parity + 1]
        w_re = turn_re * ph_re - turn_im * ph_im
        w_im = turn_re * ph_im + turn_im * ph_re
        re, im = parts[:, parity, 0], parts[:, parity, 1]
        pair = jnp.stack([re * w_re + im * w_im, im * w_re - re * w_im], axis=1)
        columns.append(pair.reshape(count * 2 * slots, width))
    high, low = split(jnp.concatenate(columns, axis=1))
    sums = dot3(table_high[...], table_low[...], high, low)
    for parity in range(2):
        out[0, parity] = sums[:, parity * width : (parity + 1) * width]


def whole(shape):
    return pl.BlockSpec(shape, lambda i: (0,) * len(shape))


def call(kernel, name, grid, in_specs, out_specs, out_shape, scratch, flops, size):
    return pl.pallas_call(
        kernel,
        grid=(grid,),
        in_specs=in_specs,
        out_specs=out_specs,
        out_shape=jax.ShapeDtypeStruct(out_shape, jnp.float32),
        scratch_shapes=scratch,
        compiler_params=pltpu.CompilerParams(vmem_limit_bytes=VMEM, dimension_semantics=("arbitrary",)),
        cost_estimate=pl.CostEstimate(flops=int(flops), bytes_accessed=int(size), transcendentals=0),
        name=name,
    )


def exchange(values):
    return lax.all_to_all(values, ("seg", "fft"), split_axis=0, concat_axis=0, tiled=True)


def phase_pair(odd_rows, column, period):
    even = np.stack(turn(odd_rows * column, period), axis=-1)
    odd = np.stack(turn(odd_rows * (2 * column + 1), 2 * period), axis=-1)
    return np.concatenate([even, odd], axis=-1)


def per_device(voltage, chirp_phase):
    groups, segments = lax.axis_size("fft"), lax.axis_size("seg")
    group, segment = lax.axis_index("fft"), lax.axis_index("seg")
    count = groups * segments
    position = segment * groups + group
    quarter, width = voltage.shape[2], voltage.shape[3]
    row_count, half = 4 * quarter, 2 * quarter
    columns = width * groups
    points = columns // LANES
    total = row_count * columns
    short = total // 2
    slots = half // groups
    tile = min(2 * LANES, width // 4)
    f32 = jnp.float32

    keys, lanes = np.arange(points), np.arange(LANES)
    twist = np.stack(
        [
            np.stack(turn(keys[:, None] * lanes[None, :], columns)),
            np.stack(turn(keys[:, None] * (2 * lanes[None, :] + 1), 2 * columns)),
        ]
    ).astype(np.float32)
    tables = []
    for cos, sin in (
        turn(lanes[:, None] * lanes[None, :], LANES),
        turn((2 * lanes[:, None] + 1) * lanes[None, :], 2 * LANES),
    ):
        tables.append(np.block([[cos, sin], [-sin, cos]]))
    tab_high, tab_low = halves(np.stack(tables + [table.T for table in tables]))
    column_tables = [twist, tab_high, tab_low]
    column_specs = [whole(table.shape) for table in column_tables]

    own_rows = max(SUB, quarter // count)
    odd_rows = 2 * np.arange(own_rows * count) + 1
    live = (odd_rows < 2 * quarter).astype(np.float64)
    cos, sin = turn(odd_rows[:, None] * np.arange(quarter)[None, :], 2 * half)
    row_table = np.stack([cos, sin], axis=1) * live[:, None, None]
    row_table = row_table.reshape(count, own_rows, 2, quarter).transpose(0, 2, 1, 3).reshape(-1, quarter)
    row_high, row_low = halves(row_table)
    back_high, back_low = halves(row_table.T / short)
    turns = np.stack(turn(odd_rows[:, None] * np.arange(width)[None, :], 2 * short))
    turns = turns.reshape(2, count, own_rows, width).transpose(1, 0, 2, 3).astype(np.float32)

    def row_phases(column_starts):
        table = phase_pair(odd_rows[None, :], column_starts[:, None], 2 * short)
        table = table.reshape(-1, count, own_rows, 4).transpose(0, 1, 3, 2)
        return jnp.asarray(table[..., None].astype(np.float32))

    phases = lax.dynamic_index_in_dim(row_phases(np.arange(groups) * width), group, 0, keepdims=False)

    chirp_slots = max(SUB, slots // segments)
    holders = slots // chirp_slots
    blocks = chirp_slots // SUB
    is_first = position == 0
    start = jnp.minimum(segment, holders - 1) * chirp_slots
    own_phase = lax.dynamic_slice_in_dim(chirp_phase, start, chirp_slots, axis=1)
    digits = own_phase.reshape(2, chirp_slots, LANES, points)
    near, far = digits[0], digits[1, :, ::-1, ::-1]
    zero_row = jnp.roll(jnp.flip(own_phase[0, 0]), 1).reshape(LANES, points)
    at_zero = jnp.logical_and(is_first, jnp.arange(chirp_slots) == 0)[:, None, None]
    extra = jnp.pad(jnp.stack([digits[1, 0], far[0]])[:, None], ((0, 0), (0, SUB - 1), (0, 0), (0, 0)))
    far = jnp.where(at_zero, zero_row[None], far)
    angles = jnp.concatenate([extra, jnp.stack([near, far])], axis=1)
    angles = angles.reshape(2, blocks + 1, SUB, LANES, points).transpose(1, 0, 4, 2, 3)
    block, key, slot, lane = (lax.broadcasted_iota(jnp.int32, angles.shape, n) for n in (0, 2, 3, 4))
    dead = is_first & (block == 1) & (key == 0) & (slot == 0) & (lane == 0)
    dead = dead | (segment >= holders)
    chirp = jnp.stack([jnp.where(dead, 0.0, jnp.cos(angles)), jnp.where(dead, 0.0, jnp.sin(angles))], axis=2)
    chirp = chirp.reshape(blocks + 1, 4, points, SUB, LANES)
    every = LANES * keys[:, None] + lanes[None, :]
    extra_turn = np.stack(
        [np.stack(turn(half * every, total)), np.stack(turn(half * (2 * every + 1), 2 * total))]
    ).astype(np.float32)
    grid_scratch = pltpu.VMEM((points * SUB, 2 * LANES), f32)
    sides_scratch = pltpu.VMEM((2, points * SUB, 2 * LANES), f32)
    chirp_columns = call(
        chirp_kernel,
        "chirp_columns",
        blocks + 1,
        [pl.BlockSpec(memory_space=pltpu.SMEM), pl.BlockSpec((1, 4, points, SUB, LANES), lambda i: (i, 0, 0, 0, 0))]
        + column_specs
        + [whole(extra_turn.shape)],
        pl.BlockSpec((points, 2, 2, SUB, LANES), lambda i: (0, 0, 0, jnp.maximum(i - 1, 0), 0)),
        (points, 2, 2, chirp_slots, LANES),
        [sides_scratch, grid_scratch, pltpu.VMEM((2, points, SUB, LANES), f32)],
        2e8 * blocks,
        3e6,
    )(position.astype(jnp.int32).reshape(1), chirp, *column_tables, extra_turn)
    if count > points:
        chirp_columns = jnp.pad(chirp_columns, ((0, count - points),) + ((0, 0),) * 4)
    chirp_parts = exchange(chirp_columns)[: holders * groups]

    rows = np.arange(half)
    order = rows.reshape(groups, holders, chirp_slots).transpose(1, 0, 2)
    chirp_turns = np.stack(turn(order[..., None] * lanes, total), axis=2).astype(np.float32)
    block_of = np.arange(points)
    chirp_phases = phase_pair(order[None], LANES * block_of[:, None, None, None], total)
    chirp_phases = chirp_phases.reshape(points, holders * groups, chirp_slots, 4).transpose(0, 1, 3, 2)
    chirp_phases = jnp.asarray(chirp_phases[..., None].astype(np.float32))
    chirp_turns = chirp_turns.reshape(holders * groups, 2, chirp_slots, LANES)
    cos, sin = turn(rows[None, :] * np.arange(row_count)[:, None], row_count)
    cos[:, 0] = 0.5
    sin[:, 0] = np.where(np.arange(row_count) % 2 == 0, 0.5, -0.5)
    taps_table = np.stack([cos, sin], axis=1).reshape(row_count, 2, groups, holders, chirp_slots) / total
    taps_table = taps_table.transpose(0, 3, 2, 1, 4).reshape(row_count, 2 * half)
    taps_high, taps_low = halves(taps_table)
    own_block = jnp.minimum(position, points - 1)
    own_chirp_phases = lax.dynamic_index_in_dim(chirp_phases, own_block, 0, keepdims=False)
    own_row_phases = lax.dynamic_index_in_dim(row_phases(block_of * LANES), own_block, 0, keepdims=False)
    response_shape = (count, 4, 2, 2, own_rows, LANES)
    response = call(
        response_kernel,
        "response",
        1,
        [
            whole(chirp_parts.shape),
            whole(chirp_turns.shape),
            whole(own_chirp_phases.shape),
            whole(taps_high.shape),
            whole(taps_low.shape),
            whole(row_high.shape),
            whole(row_low.shape),
            pl.BlockSpec((count, 2, own_rows, LANES), lambda i: (0, 0, 0, 0)),
            whole(own_row_phases.shape),
        ],
        whole(response_shape),
        response_shape,
        [pltpu.VMEM((2 * half, 2 * LANES), f32)],
        5e9,
        1e7,
    )(chirp_parts, chirp_turns, own_chirp_phases, taps_high, taps_low, row_high, row_low, turns, own_row_phases)
    taps = exchange(response)[:points]

    spread_shape = (count, 2, 2, own_rows, width)
    spread = call(
        spread_kernel,
        "spread",
        width // tile,
        [
            pl.BlockSpec((1, 2, quarter, tile), lambda c: (0, 0, 0, c)),
            whole(row_high.shape),
            whole(row_low.shape),
            pl.BlockSpec((count, 2, own_rows, tile), lambda c: (0, 0, 0, c)),
            whole(phases.shape),
        ],
        pl.BlockSpec((count, 2, 2, own_rows, tile), lambda c: (0, 0, 0, 0, c)),
        spread_shape,
        [],
        2e9,
        1e7,
    )(voltage, row_high, row_low, turns, phases)
    spread = exchange(spread).reshape(segments, groups, 2, 2, own_rows, width)

    cells = (points * SUB, 2 * LANES)
    spectrum = call(
        forward_kernel,
        "forward",
        segments,
        [pl.BlockSpec((1, groups, 2, 2, own_rows, width), lambda s: (s, 0, 0, 0, 0, 0))] + column_specs,
        pl.BlockSpec((1, 2) + cells, lambda s: (s, 0, 0, 0)),
        (segments, 2) + cells,
        [grid_scratch],
        2e9,
        1e7,
    )(spread, *column_tables)

    def lagged(i):
        return jnp.maximum(i - 4, 0)

    packed = call(
        apply_kernel,
        "apply",
        segments + 4,
        [
            pl.BlockSpec((points, 1, 2, 2, own_rows, LANES), lambda i: (0, jnp.minimum(i, 3), 0, 0, 0, 0)),
            pl.BlockSpec((1, 2) + cells, lambda i: (lagged(i), 0, 0, 0)),
        ]
        + column_specs,
        pl.BlockSpec((1, groups, 2, 2, own_rows, width), lambda i: (lagged(i), 0, 0, 0, 0, 0)),
        (segments, groups, 2, 2, own_rows, width),
        [
            pltpu.VMEM((4, 2) + cells, f32),
            pltpu.VMEM((4, 2) + cells, f32),
            sides_scratch,
            grid_scratch,
        ],
        4e9,
        2e7,
    )(taps, spectrum, *column_tables)
    parts = exchange(packed.reshape(spread_shape))

    return call(
        gather_kernel,
        "gather",
        width // tile,
        [
            pl.BlockSpec((count, 2, 2, own_rows, tile), lambda c: (0, 0, 0, 0, c)),
            pl.BlockSpec((count, 2, own_rows, tile), lambda c: (0, 0, 0, c)),
            whole(phases.shape),
            whole(back_high.shape),
            whole(back_low.shape),
        ],
        pl.BlockSpec((1, 2, quarter, tile), lambda c: (0, 0, 0, c)),
        (1, 2, quarter, width),
        [],
        2e9,
        1e7,
    )(parts, turns, phases, back_high, back_low)


def solution(mesh):
    in_specs = (P("seg", None, None, "fft"), P(None, "fft", None))
    out_specs = P("seg", None, None, "fft")
    return jax.shard_map(per_device, mesh=mesh, in_specs=in_specs, out_specs=out_specs, check_vma=False)
```

```python
import math

import jax
import jax.numpy as jnp
import ml_dtypes
import numpy as np
from jax import lax
from jax.experimental import pallas as pl
from jax.experimental.pallas import tpu as pltpu
from jax.sharding import PartitionSpec as P

LANES = 128
SUB = 8
VMEM = 50 * 1024 * 1024


def turn(products, period):
    angles = np.mod(products, period).astype(np.float64) * (-2.0 * math.pi / period)
    return np.cos(angles), np.sin(angles)


def halves(table):
    high = table.astype(ml_dtypes.bfloat16)
    low = (table - high.astype(np.float64)).astype(ml_dtypes.bfloat16)
    return high, low


def split(values):
    high = values.astype(jnp.bfloat16)
    low = (values - high.astype(jnp.float32)).astype(jnp.bfloat16)
    return high, low


def thrice(values, axis):
    high, low = split(values)
    return jnp.concatenate([high, low, high] if axis == 0 else [high, high, low], axis=axis)


def right_table(table):
    high, low = halves(table)
    return np.concatenate([high, low, high], axis=-2)


def left_table(table):
    high, low = halves(table)
    return np.concatenate([high, high, low], axis=-1)


def dot(left, right):
    return jnp.dot(left, right, preferred_element_type=jnp.float32)


def scale_by(value, cos, sin):
    re, im = value
    near = 1e-12
    if abs(sin) < near:
        return value if cos > 0 else (-re, -im)
    if abs(cos) < near:
        return (-im, re) if sin > 0 else (im, -re)
    if abs(abs(cos) - abs(sin)) < near:
        size = abs(cos)
        first = re if cos > 0 else -re
        second = im if cos > 0 else -im
        third = im if sin > 0 else -im
        fourth = re if sin > 0 else -re
        return (first - third) * size, (second + fourth) * size
    return re * cos - im * sin, re * sin + im * cos


def plus(left, right):
    return left[0] + right[0], left[1] + right[1]


def minus(left, right):
    return left[0] - right[0], left[1] - right[1]


def small_dft(values, sign):
    count = len(values)
    if count == 1:
        return values
    if count == 2:
        return [plus(values[0], values[1]), minus(values[0], values[1])]
    if count == 4:
        even_sum, even_gap = plus(values[0], values[2]), minus(values[0], values[2])
        odd_sum, odd_gap = plus(values[1], values[3]), minus(values[1], values[3])
        turned = scale_by(odd_gap, 0.0, float(sign))
        return [plus(even_sum, odd_sum), plus(even_gap, turned), minus(even_sum, odd_sum), minus(even_gap, turned)]
    radix = 4 if count == 32 else 2
    part = count // radix
    pieces = [small_dft(values[i::radix], sign) for i in range(radix)]
    result = [None] * count
    for k in range(part):
        column = []
        for i in range(radix):
            angle = sign * 2.0 * math.pi * i * k / count
            column.append(scale_by(pieces[i][k], math.cos(angle), math.sin(angle)))
        for q, value in enumerate(small_dft(column, sign)):
            result[k + part * q] = value
    return result


def forward(value_at, twist, tables, grid):
    spectra = []
    for parity in range(2):
        values = [value_at(parity, j) for j in range(twist.shape[2])]
        for k, (re, im) in enumerate(small_dft(values, -1)):
            w_re, w_im = twist[parity, 0, pl.ds(k, 1)], twist[parity, 1, pl.ds(k, 1)]
            grid[parity, pl.ds(k * SUB, SUB), pl.ds(0, LANES)] = re * w_re - im * w_im
            grid[parity, pl.ds(k * SUB, SUB), pl.ds(LANES, LANES)] = re * w_im + im * w_re
        spectra.append(dot(thrice(grid[parity], 1), tables[parity]))
    even, odd = spectra
    return even + odd, even - odd


def backward(side, parity, twist, tables, grid, put):
    grid[parity] = dot(thrice(side, 1), tables[2 + parity])
    values = []
    for k in range(twist.shape[2]):
        re = grid[parity, pl.ds(k * SUB, SUB), pl.ds(0, LANES)]
        im = grid[parity, pl.ds(k * SUB, SUB), pl.ds(LANES, LANES)]
        w_re, w_im = twist[parity, 0, pl.ds(k, 1)], twist[parity, 1, pl.ds(k, 1)]
        values.append((re * w_re + im * w_im, im * w_re - re * w_im))
    for j, (re, im) in enumerate(small_dft(values, 1)):
        put(j, re, im)


def turned_by(angles):
    half = angles * 0.5
    square = half * half
    sin, cos = 0.0, 0.0
    for n in range(6, -1, -1):
        sin = sin * square + (-1.0) ** n / math.factorial(2 * n + 1)
        cos = cos * square + (-1.0) ** n / math.factorial(2 * n)
    sin = sin * half
    return 1.0 - 2.0 * sin * sin, 2.0 * sin * cos


def spread_kernel(x, table, turns, phases, out):
    count, slots, width = out.shape[0], out.shape[3], out.shape[4]
    sums = dot(table[...], thrice(jnp.concatenate([x[0, 0], x[0, 1]], axis=1), 0))
    sums = sums.reshape(count, 2, slots, 2 * width)
    turn_re, turn_im = turns[:, 0], turns[:, 1]
    for parity in range(2):
        lanes = slice(parity * width, (parity + 1) * width)
        ph_re, ph_im = phases[:, 2 * parity], phases[:, 2 * parity + 1]
        re, im = sums[:, 0, :, lanes], sums[:, 1, :, lanes]
        w_re = turn_re * ph_re - turn_im * ph_im
        w_im = turn_re * ph_im + turn_im * ph_re
        out[:, parity, 0] = re * w_re - im * w_im
        out[:, parity, 1] = re * w_im + im * w_re


def chirp_kernel(position, angles, twist, tables, mirror, extra_turn, out, sides, grid, held):
    first_rows = jnp.logical_and(position[0] == 0, pl.program_id(0) == 0)
    points = twist.shape[2]
    for side in range(2):
        for k in range(points):
            cos, sin = turned_by(angles[side, 0, k])
            sides[side, pl.ds(k * SUB, SUB), pl.ds(0, LANES)] = cos
            sides[side, pl.ds(k * SUB, SUB), pl.ds(LANES, LANES)] = sin

    @pl.when(first_rows)
    def _():
        slot = lax.broadcasted_iota(jnp.int32, (SUB, LANES), 0)
        lane = lax.broadcasted_iota(jnp.int32, (SUB, LANES), 1)
        alive = jnp.logical_or(slot > 0, lane > 0)
        for part in range(2):
            lanes = pl.ds(part * LANES, LANES)
            sides[0, pl.ds(0, SUB), lanes] = jnp.where(alive, sides[0, pl.ds(0, SUB), lanes], 0.0)

    for parity in range(2):
        sign = 1.0 - 2.0 * parity
        for side in range(2):

            def put(j, re, im, parity=parity, side=side, sign=sign):
                held[parity, side, 0, j] = re
                held[parity, side, 1, j] = im
                if side == 1:
                    m_re, m_im = mirror[parity, 0, pl.ds(j, 1)], mirror[parity, 1, pl.ds(j, 1)]
                    out[j, parity, 0] = held[parity, 0, 0, j] + sign * (re * m_re + im * m_im)
                    out[j, parity, 1] = held[parity, 0, 1, j] + sign * (re * m_im - im * m_re)

            backward(sides[side], parity, twist, tables, grid.at[side], put)

    @pl.when(first_rows)
    def _():
        keep = lax.broadcasted_iota(jnp.int32, (SUB, LANES), 0) > 0
        for parity in range(2):
            for j in range(points):
                w_re, w_im = extra_turn[parity, 0, pl.ds(j, 1)], extra_turn[parity, 1, pl.ds(j, 1)]
                near = 2.0 * held[parity, 0, 0, j]
                far = 2.0 * (held[parity, 1, 0, j] * w_re + held[parity, 1, 1, j] * w_im)
                out[j, parity, 0] = jnp.where(keep, out[j, parity, 0], near)
                out[j, parity, 1] = jnp.where(keep, out[j, parity, 1], far)


def response_kernel(parts, turns_in, phases_in, back_table, table, turns, phases, out, packed):
    sources, slots = parts.shape[0], parts.shape[3]
    count, out_slots = out.shape[0], out.shape[4]
    depth = 2 * sources * slots

    @pl.when(pl.program_id(0) == 0)
    def _():
        for source in range(sources):
            t_re, t_im = turns_in[source, 0], turns_in[source, 1]
            for parity in range(2):
                ph_re, ph_im = phases_in[source, 2 * parity], phases_in[source, 2 * parity + 1]
                w_re = t_re * ph_re - t_im * ph_im
                w_im = t_re * ph_im + t_im * ph_re
                re, im = parts[source, parity, 0], parts[source, parity, 1]
                lanes = pl.ds(parity * LANES, LANES)
                pair = jnp.concatenate([re * w_re + im * w_im, im * w_re - re * w_im], axis=0)
                high, low = split(pair)
                for n, value in enumerate((high, low, high)):
                    packed[pl.ds(n * depth + 2 * source * slots, 2 * slots), lanes] = value

    taps = dot(back_table[...], packed[...])
    sums = dot(table[...], thrice(taps, 0)).reshape(count, 2, out_slots, 2 * LANES)
    turn_re, turn_im = turns[:, 0], turns[:, 1]
    for parity in range(2):
        lanes = slice(parity * LANES, (parity + 1) * LANES)
        ph_re, ph_im = phases[:, 2 * parity], phases[:, 2 * parity + 1]
        re, im = sums[:, 0, :, lanes], sums[:, 1, :, lanes]
        w_re = turn_re * ph_re - turn_im * ph_im
        w_im = turn_re * ph_im + turn_im * ph_re
        out[:, 0, parity, 0] = re * w_re - im * w_im
        out[:, 0, parity, 1] = re * w_im + im * w_re


def forward_kernel(x, twist, tables, out, grid):
    tiles = x.shape[5] // LANES

    def value_at(parity, j):
        group, tile = divmod(j, tiles)
        lanes = pl.ds(tile * LANES, LANES)
        return x[0, group, parity, 0, :, lanes], x[0, group, parity, 1, :, lanes]

    upper, lower = forward(value_at, twist, tables, grid)
    out[0, 0] = upper
    out[0, 1] = lower


def apply_kernel(taps, spectrum, twist, tables, out, response, ring, sides, grid):
    step = pl.program_id(0)
    points = twist.shape[2]
    tiles = out.shape[5] // LANES

    @pl.when(step < 4)
    def _():
        def value_at(parity, j):
            return taps[j, 0, parity, 0], taps[j, 0, parity, 1]

        upper, lower = forward(value_at, twist, tables, grid)
        ring[step, 0] = upper
        ring[step, 1] = lower

    @pl.when(step == 3)
    def _():
        sign = 1.0 - 2.0 * (lax.broadcasted_iota(jnp.int32, (SUB, LANES), 0) % 2).astype(jnp.float32)
        re_lanes, im_lanes = pl.ds(0, LANES), pl.ds(LANES, LANES)
        for side in range(2):
            for k in range(points):
                rows = pl.ds(k * SUB, SUB)
                res = [ring[j, side, rows, re_lanes] for j in range(4)]
                ims = [ring[j, side, rows, im_lanes] for j in range(4)]
                for j in range(4):
                    response[j, side, rows, re_lanes] = res[j] - sign * ims[j - 1]
                    response[j, side, rows, im_lanes] = ims[j] + sign * res[j - 1]
        ring[...] = jnp.zeros_like(ring)

    @pl.when(step >= 4)
    def _():
        ring[lax.rem(step, 4)] = spectrum[0]
        slots = [lax.rem(step - j, 4) for j in range(4)]
        re_lanes, im_lanes = pl.ds(0, LANES), pl.ds(LANES, LANES)
        for k in range(points):
            rows = pl.ds(k * SUB, SUB)
            sums = []
            for side in range(2):
                total_re, total_im = 0.0, 0.0
                for j in range(4):
                    h_re, h_im = response[j, side, rows, re_lanes], response[j, side, rows, im_lanes]
                    x_re, x_im = ring[slots[j], side, rows, re_lanes], ring[slots[j], side, rows, im_lanes]
                    total_re += h_re * x_re - h_im * x_im
                    total_im += h_re * x_im + h_im * x_re
                sums.append((total_re, total_im))
            for parity, side in enumerate((plus(*sums), minus(*sums))):
                sides[parity, rows, re_lanes] = side[0]
                sides[parity, rows, im_lanes] = side[1]
        for parity in range(2):

            def put(j, re, im, parity=parity):
                group, tile = divmod(j, tiles)
                lanes = pl.ds(tile * LANES, LANES)
                out[0, group, parity, 0, :, lanes] = re
                out[0, group, parity, 1, :, lanes] = im

            backward(sides[parity], parity, twist, tables, grid, put)


def gather_kernel(parts, turns, phases, table, out):
    count, slots, width = parts.shape[0], parts.shape[3], parts.shape[4]
    turn_re, turn_im = turns[:, 0], turns[:, 1]
    columns = []
    for parity in range(2):
        ph_re, ph_im = phases[:, 2 * parity], phases[:, 2 * parity + 1]
        w_re = turn_re * ph_re - turn_im * ph_im
        w_im = turn_re * ph_im + turn_im * ph_re
        re, im = parts[:, parity, 0], parts[:, parity, 1]
        pair = jnp.stack([re * w_re + im * w_im, im * w_re - re * w_im], axis=1)
        columns.append(pair.reshape(count * 2 * slots, width))
    sums = dot(table[...], thrice(jnp.concatenate(columns, axis=1), 0))
    for parity in range(2):
        out[0, parity] = sums[:, parity * width : (parity + 1) * width]


def whole(shape):
    return pl.BlockSpec(shape, lambda i: (0,) * len(shape))


def call(kernel, name, grid, in_specs, out_specs, out_shape, scratch, flops, size):
    return pl.pallas_call(
        kernel,
        grid=(grid,),
        in_specs=in_specs,
        out_specs=out_specs,
        out_shape=jax.ShapeDtypeStruct(out_shape, jnp.float32),
        scratch_shapes=scratch,
        compiler_params=pltpu.CompilerParams(vmem_limit_bytes=VMEM, dimension_semantics=("arbitrary",)),
        cost_estimate=pl.CostEstimate(flops=int(flops), bytes_accessed=int(size), transcendentals=0),
        name=name,
    )


def exchange(values):
    return lax.all_to_all(values, ("seg", "fft"), split_axis=0, concat_axis=0, tiled=True)


def phase_pair(odd_rows, column, period):
    even = np.stack(turn(odd_rows * column, period), axis=-1)
    odd = np.stack(turn(odd_rows * (2 * column + 1), 2 * period), axis=-1)
    return np.concatenate([even, odd], axis=-1)


def per_device(voltage, chirp_phase):
    groups, segments = lax.axis_size("fft"), lax.axis_size("seg")
    group, segment = lax.axis_index("fft"), lax.axis_index("seg")
    count = groups * segments
    position = segment * groups + group
    quarter, width = voltage.shape[2], voltage.shape[3]
    row_count, half = 4 * quarter, 2 * quarter
    columns = width * groups
    points = columns // LANES
    total = row_count * columns
    short = total // 2
    slots = half // groups
    tile = min(2 * LANES, width // 4)
    f32 = jnp.float32

    keys, lanes = np.arange(points), np.arange(LANES)
    twist = np.stack(
        [
            np.stack(turn(keys[:, None] * lanes[None, :], columns)),
            np.stack(turn(keys[:, None] * (2 * lanes[None, :] + 1), 2 * columns)),
        ]
    ).astype(np.float32)
    tables = []
    for cos, sin in (
        turn(lanes[:, None] * lanes[None, :], LANES),
        turn((2 * lanes[:, None] + 1) * lanes[None, :], 2 * LANES),
    ):
        tables.append(np.block([[cos, sin], [-sin, cos]]))
    column_tables = [twist, right_table(np.stack(tables + [table.T for table in tables]))]
    column_specs = [whole(table.shape) for table in column_tables]

    own_rows = max(SUB, quarter // count)
    odd_rows = 2 * np.arange(own_rows * count) + 1
    live = (odd_rows < 2 * quarter).astype(np.float64)
    cos, sin = turn(odd_rows[:, None] * np.arange(quarter)[None, :], 2 * half)
    row_table = np.stack([cos, sin], axis=1) * live[:, None, None]
    row_table = row_table.reshape(count, own_rows, 2, quarter).transpose(0, 2, 1, 3).reshape(-1, quarter)
    back_table = left_table(row_table.T / short)
    row_table = left_table(row_table)
    turns = np.stack(turn(odd_rows[:, None] * np.arange(width)[None, :], 2 * short))
    turns = turns.reshape(2, count, own_rows, width).transpose(1, 0, 2, 3).astype(np.float32)

    def row_phases(column_starts):
        table = phase_pair(odd_rows[None, :], column_starts[:, None], 2 * short)
        table = table.reshape(-1, count, own_rows, 4).transpose(0, 1, 3, 2)
        return jnp.asarray(table[..., None].astype(np.float32))

    phases = lax.dynamic_index_in_dim(row_phases(np.arange(groups) * width), group, 0, keepdims=False)

    chirp_slots = max(SUB, slots // segments)
    holders = slots // chirp_slots
    blocks = chirp_slots // SUB
    start = jnp.minimum(segment, holders - 1) * chirp_slots
    own_phase = lax.dynamic_slice_in_dim(chirp_phase, start, chirp_slots, axis=1)
    angles = own_phase.reshape(2, blocks, SUB, LANES, points).transpose(0, 1, 4, 2, 3)
    every = LANES * keys[:, None] + lanes[None, :]
    extra_turn = np.stack(
        [np.stack(turn(half * every, total)), np.stack(turn(half * (2 * every + 1), 2 * total))]
    ).astype(np.float32)
    mirror = np.stack(
        [np.stack(turn(every, columns)), np.stack(turn((1 - columns) * (2 * every + 1), 2 * columns))]
    ).astype(np.float32)
    grid_scratch = pltpu.VMEM((2, points * SUB, 2 * LANES), f32)
    sides_scratch = pltpu.VMEM((2, points * SUB, 2 * LANES), f32)
    chirp_columns = call(
        chirp_kernel,
        "chirp_columns",
        blocks,
        [
            pl.BlockSpec(memory_space=pltpu.SMEM),
            pl.BlockSpec((2, 1, points, SUB, LANES), lambda i: (0, i, 0, 0, 0)),
        ]
        + column_specs
        + [whole(mirror.shape), whole(extra_turn.shape)],
        pl.BlockSpec((points, 2, 2, SUB, LANES), lambda i: (0, 0, 0, i, 0)),
        (points, 2, 2, chirp_slots, LANES),
        [
            sides_scratch,
            pltpu.VMEM((2, 2, points * SUB, 2 * LANES), f32),
            pltpu.VMEM((2, 2, 2, points, SUB, LANES), f32),
        ],
        4e8 * blocks,
        3e6,
    )(position.astype(jnp.int32).reshape(1), angles, *column_tables, mirror, extra_turn)
    if holders < segments:
        chirp_columns = jnp.where(segment < holders, chirp_columns, 0.0)
    if count > points:
        chirp_columns = jnp.pad(chirp_columns, ((0, count - points),) + ((0, 0),) * 4)
    chirp_parts = exchange(chirp_columns)[: holders * groups]

    rows = np.arange(half)
    order = rows.reshape(groups, holders, chirp_slots).transpose(1, 0, 2)
    chirp_turns = np.stack(turn(order[..., None] * lanes, total), axis=2).astype(np.float32)
    block_of = np.arange(points)
    chirp_phases = phase_pair(order[None], LANES * block_of[:, None, None, None], total)
    chirp_phases = chirp_phases.reshape(points, holders * groups, chirp_slots, 4).transpose(0, 1, 3, 2)
    chirp_phases = jnp.asarray(chirp_phases[..., None].astype(np.float32))
    chirp_turns = chirp_turns.reshape(holders * groups, 2, chirp_slots, LANES)
    cos, sin = turn(rows[None, :] * np.arange(row_count)[:, None], row_count)
    cos[:, 0] = 0.5
    sin[:, 0] = np.where(np.arange(row_count) % 2 == 0, 0.5, -0.5)
    taps_table = np.stack([cos, sin], axis=1).reshape(row_count, 2, groups, holders, chirp_slots) / total
    taps_table = taps_table.transpose(0, 3, 2, 1, 4).reshape(row_count, 2 * half)
    taps_table = left_table(taps_table)
    own_block = jnp.minimum(position, points - 1)
    own_chirp_phases = lax.dynamic_index_in_dim(chirp_phases, own_block, 0, keepdims=False)
    own_row_phases = lax.dynamic_index_in_dim(row_phases(block_of * LANES), own_block, 0, keepdims=False)
    response_shape = (count, 4, 2, 2, own_rows, LANES)
    response = call(
        response_kernel,
        "response",
        4,
        [
            whole(chirp_parts.shape),
            whole(chirp_turns.shape),
            whole(own_chirp_phases.shape),
            pl.BlockSpec((quarter, taps_table.shape[1]), lambda i: (i, 0)),
            whole(row_table.shape),
            pl.BlockSpec((count, 2, own_rows, LANES), lambda i: (0, 0, 0, 0)),
            whole(own_row_phases.shape),
        ],
        pl.BlockSpec((count, 1, 2, 2, own_rows, LANES), lambda i: (0, i, 0, 0, 0, 0)),
        response_shape,
        [pltpu.VMEM((6 * half, 2 * LANES), jnp.bfloat16)],
        5e9,
        1e7,
    )(chirp_parts, chirp_turns, own_chirp_phases, taps_table, row_table, turns, own_row_phases)
    taps = exchange(response)[:points]

    spread_shape = (count, 2, 2, own_rows, width)
    spread = call(
        spread_kernel,
        "spread",
        width // tile,
        [
            pl.BlockSpec((1, 2, quarter, tile), lambda c: (0, 0, 0, c)),
            whole(row_table.shape),
            pl.BlockSpec((count, 2, own_rows, tile), lambda c: (0, 0, 0, c)),
            whole(phases.shape),
        ],
        pl.BlockSpec((count, 2, 2, own_rows, tile), lambda c: (0, 0, 0, 0, c)),
        spread_shape,
        [],
        2e9,
        1e7,
    )(voltage, row_table, turns, phases)
    spread = exchange(spread).reshape(segments, groups, 2, 2, own_rows, width)

    cells = (points * SUB, 2 * LANES)
    spectrum = call(
        forward_kernel,
        "forward",
        segments,
        [pl.BlockSpec((1, groups, 2, 2, own_rows, width), lambda s: (s, 0, 0, 0, 0, 0))] + column_specs,
        pl.BlockSpec((1, 2) + cells, lambda s: (s, 0, 0, 0)),
        (segments, 2) + cells,
        [grid_scratch],
        2e9,
        1e7,
    )(spread, *column_tables)

    def lagged(i):
        return jnp.maximum(i - 4, 0)

    packed = call(
        apply_kernel,
        "apply",
        segments + 4,
        [
            pl.BlockSpec((points, 1, 2, 2, own_rows, LANES), lambda i: (0, jnp.minimum(i, 3), 0, 0, 0, 0)),
            pl.BlockSpec((1, 2) + cells, lambda i: (lagged(i), 0, 0, 0)),
        ]
        + column_specs,
        pl.BlockSpec((1, groups, 2, 2, own_rows, width), lambda i: (lagged(i), 0, 0, 0, 0, 0)),
        (segments, groups, 2, 2, own_rows, width),
        [
            pltpu.VMEM((4, 2) + cells, f32),
            pltpu.VMEM((4, 2) + cells, f32),
            sides_scratch,
            grid_scratch,
        ],
        4e9,
        2e7,
    )(taps, spectrum, *column_tables)
    parts = exchange(packed.reshape(spread_shape))

    return call(
        gather_kernel,
        "gather",
        width // tile,
        [
            pl.BlockSpec((count, 2, 2, own_rows, tile), lambda c: (0, 0, 0, 0, c)),
            pl.BlockSpec((count, 2, own_rows, tile), lambda c: (0, 0, 0, c)),
            whole(phases.shape),
            whole(back_table.shape),
        ],
        pl.BlockSpec((1, 2, quarter, tile), lambda c: (0, 0, 0, c)),
        (1, 2, quarter, width),
        [],
        2e9,
        1e7,
    )(parts, turns, phases, back_table)


def solution(mesh):
    in_specs = (P("seg", None, None, "fft"), P(None, "fft", None))
    out_specs = P("seg", None, None, "fft")
    return jax.shard_map(per_device, mesh=mesh, in_specs=in_specs, out_specs=out_specs, check_vma=False)
```

```python
import math

import jax
import jax.numpy as jnp
import ml_dtypes
import numpy as np
from jax import lax
from jax.experimental import pallas as pl
from jax.experimental.pallas import tpu as pltpu
from jax.sharding import PartitionSpec as P

LANES = 128
SUB = 8
VMEM = 50 * 1024 * 1024


def turn(products, period):
    angles = np.mod(products, period).astype(np.float64) * (-2.0 * math.pi / period)
    return np.cos(angles), np.sin(angles)


def halves(table):
    high = table.astype(ml_dtypes.bfloat16)
    low = (table - high.astype(np.float64)).astype(ml_dtypes.bfloat16)
    return high, low


def split(values):
    high = values.astype(jnp.bfloat16)
    low = (values - high.astype(jnp.float32)).astype(jnp.bfloat16)
    return high, low


def thrice(values, axis):
    high, low = split(values)
    return jnp.concatenate([high, low, high] if axis == 0 else [high, high, low], axis=axis)


def right_table(table):
    high, low = halves(table)
    return np.concatenate([high, low, high], axis=-2)


def left_table(table):
    high, low = halves(table)
    return np.concatenate([high, high, low], axis=-1)


def dot(left, right):
    return jnp.dot(left, right, preferred_element_type=jnp.float32)


def scale_by(value, cos, sin):
    re, im = value
    near = 1e-12
    if abs(sin) < near:
        return value if cos > 0 else (-re, -im)
    if abs(cos) < near:
        return (-im, re) if sin > 0 else (im, -re)
    if abs(abs(cos) - abs(sin)) < near:
        size = abs(cos)
        first = re if cos > 0 else -re
        second = im if cos > 0 else -im
        third = im if sin > 0 else -im
        fourth = re if sin > 0 else -re
        return (first - third) * size, (second + fourth) * size
    return re * cos - im * sin, re * sin + im * cos


def plus(left, right):
    return left[0] + right[0], left[1] + right[1]


def minus(left, right):
    return left[0] - right[0], left[1] - right[1]


def small_dft(values, sign):
    count = len(values)
    if count == 1:
        return values
    if count == 2:
        return [plus(values[0], values[1]), minus(values[0], values[1])]
    if count == 4:
        even_sum, even_gap = plus(values[0], values[2]), minus(values[0], values[2])
        odd_sum, odd_gap = plus(values[1], values[3]), minus(values[1], values[3])
        turned = scale_by(odd_gap, 0.0, float(sign))
        return [plus(even_sum, odd_sum), plus(even_gap, turned), minus(even_sum, odd_sum), minus(even_gap, turned)]
    radix = 4 if count == 32 else 2
    part = count // radix
    pieces = [small_dft(values[i::radix], sign) for i in range(radix)]
    result = [None] * count
    for k in range(part):
        column = []
        for i in range(radix):
            angle = sign * 2.0 * math.pi * i * k / count
            column.append(scale_by(pieces[i][k], math.cos(angle), math.sin(angle)))
        for q, value in enumerate(small_dft(column, sign)):
            result[k + part * q] = value
    return result


def forward(value_at, twist, tables, grid):
    spectra = []
    for parity in range(2):
        values = [value_at(parity, j) for j in range(twist.shape[2])]
        for k, (re, im) in enumerate(small_dft(values, -1)):
            w_re, w_im = twist[parity, 0, pl.ds(k, 1)], twist[parity, 1, pl.ds(k, 1)]
            grid[parity, pl.ds(k * SUB, SUB), pl.ds(0, LANES)] = re * w_re - im * w_im
            grid[parity, pl.ds(k * SUB, SUB), pl.ds(LANES, LANES)] = re * w_im + im * w_re
        spectra.append(dot(thrice(grid[parity], 1), tables[parity]))
    even, odd = spectra
    return even + odd, even - odd


def backward(side, parity, twist, tables, grid, put):
    grid[parity] = dot(thrice(side, 1), tables[2 + parity])
    values = []
    for k in range(twist.shape[2]):
        re = grid[parity, pl.ds(k * SUB, SUB), pl.ds(0, LANES)]
        im = grid[parity, pl.ds(k * SUB, SUB), pl.ds(LANES, LANES)]
        w_re, w_im = twist[parity, 0, pl.ds(k, 1)], twist[parity, 1, pl.ds(k, 1)]
        values.append((re * w_re + im * w_im, im * w_re - re * w_im))
    for j, (re, im) in enumerate(small_dft(values, 1)):
        put(j, re, im)


def turned_by(angles):
    half = angles * 0.5
    square = half * half
    sin, cos = 0.0, 0.0
    for n in range(6, -1, -1):
        sin = sin * square + (-1.0) ** n / math.factorial(2 * n + 1)
        cos = cos * square + (-1.0) ** n / math.factorial(2 * n)
    sin = sin * half
    return 1.0 - 2.0 * sin * sin, 2.0 * sin * cos


def spread_kernel(x, table, turns, phases, out):
    count, slots, width = out.shape[0], out.shape[3], out.shape[4]
    sums = dot(table[...], thrice(jnp.concatenate([x[0, 0], x[0, 1]], axis=1), 0))
    sums = sums.reshape(count, 2, slots, 2 * width)
    turn_re, turn_im = turns[:, 0], turns[:, 1]
    for parity in range(2):
        lanes = slice(parity * width, (parity + 1) * width)
        ph_re, ph_im = phases[:, 2 * parity], phases[:, 2 * parity + 1]
        re, im = sums[:, 0, :, lanes], sums[:, 1, :, lanes]
        w_re = turn_re * ph_re - turn_im * ph_im
        w_im = turn_re * ph_im + turn_im * ph_re
        out[:, parity, 0] = re * w_re - im * w_im
        out[:, parity, 1] = re * w_im + im * w_re


def chirp_kernel(position, angles, twist, tables, mirror, extra_turn, out, sides, grid, held):
    first_rows = jnp.logical_and(position[0] == 0, pl.program_id(0) == 0)
    points = twist.shape[2]
    tiles = out.shape[4] // LANES

    def place(j):
        return j // tiles, pl.ds(j % tiles * LANES, LANES)

    for side in range(2):
        for k in range(points):
            cos, sin = turned_by(angles[0, side, 0, k])
            sides[side, pl.ds(k * SUB, SUB), pl.ds(0, LANES)] = cos
            sides[side, pl.ds(k * SUB, SUB), pl.ds(LANES, LANES)] = sin

    @pl.when(first_rows)
    def _():
        slot = lax.broadcasted_iota(jnp.int32, (SUB, LANES), 0)
        lane = lax.broadcasted_iota(jnp.int32, (SUB, LANES), 1)
        alive = jnp.logical_or(slot > 0, lane > 0)
        for part in range(2):
            lanes = pl.ds(part * LANES, LANES)
            sides[0, pl.ds(0, SUB), lanes] = jnp.where(alive, sides[0, pl.ds(0, SUB), lanes], 0.0)

    for parity in range(2):
        sign = 1.0 - 2.0 * parity
        for side in range(2):

            def put(j, re, im, parity=parity, side=side, sign=sign):
                held[parity, side, 0, j] = re
                held[parity, side, 1, j] = im
                if side == 1:
                    m_re, m_im = mirror[parity, 0, pl.ds(j, 1)], mirror[parity, 1, pl.ds(j, 1)]
                    to, lanes = place(j)
                    out[to, parity, 0, :, lanes] = held[parity, 0, 0, j] + sign * (re * m_re + im * m_im)
                    out[to, parity, 1, :, lanes] = held[parity, 0, 1, j] + sign * (re * m_im - im * m_re)

            backward(sides[side], parity, twist, tables, grid.at[side], put)

    @pl.when(first_rows)
    def _():
        keep = lax.broadcasted_iota(jnp.int32, (SUB, LANES), 0) > 0
        for parity in range(2):
            for j in range(points):
                w_re, w_im = extra_turn[parity, 0, pl.ds(j, 1)], extra_turn[parity, 1, pl.ds(j, 1)]
                near = 2.0 * held[parity, 0, 0, j]
                far = 2.0 * (held[parity, 1, 0, j] * w_re + held[parity, 1, 1, j] * w_im)
                to, lanes = place(j)
                out[to, parity, 0, :, lanes] = jnp.where(keep, out[to, parity, 0, :, lanes], near)
                out[to, parity, 1, :, lanes] = jnp.where(keep, out[to, parity, 1, :, lanes], far)


def response_kernel(segment, *refs):
    turns_in, phases_in, back_table, table, turns, phases, out, packed = refs[-8:]
    pieces = refs[:-8]
    holders, groups, slots, width = turns_in.shape[0], turns_in.shape[1], turns_in.shape[3], turns_in.shape[4]
    count, out_slots = out.shape[0], out.shape[4]
    depth = 2 * holders * groups * slots

    def fill(piece, source):
        for group in range(groups):
            t_re, t_im = turns_in[source, group, 0], turns_in[source, group, 1]
            base = pl.multiple_of((source * groups + group) * (2 * slots), 2 * slots)
            for parity in range(2):
                ph_re, ph_im = phases_in[source, group, 2 * parity], phases_in[source, group, 2 * parity + 1]
                w_re = t_re * ph_re - t_im * ph_im
                w_im = t_re * ph_im + t_im * ph_re
                own = pl.ds(group * slots, slots)
                re, im = piece[parity, 0, own], piece[parity, 1, own]
                lanes = pl.ds(parity * width, width)
                pair = jnp.concatenate([re * w_re + im * w_im, im * w_re - re * w_im], axis=0)
                high, low = split(pair)
                for n, value in enumerate((high, low, high)):
                    packed[pl.ds(n * depth + base, 2 * slots), lanes] = value

    @pl.when(pl.program_id(0) == 0)
    def _():
        for i, piece in enumerate(pieces):
            source = jnp.bitwise_xor(segment[0], i)
            pl.when(source < holders)(lambda piece=piece, source=source: fill(piece, source))

    taps = dot(back_table[...], packed[...])
    sums = dot(table[...], thrice(taps, 0)).reshape(count, 2, out_slots, 2 * width)
    turn_re, turn_im = turns[:, 0], turns[:, 1]
    for parity in range(2):
        lanes = slice(parity * width, (parity + 1) * width)
        ph_re, ph_im = phases[:, 2 * parity], phases[:, 2 * parity + 1]
        re, im = sums[:, 0, :, lanes], sums[:, 1, :, lanes]
        w_re = turn_re * ph_re - turn_im * ph_im
        w_im = turn_re * ph_im + turn_im * ph_re
        out[:, 0, parity, 0] = re * w_re - im * w_im
        out[:, 0, parity, 1] = re * w_im + im * w_re


def forward_kernel(x, twist, tables, out, grid):
    tiles = x.shape[5] // LANES

    def value_at(parity, j):
        group, tile = divmod(j, tiles)
        lanes = pl.ds(tile * LANES, LANES)
        return x[0, group, parity, 0, :, lanes], x[0, group, parity, 1, :, lanes]

    upper, lower = forward(value_at, twist, tables, grid)
    out[0, 0] = upper
    out[0, 1] = lower


def apply_kernel(segment, *refs):
    spectrum, twist, tables, out, taps, response, ring, sides, grid = refs[-9:]
    pieces = refs[:-9]
    step = pl.program_id(0)
    points = twist.shape[2]
    tiles = out.shape[5] // LANES
    block_tiles = taps.shape[4] // LANES

    @pl.when(step < 4)
    def _():
        for i, piece in enumerate(pieces):
            taps[jnp.bitwise_xor(segment[0], i)] = piece[0]

        def value_at(parity, j):
            lanes = pl.ds(j % block_tiles * LANES, LANES)
            return taps[j // block_tiles, parity, 0, :, lanes], taps[j // block_tiles, parity, 1, :, lanes]

        upper, lower = forward(value_at, twist, tables, grid)
        ring[step, 0] = upper
        ring[step, 1] = lower

    @pl.when(step == 3)
    def _():
        sign = 1.0 - 2.0 * (lax.broadcasted_iota(jnp.int32, (SUB, LANES), 0) % 2).astype(jnp.float32)
        re_lanes, im_lanes = pl.ds(0, LANES), pl.ds(LANES, LANES)
        for side in range(2):
            for k in range(points):
                rows = pl.ds(k * SUB, SUB)
                res = [ring[j, side, rows, re_lanes] for j in range(4)]
                ims = [ring[j, side, rows, im_lanes] for j in range(4)]
                for j in range(4):
                    response[j, side, rows, re_lanes] = res[j] - sign * ims[j - 1]
                    response[j, side, rows, im_lanes] = ims[j] + sign * res[j - 1]
        ring[...] = jnp.zeros_like(ring)

    @pl.when(step >= 4)
    def _():
        ring[lax.rem(step, 4)] = spectrum[0]
        slots = [lax.rem(step - j, 4) for j in range(4)]
        re_lanes, im_lanes = pl.ds(0, LANES), pl.ds(LANES, LANES)
        for k in range(points):
            rows = pl.ds(k * SUB, SUB)
            sums = []
            for side in range(2):
                total_re, total_im = 0.0, 0.0
                for j in range(4):
                    h_re, h_im = response[j, side, rows, re_lanes], response[j, side, rows, im_lanes]
                    x_re, x_im = ring[slots[j], side, rows, re_lanes], ring[slots[j], side, rows, im_lanes]
                    total_re += h_re * x_re - h_im * x_im
                    total_im += h_re * x_im + h_im * x_re
                sums.append((total_re, total_im))
            for parity, side in enumerate((plus(*sums), minus(*sums))):
                sides[parity, rows, re_lanes] = side[0]
                sides[parity, rows, im_lanes] = side[1]
        for parity in range(2):

            def put(j, re, im, parity=parity):
                group, tile = divmod(j, tiles)
                lanes = pl.ds(tile * LANES, LANES)
                out[0, group, parity, 0, :, lanes] = re
                out[0, group, parity, 1, :, lanes] = im

            backward(sides[parity], parity, twist, tables, grid, put)


def gather_kernel(parts, turns, phases, table, out):
    count, slots, width = parts.shape[0], parts.shape[3], parts.shape[4]
    turn_re, turn_im = turns[:, 0], turns[:, 1]
    columns = []
    for parity in range(2):
        ph_re, ph_im = phases[:, 2 * parity], phases[:, 2 * parity + 1]
        w_re = turn_re * ph_re - turn_im * ph_im
        w_im = turn_re * ph_im + turn_im * ph_re
        re, im = parts[:, parity, 0], parts[:, parity, 1]
        pair = jnp.stack([re * w_re + im * w_im, im * w_re - re * w_im], axis=1)
        columns.append(pair.reshape(count * 2 * slots, width))
    sums = dot(table[...], thrice(jnp.concatenate(columns, axis=1), 0))
    for parity in range(2):
        out[0, parity] = sums[:, parity * width : (parity + 1) * width]


def whole(shape):
    return pl.BlockSpec(shape, lambda i: (0,) * len(shape))


def call(kernel, name, grid, in_specs, out_specs, out_shape, scratch, flops, size):
    return pl.pallas_call(
        kernel,
        grid=(grid,),
        in_specs=in_specs,
        out_specs=out_specs,
        out_shape=jax.ShapeDtypeStruct(out_shape, jnp.float32),
        scratch_shapes=scratch,
        compiler_params=pltpu.CompilerParams(vmem_limit_bytes=VMEM, dimension_semantics=("arbitrary",)),
        cost_estimate=pl.CostEstimate(flops=int(flops), bytes_accessed=int(size), transcendentals=0),
        name=name,
    )


def exchange(values):
    return lax.all_to_all(values, ("seg", "fft"), split_axis=0, concat_axis=0, tiled=True)


def within_slab(values):
    segments = lax.axis_size("seg")
    segment = lax.axis_index("seg")
    pieces = []
    for i in range(segments):
        piece = lax.dynamic_index_in_dim(values, jnp.bitwise_xor(segment, i), 0, keepdims=False)
        pieces.append(lax.ppermute(piece, "seg", [(n, n ^ i) for n in range(segments)]) if i else piece)
    return pieces


def phase_pair(odd_rows, column, period):
    even = np.stack(turn(odd_rows * column, period), axis=-1)
    odd = np.stack(turn(odd_rows * (2 * column + 1), 2 * period), axis=-1)
    return np.concatenate([even, odd], axis=-1)


def per_device(voltage, chirp_phase):
    groups, segments = lax.axis_size("fft"), lax.axis_size("seg")
    group, segment = lax.axis_index("fft"), lax.axis_index("seg")
    count = groups * segments
    quarter, width = voltage.shape[2], voltage.shape[3]
    row_count, half = 4 * quarter, 2 * quarter
    columns = width * groups
    points = columns // LANES
    total = row_count * columns
    short = total // 2
    slots = half // groups
    tile = min(2 * LANES, width // 4)
    f32 = jnp.float32

    keys, lanes = np.arange(points), np.arange(LANES)
    twist = np.stack(
        [
            np.stack(turn(keys[:, None] * lanes[None, :], columns)),
            np.stack(turn(keys[:, None] * (2 * lanes[None, :] + 1), 2 * columns)),
        ]
    ).astype(np.float32)
    tables = []
    for cos, sin in (
        turn(lanes[:, None] * lanes[None, :], LANES),
        turn((2 * lanes[:, None] + 1) * lanes[None, :], 2 * LANES),
    ):
        tables.append(np.block([[cos, sin], [-sin, cos]]))
    column_tables = [twist, right_table(np.stack(tables + [table.T for table in tables]))]
    column_specs = [whole(table.shape) for table in column_tables]

    own_rows = max(SUB, quarter // count)
    odd_rows = 2 * np.arange(own_rows * count) + 1
    live = (odd_rows < 2 * quarter).astype(np.float64)
    cos, sin = turn(odd_rows[:, None] * np.arange(quarter)[None, :], 2 * half)
    row_table = np.stack([cos, sin], axis=1) * live[:, None, None]
    row_table = row_table.reshape(count, own_rows, 2, quarter).transpose(0, 2, 1, 3).reshape(-1, quarter)
    back_table = left_table(row_table.T / short)
    row_table = left_table(row_table)
    turns = np.stack(turn(odd_rows[:, None] * np.arange(width)[None, :], 2 * short))
    turns = turns.reshape(2, count, own_rows, width).transpose(1, 0, 2, 3).astype(np.float32)

    def row_phases(column_starts):
        table = phase_pair(odd_rows[None, :], column_starts[:, None], 2 * short)
        table = table.reshape(-1, count, own_rows, 4).transpose(0, 1, 3, 2)
        return table[..., None].astype(np.float32)

    phases = lax.dynamic_index_in_dim(jnp.asarray(row_phases(np.arange(groups) * width)), group, 0, keepdims=False)

    chirp_slots = max(SUB, slots // segments)
    holders = slots // chirp_slots
    blocks = chirp_slots // SUB
    start = jnp.minimum(segment, holders - 1) * chirp_slots
    own_phase = lax.dynamic_slice_in_dim(chirp_phase, start, chirp_slots, axis=1)
    angles = own_phase.reshape(2, blocks, SUB, LANES, points).transpose(0, 1, 4, 2, 3)
    angles = lax.all_gather(angles, "fft")
    block_width = columns // segments
    segment_word = segment.astype(jnp.int32).reshape(1)
    every = LANES * keys[:, None] + lanes[None, :]
    extra_turn = np.stack(
        [np.stack(turn(half * every, total)), np.stack(turn(half * (2 * every + 1), 2 * total))]
    ).astype(np.float32)
    mirror = np.stack(
        [np.stack(turn(every, columns)), np.stack(turn((1 - columns) * (2 * every + 1), 2 * columns))]
    ).astype(np.float32)
    grid_scratch = pltpu.VMEM((2, points * SUB, 2 * LANES), f32)
    sides_scratch = pltpu.VMEM((2, points * SUB, 2 * LANES), f32)
    chirp_columns = call(
        chirp_kernel,
        "chirp_columns",
        groups * blocks,
        [
            pl.BlockSpec(memory_space=pltpu.SMEM),
            pl.BlockSpec((1, 2, 1, points, SUB, LANES), lambda i: (i // blocks, 0, i % blocks, 0, 0, 0)),
        ]
        + column_specs
        + [whole(mirror.shape), whole(extra_turn.shape)],
        pl.BlockSpec((segments, 2, 2, SUB, block_width), lambda i: (0, 0, 0, i, 0)),
        (segments, 2, 2, groups * chirp_slots, block_width),
        [
            sides_scratch,
            pltpu.VMEM((2, 2, points * SUB, 2 * LANES), f32),
            pltpu.VMEM((2, 2, 2, points, SUB, LANES), f32),
        ],
        4e8 * blocks * groups,
        3e6 * groups,
    )(segment_word, angles, *column_tables, mirror, extra_turn)
    chirp_pieces = within_slab(chirp_columns)

    rows = np.arange(half)
    order = rows.reshape(groups, holders, chirp_slots).transpose(1, 0, 2)
    block_starts = np.arange(segments) * block_width
    chirp_turns = np.stack(turn(order[..., None] * np.arange(block_width), total), axis=2).astype(np.float32)
    chirp_phases = phase_pair(order[None], block_starts[:, None, None, None], total).transpose(0, 1, 2, 4, 3)
    chirp_phases = jnp.asarray(chirp_phases[..., None].astype(np.float32))
    cos, sin = turn(rows[None, :] * np.arange(row_count)[:, None], row_count)
    cos[:, 0] = 0.5
    sin[:, 0] = np.where(np.arange(row_count) % 2 == 0, 0.5, -0.5)
    taps_table = np.stack([cos, sin], axis=1).reshape(row_count, 2, groups, holders, chirp_slots) / total
    taps_table = left_table(taps_table.transpose(0, 3, 2, 1, 4).reshape(row_count, 2 * half))
    own_chirp_phases = lax.dynamic_index_in_dim(chirp_phases, segment, 0, keepdims=False)

    def of_slab(table, axis):
        shape = table.shape
        table = table.reshape(shape[:axis] + (segments, groups) + shape[axis + 1 :])
        table = jnp.asarray(np.ascontiguousarray(np.moveaxis(table, axis + 1, 0)))
        return lax.dynamic_index_in_dim(table, group, 0, keepdims=False)

    slab_phases = of_slab(row_phases(block_starts), 1)
    slab_phases = lax.dynamic_index_in_dim(slab_phases, segment, 0, keepdims=False)
    slab_turns = of_slab(turns[..., :block_width], 0)
    slab_rows = of_slab(row_table.reshape(count, 2 * own_rows, 3 * quarter), 0).reshape(-1, 3 * quarter)
    response_shape = (segments, 4, 2, 2, own_rows, block_width)
    piece_shape = chirp_pieces[0].shape
    response = call(
        response_kernel,
        "response",
        4,
        [pl.BlockSpec(memory_space=pltpu.SMEM)]
        + [whole(piece_shape)] * segments
        + [
            whole(chirp_turns.shape),
            whole(own_chirp_phases.shape),
            pl.BlockSpec((quarter, taps_table.shape[1]), lambda i: (i, 0)),
            whole(slab_rows.shape),
            whole(slab_turns.shape),
            whole(slab_phases.shape),
        ],
        pl.BlockSpec((segments, 1, 2, 2, own_rows, block_width), lambda i: (0, i, 0, 0, 0, 0)),
        response_shape,
        [pltpu.VMEM((6 * half, 2 * block_width), jnp.bfloat16)],
        1e10,
        2e7,
    )(segment_word, *chirp_pieces, chirp_turns, own_chirp_phases, taps_table, slab_rows, slab_turns, slab_phases)
    taps = within_slab(response)

    spread_shape = (count, 2, 2, own_rows, width)
    spread = call(
        spread_kernel,
        "spread",
        width // tile,
        [
            pl.BlockSpec((1, 2, quarter, tile), lambda c: (0, 0, 0, c)),
            whole(row_table.shape),
            pl.BlockSpec((count, 2, own_rows, tile), lambda c: (0, 0, 0, c)),
            whole(phases.shape),
        ],
        pl.BlockSpec((count, 2, 2, own_rows, tile), lambda c: (0, 0, 0, 0, c)),
        spread_shape,
        [],
        2e9,
        1e7,
    )(voltage, row_table, turns, phases)
    spread = exchange(spread).reshape(segments, groups, 2, 2, own_rows, width)

    cells = (points * SUB, 2 * LANES)
    spectrum = call(
        forward_kernel,
        "forward",
        segments,
        [pl.BlockSpec((1, groups, 2, 2, own_rows, width), lambda s: (s, 0, 0, 0, 0, 0))] + column_specs,
        pl.BlockSpec((1, 2) + cells, lambda s: (s, 0, 0, 0)),
        (segments, 2) + cells,
        [grid_scratch],
        2e9,
        1e7,
    )(spread, *column_tables)

    def lagged(i):
        return jnp.maximum(i - 4, 0)

    packed = call(
        apply_kernel,
        "apply",
        segments + 4,
        [pl.BlockSpec(memory_space=pltpu.SMEM)]
        + [pl.BlockSpec((1, 2, 2, own_rows, block_width), lambda i: (jnp.minimum(i, 3), 0, 0, 0, 0))] * segments
        + [pl.BlockSpec((1, 2) + cells, lambda i: (lagged(i), 0, 0, 0))]
        + column_specs,
        pl.BlockSpec((1, groups, 2, 2, own_rows, width), lambda i: (lagged(i), 0, 0, 0, 0, 0)),
        (segments, groups, 2, 2, own_rows, width),
        [
            pltpu.VMEM((segments, 2, 2, own_rows, block_width), f32),
            pltpu.VMEM((4, 2) + cells, f32),
            pltpu.VMEM((4, 2) + cells, f32),
            sides_scratch,
            grid_scratch,
        ],
        4e9,
        2e7,
    )(segment_word, *taps, spectrum, *column_tables)
    parts = exchange(packed.reshape(spread_shape))

    return call(
        gather_kernel,
        "gather",
        width // tile,
        [
            pl.BlockSpec((count, 2, 2, own_rows, tile), lambda c: (0, 0, 0, 0, c)),
            pl.BlockSpec((count, 2, own_rows, tile), lambda c: (0, 0, 0, c)),
            whole(phases.shape),
            whole(back_table.shape),
        ],
        pl.BlockSpec((1, 2, quarter, tile), lambda c: (0, 0, 0, c)),
        (1, 2, quarter, width),
        [],
        2e9,
        1e7,
    )(parts, turns, phases, back_table)


def solution(mesh):
    in_specs = (P("seg", None, None, "fft"), P(None, "fft", None))
    out_specs = P("seg", None, None, "fft")
    return jax.shard_map(per_device, mesh=mesh, in_specs=in_specs, out_specs=out_specs, check_vma=False)
```

```python
import math

import jax
import jax.numpy as jnp
import ml_dtypes
import numpy as np
from jax import lax
from jax.experimental import pallas as pl
from jax.experimental.pallas import tpu as pltpu
from jax.sharding import PartitionSpec as P

LANES = 128
SUB = 8
VMEM = 50 * 1024 * 1024


def turn(products, period):
    angles = np.mod(products, period).astype(np.float64) * (-2.0 * math.pi / period)
    return np.cos(angles), np.sin(angles)


def halves(table):
    high = table.astype(ml_dtypes.bfloat16)
    low = (table - high.astype(np.float64)).astype(ml_dtypes.bfloat16)
    return high, low


def split(values):
    high = values.astype(jnp.bfloat16)
    low = (values - high.astype(jnp.float32)).astype(jnp.bfloat16)
    return high, low


def thrice(values, axis):
    high, low = split(values)
    return jnp.concatenate([high, low, high] if axis == 0 else [high, high, low], axis=axis)


def right_table(table):
    high, low = halves(table)
    return np.concatenate([high, low, high], axis=-2)


def left_table(table):
    high, low = halves(table)
    return np.concatenate([high, high, low], axis=-1)


def dot(left, right):
    return jnp.dot(left, right, preferred_element_type=jnp.float32)


def scale_by(value, cos, sin):
    re, im = value
    near = 1e-12
    if abs(sin) < near:
        return value if cos > 0 else (-re, -im)
    if abs(cos) < near:
        return (-im, re) if sin > 0 else (im, -re)
    if abs(abs(cos) - abs(sin)) < near:
        size = abs(cos)
        first = re if cos > 0 else -re
        second = im if cos > 0 else -im
        third = im if sin > 0 else -im
        fourth = re if sin > 0 else -re
        return (first - third) * size, (second + fourth) * size
    return re * cos - im * sin, re * sin + im * cos


def plus(left, right):
    return left[0] + right[0], left[1] + right[1]


def minus(left, right):
    return left[0] - right[0], left[1] - right[1]


def small_dft(values, sign):
    count = len(values)
    if count == 1:
        return values
    if count == 2:
        return [plus(values[0], values[1]), minus(values[0], values[1])]
    if count == 4:
        even_sum, even_gap = plus(values[0], values[2]), minus(values[0], values[2])
        odd_sum, odd_gap = plus(values[1], values[3]), minus(values[1], values[3])
        turned = scale_by(odd_gap, 0.0, float(sign))
        return [plus(even_sum, odd_sum), plus(even_gap, turned), minus(even_sum, odd_sum), minus(even_gap, turned)]
    radix = 4 if count == 32 else 2
    part = count // radix
    pieces = [small_dft(values[i::radix], sign) for i in range(radix)]
    result = [None] * count
    for k in range(part):
        column = []
        for i in range(radix):
            angle = sign * 2.0 * math.pi * i * k / count
            column.append(scale_by(pieces[i][k], math.cos(angle), math.sin(angle)))
        for q, value in enumerate(small_dft(column, sign)):
            result[k + part * q] = value
    return result


def forward(value_at, twist, tables, grid):
    spectra = []
    for parity in range(2):
        values = [value_at(parity, j) for j in range(twist.shape[2])]
        for k, (re, im) in enumerate(small_dft(values, -1)):
            w_re, w_im = twist[parity, 0, pl.ds(k, 1)], twist[parity, 1, pl.ds(k, 1)]
            grid[parity, pl.ds(k * SUB, SUB), pl.ds(0, LANES)] = re * w_re - im * w_im
            grid[parity, pl.ds(k * SUB, SUB), pl.ds(LANES, LANES)] = re * w_im + im * w_re
        spectra.append(dot(thrice(grid[parity], 1), tables[parity]))
    even, odd = spectra
    return even + odd, even - odd


def backward(side, parity, twist, tables, grid, put):
    grid[parity] = dot(thrice(side, 1), tables[2 + parity])
    values = []
    for k in range(twist.shape[2]):
        re = grid[parity, pl.ds(k * SUB, SUB), pl.ds(0, LANES)]
        im = grid[parity, pl.ds(k * SUB, SUB), pl.ds(LANES, LANES)]
        w_re, w_im = twist[parity, 0, pl.ds(k, 1)], twist[parity, 1, pl.ds(k, 1)]
        values.append((re * w_re + im * w_im, im * w_re - re * w_im))
    for j, (re, im) in enumerate(small_dft(values, 1)):
        put(j, re, im)


def turned_by(angles):
    half = angles * 0.5
    square = half * half
    sin, cos = 0.0, 0.0
    for n in range(6, -1, -1):
        sin = sin * square + (-1.0) ** n / math.factorial(2 * n + 1)
        cos = cos * square + (-1.0) ** n / math.factorial(2 * n)
    sin = sin * half
    return 1.0 - 2.0 * sin * sin, 2.0 * sin * cos


def spread_kernel(x, table, turns, phases, out):
    count, slots, width = out.shape[0], out.shape[3], out.shape[4]
    sums = dot(table[...], thrice(jnp.concatenate([x[0, 0], x[0, 1]], axis=1), 0))
    sums = sums.reshape(count, 2, slots, 2 * width)
    turn_re, turn_im = turns[:, 0], turns[:, 1]
    for parity in range(2):
        lanes = slice(parity * width, (parity + 1) * width)
        ph_re, ph_im = phases[:, 2 * parity], phases[:, 2 * parity + 1]
        re, im = sums[:, 0, :, lanes], sums[:, 1, :, lanes]
        w_re = turn_re * ph_re - turn_im * ph_im
        w_im = turn_re * ph_im + turn_im * ph_re
        out[:, parity, 0] = re * w_re - im * w_im
        out[:, parity, 1] = re * w_im + im * w_re


def chirp_kernel(position, angles, twist, tables, mirror, extra_turn, out, sides, grid, held):
    first_rows = jnp.logical_and(position[0] == 0, pl.program_id(0) == 0)
    points = twist.shape[2]
    tiles = out.shape[4] // LANES

    def place(j):
        return j // tiles, pl.ds(j % tiles * LANES, LANES)

    for side in range(2):
        for k in range(points):
            cos, sin = turned_by(angles[0, side, 0, k])
            sides[side, pl.ds(k * SUB, SUB), pl.ds(0, LANES)] = cos
            sides[side, pl.ds(k * SUB, SUB), pl.ds(LANES, LANES)] = sin

    @pl.when(first_rows)
    def _():
        slot = lax.broadcasted_iota(jnp.int32, (SUB, LANES), 0)
        lane = lax.broadcasted_iota(jnp.int32, (SUB, LANES), 1)
        alive = jnp.logical_or(slot > 0, lane > 0)
        for part in range(2):
            lanes = pl.ds(part * LANES, LANES)
            sides[0, pl.ds(0, SUB), lanes] = jnp.where(alive, sides[0, pl.ds(0, SUB), lanes], 0.0)

    for parity in range(2):
        sign = 1.0 - 2.0 * parity
        for side in range(2):

            def put(j, re, im, parity=parity, side=side, sign=sign):
                held[parity, side, 0, j] = re
                held[parity, side, 1, j] = im
                if side == 1:
                    m_re, m_im = mirror[parity, 0, pl.ds(j, 1)], mirror[parity, 1, pl.ds(j, 1)]
                    to, lanes = place(j)
                    out[to, parity, 0, :, lanes] = held[parity, 0, 0, j] + sign * (re * m_re + im * m_im)
                    out[to, parity, 1, :, lanes] = held[parity, 0, 1, j] + sign * (re * m_im - im * m_re)

            backward(sides[side], parity, twist, tables, grid.at[side], put)

    @pl.when(first_rows)
    def _():
        keep = lax.broadcasted_iota(jnp.int32, (SUB, LANES), 0) > 0
        for parity in range(2):
            for j in range(points):
                w_re, w_im = extra_turn[parity, 0, pl.ds(j, 1)], extra_turn[parity, 1, pl.ds(j, 1)]
                near = 2.0 * held[parity, 0, 0, j]
                far = 2.0 * (held[parity, 1, 0, j] * w_re + held[parity, 1, 1, j] * w_im)
                to, lanes = place(j)
                out[to, parity, 0, :, lanes] = jnp.where(keep, out[to, parity, 0, :, lanes], near)
                out[to, parity, 1, :, lanes] = jnp.where(keep, out[to, parity, 1, :, lanes], far)


def response_kernel(segment, *refs):
    turns_in, phases_in, back_table, table, turns, phases, out, packed = refs[-8:]
    pieces = refs[:-8]
    holders, groups, slots, width = turns_in.shape[0], turns_in.shape[1], turns_in.shape[3], turns_in.shape[4]
    count, out_slots = out.shape[0], out.shape[4]
    depth = 2 * holders * groups * slots

    def fill(piece, source):
        for group in range(groups):
            t_re, t_im = turns_in[source, group, 0], turns_in[source, group, 1]
            base = pl.multiple_of((source * groups + group) * (2 * slots), 2 * slots)
            for parity in range(2):
                ph_re, ph_im = phases_in[source, group, 2 * parity], phases_in[source, group, 2 * parity + 1]
                w_re = t_re * ph_re - t_im * ph_im
                w_im = t_re * ph_im + t_im * ph_re
                own = pl.ds(group * slots, slots)
                re, im = piece[parity, 0, own], piece[parity, 1, own]
                lanes = pl.ds(parity * width, width)
                pair = jnp.concatenate([re * w_re + im * w_im, im * w_re - re * w_im], axis=0)
                high, low = split(pair)
                for n, value in enumerate((high, low, high)):
                    packed[pl.ds(n * depth + base, 2 * slots), lanes] = value

    @pl.when(pl.program_id(0) == 0)
    def _():
        for i, piece in enumerate(pieces):
            source = jnp.bitwise_xor(segment[0], i)
            pl.when(source < holders)(lambda piece=piece, source=source: fill(piece, source))

    taps = dot(back_table[...], packed[...])
    sums = dot(table[...], thrice(taps, 0)).reshape(count, 2, out_slots, 2 * width)
    turn_re, turn_im = turns[:, 0], turns[:, 1]
    for parity in range(2):
        lanes = slice(parity * width, (parity + 1) * width)
        ph_re, ph_im = phases[:, 2 * parity], phases[:, 2 * parity + 1]
        re, im = sums[:, 0, :, lanes], sums[:, 1, :, lanes]
        w_re = turn_re * ph_re - turn_im * ph_im
        w_im = turn_re * ph_im + turn_im * ph_re
        out[:, 0, parity, 0] = re * w_re - im * w_im
        out[:, 0, parity, 1] = re * w_im + im * w_re


def forward_kernel(x, twist, tables, out, grid):
    tiles = x.shape[5] // LANES

    def value_at(parity, j):
        group, tile = divmod(j, tiles)
        lanes = pl.ds(tile * LANES, LANES)
        return x[0, group, parity, 0, :, lanes], x[0, group, parity, 1, :, lanes]

    upper, lower = forward(value_at, twist, tables, grid)
    out[0, 0] = upper
    out[0, 1] = lower


def apply_kernel(segment, *refs):
    spectrum, twist, tables, out, taps, response, ring, sides, grid = refs[-9:]
    pieces = refs[:-9]
    step = pl.program_id(0)
    points = twist.shape[2]
    tiles = out.shape[5] // LANES
    block_tiles = taps.shape[4] // LANES

    @pl.when(step < 4)
    def _():
        for i, piece in enumerate(pieces):
            taps[jnp.bitwise_xor(segment[0], i)] = piece[0]

        def value_at(parity, j):
            lanes = pl.ds(j % block_tiles * LANES, LANES)
            return taps[j // block_tiles, parity, 0, :, lanes], taps[j // block_tiles, parity, 1, :, lanes]

        upper, lower = forward(value_at, twist, tables, grid)
        ring[step, 0] = upper
        ring[step, 1] = lower

    @pl.when(step == 3)
    def _():
        sign = 1.0 - 2.0 * (lax.broadcasted_iota(jnp.int32, (SUB, LANES), 0) % 2).astype(jnp.float32)
        re_lanes, im_lanes = pl.ds(0, LANES), pl.ds(LANES, LANES)
        for side in range(2):
            for k in range(points):
                rows = pl.ds(k * SUB, SUB)
                res = [ring[j, side, rows, re_lanes] for j in range(4)]
                ims = [ring[j, side, rows, im_lanes] for j in range(4)]
                for j in range(4):
                    response[j, side, rows, re_lanes] = res[j] - sign * ims[j - 1]
                    response[j, side, rows, im_lanes] = ims[j] + sign * res[j - 1]
        ring[...] = jnp.zeros_like(ring)

    @pl.when(step >= 4)
    def _():
        ring[lax.rem(step, 4)] = spectrum[0]
        slots = [lax.rem(step - j, 4) for j in range(4)]
        re_lanes, im_lanes = pl.ds(0, LANES), pl.ds(LANES, LANES)
        for k in range(points):
            rows = pl.ds(k * SUB, SUB)
            sums = []
            for side in range(2):
                total_re, total_im = 0.0, 0.0
                for j in range(4):
                    h_re, h_im = response[j, side, rows, re_lanes], response[j, side, rows, im_lanes]
                    x_re, x_im = ring[slots[j], side, rows, re_lanes], ring[slots[j], side, rows, im_lanes]
                    total_re += h_re * x_re - h_im * x_im
                    total_im += h_re * x_im + h_im * x_re
                sums.append((total_re, total_im))
            for parity, side in enumerate((plus(*sums), minus(*sums))):
                sides[parity, rows, re_lanes] = side[0]
                sides[parity, rows, im_lanes] = side[1]
        for parity in range(2):

            def put(j, re, im, parity=parity):
                group, tile = divmod(j, tiles)
                lanes = pl.ds(tile * LANES, LANES)
                out[0, group, parity, 0, :, lanes] = re
                out[0, group, parity, 1, :, lanes] = im

            backward(sides[parity], parity, twist, tables, grid, put)


def gather_kernel(parts, turns, phases, table, out):
    count, slots, width = parts.shape[0], parts.shape[3], parts.shape[4]
    turn_re, turn_im = turns[:, 0], turns[:, 1]
    columns = []
    for parity in range(2):
        ph_re, ph_im = phases[:, 2 * parity], phases[:, 2 * parity + 1]
        w_re = turn_re * ph_re - turn_im * ph_im
        w_im = turn_re * ph_im + turn_im * ph_re
        re, im = parts[:, parity, 0], parts[:, parity, 1]
        pair = jnp.stack([re * w_re + im * w_im, im * w_re - re * w_im], axis=1)
        columns.append(pair.reshape(count * 2 * slots, width))
    sums = dot(table[...], thrice(jnp.concatenate(columns, axis=1), 0))
    for parity in range(2):
        out[0, parity] = sums[:, parity * width : (parity + 1) * width]


def whole(shape):
    return pl.BlockSpec(shape, lambda i: (0,) * len(shape))


def call(kernel, name, grid, in_specs, out_specs, out_shape, scratch, flops, size):
    return pl.pallas_call(
        kernel,
        grid=(grid,),
        in_specs=in_specs,
        out_specs=out_specs,
        out_shape=jax.ShapeDtypeStruct(out_shape, jnp.float32),
        scratch_shapes=scratch,
        compiler_params=pltpu.CompilerParams(vmem_limit_bytes=VMEM, dimension_semantics=("arbitrary",)),
        cost_estimate=pl.CostEstimate(flops=int(flops), bytes_accessed=int(size), transcendentals=0),
        name=name,
    )


def exchange(values):
    return lax.all_to_all(values, ("seg", "fft"), split_axis=0, concat_axis=0, tiled=True)


def within_slab(values):
    segments = lax.axis_size("seg")
    segment = lax.axis_index("seg")
    pieces = []
    for i in range(segments):
        piece = lax.dynamic_index_in_dim(values, jnp.bitwise_xor(segment, i), 0, keepdims=False)
        pieces.append(lax.ppermute(piece, "seg", [(n, n ^ i) for n in range(segments)]) if i else piece)
    return pieces


def phase_pair(odd_rows, column, period):
    even = np.stack(turn(odd_rows * column, period), axis=-1)
    odd = np.stack(turn(odd_rows * (2 * column + 1), 2 * period), axis=-1)
    return np.concatenate([even, odd], axis=-1)


def per_device(voltage, chirp_phase):
    groups, segments = lax.axis_size("fft"), lax.axis_size("seg")
    group, segment = lax.axis_index("fft"), lax.axis_index("seg")
    count = groups * segments
    quarter, width = voltage.shape[2], voltage.shape[3]
    row_count, half = 4 * quarter, 2 * quarter
    columns = width * groups
    points = columns // LANES
    total = row_count * columns
    short = total // 2
    slots = half // groups
    tile = min(2 * LANES, width // 4)
    f32 = jnp.float32

    keys, lanes = np.arange(points), np.arange(LANES)
    twist = np.stack(
        [
            np.stack(turn(keys[:, None] * lanes[None, :], columns)),
            np.stack(turn(keys[:, None] * (2 * lanes[None, :] + 1), 2 * columns)),
        ]
    ).astype(np.float32)
    tables = []
    for cos, sin in (
        turn(lanes[:, None] * lanes[None, :], LANES),
        turn((2 * lanes[:, None] + 1) * lanes[None, :], 2 * LANES),
    ):
        tables.append(np.block([[cos, sin], [-sin, cos]]))
    column_tables = [twist, right_table(np.stack(tables + [table.T for table in tables]))]
    column_specs = [whole(table.shape) for table in column_tables]

    own_rows = max(SUB, quarter // count)
    odd_rows = 2 * np.arange(own_rows * count) + 1
    live = (odd_rows < 2 * quarter).astype(np.float64)
    cos, sin = turn(odd_rows[:, None] * np.arange(quarter)[None, :], 2 * half)
    row_table = np.stack([cos, sin], axis=1) * live[:, None, None]
    row_table = row_table.reshape(count, own_rows, 2, quarter).transpose(0, 2, 1, 3).reshape(-1, quarter)
    back_table = left_table(row_table.T / short)
    row_table = left_table(row_table)
    turns = np.stack(turn(odd_rows[:, None] * np.arange(width)[None, :], 2 * short))
    turns = turns.reshape(2, count, own_rows, width).transpose(1, 0, 2, 3).astype(np.float32)

    def row_phases(column_starts):
        table = phase_pair(odd_rows[None, :], column_starts[:, None], 2 * short)
        table = table.reshape(-1, count, own_rows, 4).transpose(0, 1, 3, 2)
        return table[..., None].astype(np.float32)

    phases = lax.dynamic_index_in_dim(jnp.asarray(row_phases(np.arange(groups) * width)), group, 0, keepdims=False)

    chirp_slots = max(SUB, slots // segments)
    holders = slots // chirp_slots
    blocks = chirp_slots // SUB
    start = jnp.minimum(segment, holders - 1) * chirp_slots
    own_phase = lax.dynamic_slice_in_dim(chirp_phase, start, chirp_slots, axis=1)
    angles = own_phase.reshape(2, blocks, SUB, LANES, points).transpose(0, 1, 4, 2, 3)
    spread_shape = (count, 2, 2, own_rows, width)
    spread = call(
        spread_kernel,
        "spread",
        width // tile,
        [
            pl.BlockSpec((1, 2, quarter, tile), lambda c: (0, 0, 0, c)),
            whole(row_table.shape),
            pl.BlockSpec((count, 2, own_rows, tile), lambda c: (0, 0, 0, c)),
            whole(phases.shape),
        ],
        pl.BlockSpec((count, 2, 2, own_rows, tile), lambda c: (0, 0, 0, 0, c)),
        spread_shape,
        [],
        2e9,
        1e7,
    )(voltage, row_table, turns, phases)
    angles, spread = lax.optimization_barrier((lax.all_gather(angles, "fft"), spread))
    block_width = columns // segments
    segment_word = segment.astype(jnp.int32).reshape(1)
    every = LANES * keys[:, None] + lanes[None, :]
    extra_turn = np.stack(
        [np.stack(turn(half * every, total)), np.stack(turn(half * (2 * every + 1), 2 * total))]
    ).astype(np.float32)
    mirror = np.stack(
        [np.stack(turn(every, columns)), np.stack(turn((1 - columns) * (2 * every + 1), 2 * columns))]
    ).astype(np.float32)
    grid_scratch = pltpu.VMEM((2, points * SUB, 2 * LANES), f32)
    sides_scratch = pltpu.VMEM((2, points * SUB, 2 * LANES), f32)
    chirp_columns = call(
        chirp_kernel,
        "chirp_columns",
        groups * blocks,
        [
            pl.BlockSpec(memory_space=pltpu.SMEM),
            pl.BlockSpec((1, 2, 1, points, SUB, LANES), lambda i: (i // blocks, 0, i % blocks, 0, 0, 0)),
        ]
        + column_specs
        + [whole(mirror.shape), whole(extra_turn.shape)],
        pl.BlockSpec((segments, 2, 2, SUB, block_width), lambda i: (0, 0, 0, i, 0)),
        (segments, 2, 2, groups * chirp_slots, block_width),
        [
            sides_scratch,
            pltpu.VMEM((2, 2, points * SUB, 2 * LANES), f32),
            pltpu.VMEM((2, 2, 2, points, SUB, LANES), f32),
        ],
        4e8 * blocks * groups,
        3e6 * groups,
    )(segment_word, angles, *column_tables, mirror, extra_turn)
    chirp_pieces = within_slab(chirp_columns)

    rows = np.arange(half)
    order = rows.reshape(groups, holders, chirp_slots).transpose(1, 0, 2)
    block_starts = np.arange(segments) * block_width
    chirp_turns = np.stack(turn(order[..., None] * np.arange(block_width), total), axis=2).astype(np.float32)
    chirp_phases = phase_pair(order[None], block_starts[:, None, None, None], total).transpose(0, 1, 2, 4, 3)
    chirp_phases = jnp.asarray(chirp_phases[..., None].astype(np.float32))
    cos, sin = turn(rows[None, :] * np.arange(row_count)[:, None], row_count)
    cos[:, 0] = 0.5
    sin[:, 0] = np.where(np.arange(row_count) % 2 == 0, 0.5, -0.5)
    taps_table = np.stack([cos, sin], axis=1).reshape(row_count, 2, groups, holders, chirp_slots) / total
    taps_table = left_table(taps_table.transpose(0, 3, 2, 1, 4).reshape(row_count, 2 * half))
    own_chirp_phases = lax.dynamic_index_in_dim(chirp_phases, segment, 0, keepdims=False)

    def of_slab(table, axis):
        shape = table.shape
        table = table.reshape(shape[:axis] + (segments, groups) + shape[axis + 1 :])
        table = jnp.asarray(np.ascontiguousarray(np.moveaxis(table, axis + 1, 0)))
        return lax.dynamic_index_in_dim(table, group, 0, keepdims=False)

    slab_phases = of_slab(row_phases(block_starts), 1)
    slab_phases = lax.dynamic_index_in_dim(slab_phases, segment, 0, keepdims=False)
    slab_turns = of_slab(turns[..., :block_width], 0)
    slab_rows = of_slab(row_table.reshape(count, 2 * own_rows, 3 * quarter), 0).reshape(-1, 3 * quarter)
    response_shape = (segments, 4, 2, 2, own_rows, block_width)
    piece_shape = chirp_pieces[0].shape
    response = call(
        response_kernel,
        "response",
        4,
        [pl.BlockSpec(memory_space=pltpu.SMEM)]
        + [whole(piece_shape)] * segments
        + [
            whole(chirp_turns.shape),
            whole(own_chirp_phases.shape),
            pl.BlockSpec((quarter, taps_table.shape[1]), lambda i: (i, 0)),
            whole(slab_rows.shape),
            whole(slab_turns.shape),
            whole(slab_phases.shape),
        ],
        pl.BlockSpec((segments, 1, 2, 2, own_rows, block_width), lambda i: (0, i, 0, 0, 0, 0)),
        response_shape,
        [pltpu.VMEM((6 * half, 2 * block_width), jnp.bfloat16)],
        1e10,
        2e7,
    )(segment_word, *chirp_pieces, chirp_turns, own_chirp_phases, taps_table, slab_rows, slab_turns, slab_phases)
    taps = within_slab(response)

    spread = exchange(spread).reshape(segments, groups, 2, 2, own_rows, width)

    cells = (points * SUB, 2 * LANES)
    spectrum = call(
        forward_kernel,
        "forward",
        segments,
        [pl.BlockSpec((1, groups, 2, 2, own_rows, width), lambda s: (s, 0, 0, 0, 0, 0))] + column_specs,
        pl.BlockSpec((1, 2) + cells, lambda s: (s, 0, 0, 0)),
        (segments, 2) + cells,
        [grid_scratch],
        2e9,
        1e7,
    )(spread, *column_tables)

    def lagged(i):
        return jnp.maximum(i - 4, 0)

    packed = call(
        apply_kernel,
        "apply",
        segments + 4,
        [pl.BlockSpec(memory_space=pltpu.SMEM)]
        + [pl.BlockSpec((1, 2, 2, own_rows, block_width), lambda i: (jnp.minimum(i, 3), 0, 0, 0, 0))] * segments
        + [pl.BlockSpec((1, 2) + cells, lambda i: (lagged(i), 0, 0, 0))]
        + column_specs,
        pl.BlockSpec((1, groups, 2, 2, own_rows, width), lambda i: (lagged(i), 0, 0, 0, 0, 0)),
        (segments, groups, 2, 2, own_rows, width),
        [
            pltpu.VMEM((segments, 2, 2, own_rows, block_width), f32),
            pltpu.VMEM((4, 2) + cells, f32),
            pltpu.VMEM((4, 2) + cells, f32),
            sides_scratch,
            grid_scratch,
        ],
        4e9,
        2e7,
    )(segment_word, *taps, spectrum, *column_tables)
    parts = exchange(packed.reshape(spread_shape))

    return call(
        gather_kernel,
        "gather",
        width // tile,
        [
            pl.BlockSpec((count, 2, 2, own_rows, tile), lambda c: (0, 0, 0, 0, c)),
            pl.BlockSpec((count, 2, own_rows, tile), lambda c: (0, 0, 0, c)),
            whole(phases.shape),
            whole(back_table.shape),
        ],
        pl.BlockSpec((1, 2, quarter, tile), lambda c: (0, 0, 0, c)),
        (1, 2, quarter, width),
        [],
        2e9,
        1e7,
    )(parts, turns, phases, back_table)


def solution(mesh):
    in_specs = (P("seg", None, None, "fft"), P(None, "fft", None))
    out_specs = P("seg", None, None, "fft")
    return jax.shard_map(per_device, mesh=mesh, in_specs=in_specs, out_specs=out_specs, check_vma=False)
```

```python
import math

import jax
import jax.numpy as jnp
import ml_dtypes
import numpy as np
from jax import lax
from jax.experimental import pallas as pl
from jax.experimental.pallas import tpu as pltpu
from jax.sharding import PartitionSpec as P

LANES = 128
SUB = 8
VMEM = 50 * 1024 * 1024


def turn(products, period):
    angles = np.mod(products, period).astype(np.float64) * (-2.0 * math.pi / period)
    return np.cos(angles), np.sin(angles)


def halves(table):
    high = table.astype(ml_dtypes.bfloat16)
    low = (table - high.astype(np.float64)).astype(ml_dtypes.bfloat16)
    return high, low


def split(values):
    high = values.astype(jnp.bfloat16)
    low = (values - high.astype(jnp.float32)).astype(jnp.bfloat16)
    return high, low


def thrice(values, axis):
    high, low = split(values)
    return jnp.concatenate([high, low, high] if axis == 0 else [high, high, low], axis=axis)


def right_table(table):
    high, low = halves(table)
    return np.concatenate([high, low, high], axis=-2)


def left_table(table):
    high, low = halves(table)
    return np.concatenate([high, high, low], axis=-1)


def dot(left, right):
    return jnp.dot(left, right, preferred_element_type=jnp.float32)


def scale_by(value, cos, sin):
    re, im = value
    near = 1e-12
    if abs(sin) < near:
        return value if cos > 0 else (-re, -im)
    if abs(cos) < near:
        return (-im, re) if sin > 0 else (im, -re)
    if abs(abs(cos) - abs(sin)) < near:
        size = abs(cos)
        first = re if cos > 0 else -re
        second = im if cos > 0 else -im
        third = im if sin > 0 else -im
        fourth = re if sin > 0 else -re
        return (first - third) * size, (second + fourth) * size
    return re * cos - im * sin, re * sin + im * cos


def plus(left, right):
    return left[0] + right[0], left[1] + right[1]


def minus(left, right):
    return left[0] - right[0], left[1] - right[1]


def small_dft(values, sign):
    count = len(values)
    if count == 1:
        return values
    if count == 2:
        return [plus(values[0], values[1]), minus(values[0], values[1])]
    if count == 4:
        even_sum, even_gap = plus(values[0], values[2]), minus(values[0], values[2])
        odd_sum, odd_gap = plus(values[1], values[3]), minus(values[1], values[3])
        turned = scale_by(odd_gap, 0.0, float(sign))
        return [plus(even_sum, odd_sum), plus(even_gap, turned), minus(even_sum, odd_sum), minus(even_gap, turned)]
    radix = 4 if count == 32 else 2
    part = count // radix
    pieces = [small_dft(values[i::radix], sign) for i in range(radix)]
    result = [None] * count
    for k in range(part):
        column = []
        for i in range(radix):
            angle = sign * 2.0 * math.pi * i * k / count
            column.append(scale_by(pieces[i][k], math.cos(angle), math.sin(angle)))
        for q, value in enumerate(small_dft(column, sign)):
            result[k + part * q] = value
    return result


def forward(value_at, twist, tables, grid):
    spectra = []
    for parity in range(2):
        values = [value_at(parity, j) for j in range(twist.shape[2])]
        for k, (re, im) in enumerate(small_dft(values, -1)):
            w_re, w_im = twist[parity, 0, pl.ds(k, 1)], twist[parity, 1, pl.ds(k, 1)]
            grid[parity, pl.ds(k * SUB, SUB), pl.ds(0, LANES)] = re * w_re - im * w_im
            grid[parity, pl.ds(k * SUB, SUB), pl.ds(LANES, LANES)] = re * w_im + im * w_re
        spectra.append(dot(thrice(grid[parity], 1), tables[parity]))
    even, odd = spectra
    return even + odd, even - odd


def backward(side, parity, twist, table, grid, put):
    grid[parity] = dot(thrice(side, 1), table)
    values = []
    for k in range(twist.shape[2]):
        re = grid[parity, pl.ds(k * SUB, SUB), pl.ds(0, LANES)]
        im = grid[parity, pl.ds(k * SUB, SUB), pl.ds(LANES, LANES)]
        w_re, w_im = twist[parity, 0, pl.ds(k, 1)], twist[parity, 1, pl.ds(k, 1)]
        values.append((re * w_re + im * w_im, im * w_re - re * w_im))
    for j, (re, im) in enumerate(small_dft(values, 1)):
        put(j, re, im)


def turned_by(angles):
    half = angles * 0.5
    square = half * half
    sin, cos = 0.0, 0.0
    for n in range(6, -1, -1):
        sin = sin * square + (-1.0) ** n / math.factorial(2 * n + 1)
        cos = cos * square + (-1.0) ** n / math.factorial(2 * n)
    sin = sin * half
    return 1.0 - 2.0 * sin * sin, 2.0 * sin * cos


def spread_kernel(x, table, turns, phases, out):
    count, slots, width = out.shape[0], out.shape[3], out.shape[4]
    sums = dot(table[...], thrice(jnp.concatenate([x[0, 0], x[0, 1]], axis=1), 0))
    sums = sums.reshape(count, 2, slots, 2 * width)
    turn_re, turn_im = turns[:, 0], turns[:, 1]
    for parity in range(2):
        lanes = slice(parity * width, (parity + 1) * width)
        ph_re, ph_im = phases[:, 2 * parity], phases[:, 2 * parity + 1]
        re, im = sums[:, 0, :, lanes], sums[:, 1, :, lanes]
        w_re = turn_re * ph_re - turn_im * ph_im
        w_im = turn_re * ph_im + turn_im * ph_re
        out[:, parity, 0] = re * w_re - im * w_im
        out[:, parity, 1] = re * w_im + im * w_re


def digits_swapped(tiles):
    lane = lax.broadcasted_iota(jnp.int32, tiles[0].shape, 1)
    step = 1
    while step < len(tiles):
        low_half = jnp.bitwise_and(lane, step) == 0
        swapped = list(tiles)
        for k in range(len(tiles)):
            if k & step == 0:
                first, second = tiles[k], tiles[k + step]
                swapped[k] = jnp.where(low_half, first, pltpu.roll(second, step, 1))
                swapped[k + step] = jnp.where(low_half, pltpu.roll(first, LANES - step, 1), second)
        tiles = swapped
        step *= 2
    return tiles


def chirp_kernel(place, angles, twist, tables, mirror, extra_turn, out, sides, grid, held):
    first_rows = jnp.logical_and(place[0] == 0, pl.program_id(0) == 0)
    points = twist.shape[2]
    for side in range(2):
        tiles = [angles[side, :, pl.ds(k * LANES, LANES)] for k in range(points)]
        for k, value in enumerate(digits_swapped(tiles)):
            cos, sin = turned_by(value)
            sides[side, pl.ds(k * SUB, SUB), pl.ds(0, LANES)] = cos
            sides[side, pl.ds(k * SUB, SUB), pl.ds(LANES, LANES)] = sin

    @pl.when(first_rows)
    def _():
        slot = lax.broadcasted_iota(jnp.int32, (SUB, LANES), 0)
        lane = lax.broadcasted_iota(jnp.int32, (SUB, LANES), 1)
        alive = jnp.logical_or(slot > 0, lane > 0)
        for part in range(2):
            lanes = pl.ds(part * LANES, LANES)
            sides[0, pl.ds(0, SUB), lanes] = jnp.where(alive, sides[0, pl.ds(0, SUB), lanes], 0.0)

    for parity in range(2):
        sign = 1.0 - 2.0 * parity
        for side in range(2):

            def put(j, re, im, parity=parity, side=side, sign=sign):
                held[parity, side, 0, j] = re
                held[parity, side, 1, j] = im
                if side == 1:
                    m_re, m_im = mirror[parity, 0, pl.ds(j, 1)], mirror[parity, 1, pl.ds(j, 1)]
                    out[j, parity, 0] = held[parity, 0, 0, j] + sign * (re * m_re + im * m_im)
                    out[j, parity, 1] = held[parity, 0, 1, j] + sign * (re * m_im - im * m_re)

            backward(sides[side], parity, twist, tables[parity], grid.at[side], put)

    @pl.when(first_rows)
    def _():
        keep = lax.broadcasted_iota(jnp.int32, (SUB, LANES), 0) > 0
        for parity in range(2):
            for j in range(points):
                w_re, w_im = extra_turn[parity, 0, pl.ds(j, 1)], extra_turn[parity, 1, pl.ds(j, 1)]
                near = 2.0 * held[parity, 0, 0, j]
                far = 2.0 * (held[parity, 1, 0, j] * w_re + held[parity, 1, 1, j] * w_im)
                out[j, parity, 0] = jnp.where(keep, out[j, parity, 0], near)
                out[j, parity, 1] = jnp.where(keep, out[j, parity, 1], far)


def response_kernel(parts, turns_in, phases_in, back_table, table, turns, phases, out, packed):
    sources, slots = parts.shape[0], parts.shape[3]
    count, out_slots = out.shape[0], out.shape[4]
    depth = 2 * sources * slots

    @pl.when(pl.program_id(0) == 0)
    def _():
        for source in range(sources):
            t_re, t_im = turns_in[source, 0], turns_in[source, 1]
            for parity in range(2):
                ph_re, ph_im = phases_in[source, 2 * parity], phases_in[source, 2 * parity + 1]
                w_re = t_re * ph_re - t_im * ph_im
                w_im = t_re * ph_im + t_im * ph_re
                re, im = parts[source, parity, 0], parts[source, parity, 1]
                lanes = pl.ds(parity * LANES, LANES)
                pair = jnp.concatenate([re * w_re + im * w_im, im * w_re - re * w_im], axis=0)
                high, low = split(pair)
                for n, value in enumerate((high, low, high)):
                    packed[pl.ds(n * depth + 2 * source * slots, 2 * slots), lanes] = value

    taps = dot(back_table[...], packed[...])
    sums = dot(table[...], thrice(taps, 0)).reshape(count, 2, out_slots, 2 * LANES)
    turn_re, turn_im = turns[:, 0], turns[:, 1]
    for parity in range(2):
        lanes = slice(parity * LANES, (parity + 1) * LANES)
        ph_re, ph_im = phases[:, 2 * parity], phases[:, 2 * parity + 1]
        re, im = sums[:, 0, :, lanes], sums[:, 1, :, lanes]
        w_re = turn_re * ph_re - turn_im * ph_im
        w_im = turn_re * ph_im + turn_im * ph_re
        out[:, 0, parity, 0] = re * w_re - im * w_im
        out[:, 0, parity, 1] = re * w_im + im * w_re


def forward_kernel(x, twist, tables, out, grid):
    tiles = x.shape[5] // LANES
    for n in range(x.shape[0]):

        def value_at(parity, j, n=n):
            group, tile = divmod(j, tiles)
            lanes = pl.ds(tile * LANES, LANES)
            return x[n, group, parity, 0, :, lanes], x[n, group, parity, 1, :, lanes]

        upper, lower = forward(value_at, twist, tables, grid.at[n])
        out[n, 0] = upper
        out[n, 1] = lower


def apply_kernel(taps, spectrum, twist, tables, out, raw, response, past, sides, grid):
    step = pl.program_id(0)
    points = twist.shape[2]
    tiles = out.shape[5] // LANES
    re_lanes, im_lanes = pl.ds(0, LANES), pl.ds(LANES, LANES)

    @pl.when(step == 0)
    def _():
        past[...] = jnp.zeros_like(past)

    @pl.when(step < 2)
    def _():
        for n in range(2):

            def value_at(parity, j, n=n):
                return taps[j, n, parity, 0], taps[j, n, parity, 1]

            upper, lower = forward(value_at, twist, tables, grid.at[n])
            raw[2 * step + n, 0] = upper
            raw[2 * step + n, 1] = lower

    @pl.when(step == 1)
    def _():
        sign = 1.0 - 2.0 * (lax.broadcasted_iota(jnp.int32, (SUB, LANES), 0) % 2).astype(jnp.float32)
        for side in range(2):
            for k in range(points):
                rows = pl.ds(k * SUB, SUB)
                res = [raw[j, side, rows, re_lanes] for j in range(4)]
                ims = [raw[j, side, rows, im_lanes] for j in range(4)]
                for j in range(4):
                    response[j, side, rows, re_lanes] = res[j] - sign * ims[j - 1]
                    response[j, side, rows, im_lanes] = ims[j] + sign * res[j - 1]

    @pl.when(step >= 2)
    def _():
        window = [past.at[n] for n in range(3)] + [spectrum.at[n] for n in range(2)]
        for k in range(points):
            rows = pl.ds(k * SUB, SUB)
            sums = [[], []]
            for side in range(2):
                xs = [(ref[side, rows, re_lanes], ref[side, rows, im_lanes]) for ref in window]
                totals = [None, None]
                for j in range(4):
                    h_re, h_im = response[j, side, rows, re_lanes], response[j, side, rows, im_lanes]
                    for n in range(2):
                        x_re, x_im = xs[3 + n - j]
                        term = h_re * x_re - h_im * x_im, h_re * x_im + h_im * x_re
                        totals[n] = term if j == 0 else plus(totals[n], term)
                for n in range(2):
                    sums[n].append(totals[n])
            for n in range(2):
                for parity, value in enumerate((plus(*sums[n]), minus(*sums[n]))):
                    sides[n, parity, rows, re_lanes] = value[0]
                    sides[n, parity, rows, im_lanes] = value[1]
        for n in range(2):
            for parity in range(2):

                def put(j, re, im, n=n, parity=parity):
                    group, tile = divmod(j, tiles)
                    lanes = pl.ds(tile * LANES, LANES)
                    out[n, group, parity, 0, :, lanes] = re
                    out[n, group, parity, 1, :, lanes] = im

                backward(sides[n, parity], parity, twist, tables[2 + parity], grid.at[n], put)
        past[0] = past[2]
        past[1] = spectrum[0]
        past[2] = spectrum[1]


def gather_kernel(parts, turns, phases, table, out):
    count, slots, width = parts.shape[0], parts.shape[3], parts.shape[4]
    turn_re, turn_im = turns[:, 0], turns[:, 1]
    columns = []
    for parity in range(2):
        ph_re, ph_im = phases[:, 2 * parity], phases[:, 2 * parity + 1]
        w_re = turn_re * ph_re - turn_im * ph_im
        w_im = turn_re * ph_im + turn_im * ph_re
        re, im = parts[:, parity, 0], parts[:, parity, 1]
        pair = jnp.stack([re * w_re + im * w_im, im * w_re - re * w_im], axis=1)
        columns.append(pair.reshape(count * 2 * slots, width))
    sums = dot(table[...], thrice(jnp.concatenate(columns, axis=1), 0))
    for parity in range(2):
        out[0, parity] = sums[:, parity * width : (parity + 1) * width]


def whole(shape):
    return pl.BlockSpec(shape, lambda i, *_: (0,) * len(shape))


def call(kernel, name, grid, in_specs, out_specs, out_shape, scratch, flops, size, scalars=0):
    return pl.pallas_call(
        kernel,
        grid_spec=pltpu.PrefetchScalarGridSpec(
            num_scalar_prefetch=scalars,
            grid=(grid,),
            in_specs=in_specs,
            out_specs=out_specs,
            scratch_shapes=scratch,
        ),
        out_shape=jax.ShapeDtypeStruct(out_shape, jnp.float32),
        compiler_params=pltpu.CompilerParams(vmem_limit_bytes=VMEM, dimension_semantics=("arbitrary",)),
        cost_estimate=pl.CostEstimate(flops=int(flops), bytes_accessed=int(size), transcendentals=0),
        name=name,
    )


def exchange(values):
    return lax.all_to_all(values, ("seg", "fft"), split_axis=0, concat_axis=0, tiled=True)


def phase_pair(odd_rows, column, period):
    even = np.stack(turn(odd_rows * column, period), axis=-1)
    odd = np.stack(turn(odd_rows * (2 * column + 1), 2 * period), axis=-1)
    return np.concatenate([even, odd], axis=-1)


def per_device(voltage, chirp_phase):
    groups, segments = lax.axis_size("fft"), lax.axis_size("seg")
    group, segment = lax.axis_index("fft"), lax.axis_index("seg")
    count = groups * segments
    position = segment * groups + group
    quarter, width = voltage.shape[2], voltage.shape[3]
    row_count, half = 4 * quarter, 2 * quarter
    columns = width * groups
    points = columns // LANES
    total = row_count * columns
    short = total // 2
    slots = half // groups
    tile, narrow = min(2 * LANES, width // 4), LANES
    f32 = jnp.float32

    keys, lanes = np.arange(points), np.arange(LANES)
    twist = np.stack(
        [
            np.stack(turn(keys[:, None] * lanes[None, :], columns)),
            np.stack(turn(keys[:, None] * (2 * lanes[None, :] + 1), 2 * columns)),
        ]
    ).astype(np.float32)
    tables = []
    for cos, sin in (
        turn(lanes[:, None] * lanes[None, :], LANES),
        turn((2 * lanes[:, None] + 1) * lanes[None, :], 2 * LANES),
    ):
        tables.append(np.block([[cos, sin], [-sin, cos]]))
    column_tables = [twist, right_table(np.stack(tables + [table.T for table in tables]))]
    digit_order = (LANES // points * (lanes % points) + lanes // points).astype(np.int64)
    digit_order = np.concatenate([digit_order, LANES + digit_order])
    swapped_tables = right_table(np.stack([table.T[digit_order] for table in tables]))
    column_specs = [whole(table.shape) for table in column_tables]

    own_rows = max(SUB, quarter // count)
    odd_rows = 2 * np.arange(own_rows * count) + 1
    live = (odd_rows < 2 * quarter).astype(np.float64)
    cos, sin = turn(odd_rows[:, None] * np.arange(quarter)[None, :], 2 * half)
    row_table = np.stack([cos, sin], axis=1) * live[:, None, None]
    row_table = row_table.reshape(count, own_rows, 2, quarter).transpose(0, 2, 1, 3).reshape(-1, quarter)
    back_table = left_table(row_table.T / short)
    row_table = left_table(row_table)
    turns = np.stack(turn(odd_rows[:, None] * np.arange(width)[None, :], 2 * short))
    turns = turns.reshape(2, count, own_rows, width).transpose(1, 0, 2, 3).astype(np.float32)

    def row_phases(column_starts):
        table = phase_pair(odd_rows[None, :], column_starts[:, None], 2 * short)
        table = table.reshape(-1, count, own_rows, 4).transpose(0, 1, 3, 2)
        return jnp.asarray(table[..., None].astype(np.float32))

    phases = lax.dynamic_index_in_dim(row_phases(np.arange(groups) * width), group, 0, keepdims=False)

    chirp_slots = max(SUB, slots // segments)
    holders = slots // chirp_slots
    blocks = chirp_slots // SUB
    start = jnp.minimum(segment, holders - 1) * blocks
    place = jnp.stack([position, start]).astype(jnp.int32)
    every = LANES * keys[:, None] + lanes[None, :]
    extra_turn = np.stack(
        [np.stack(turn(half * every, total)), np.stack(turn(half * (2 * every + 1), 2 * total))]
    ).astype(np.float32)
    mirror = np.stack(
        [np.stack(turn(every, columns)), np.stack(turn((1 - columns) * (2 * every + 1), 2 * columns))]
    ).astype(np.float32)
    cells = (points * SUB, 2 * LANES)
    chirp_columns = call(
        chirp_kernel,
        "chirp_columns",
        blocks,
        [
            pl.BlockSpec((2, SUB, columns), lambda i, place: (0, place[1] + i, 0)),
            whole(twist.shape),
            whole(swapped_tables.shape),
            whole(mirror.shape),
            whole(extra_turn.shape),
        ],
        pl.BlockSpec((points, 2, 2, SUB, LANES), lambda i, place: (0, 0, 0, i, 0)),
        (points, 2, 2, chirp_slots, LANES),
        [
            pltpu.VMEM((2,) + cells, f32),
            pltpu.VMEM((2, 2) + cells, f32),
            pltpu.VMEM((2, 2, 2, points, SUB, LANES), f32),
        ],
        4e8 * blocks,
        3e6,
        scalars=1,
    )(place, chirp_phase, twist, swapped_tables, mirror, extra_turn)
    if holders < segments:
        chirp_columns = jnp.where(segment < holders, chirp_columns, 0.0)
    if count > points:
        chirp_columns = jnp.pad(chirp_columns, ((0, count - points),) + ((0, 0),) * 4)
    chirp_parts = exchange(chirp_columns)[: holders * groups]

    rows = np.arange(half)
    order = rows.reshape(groups, holders, chirp_slots).transpose(1, 0, 2)
    chirp_turns = np.stack(turn(order[..., None] * lanes, total), axis=2).astype(np.float32)
    block_of = np.arange(points)
    chirp_phases = phase_pair(order[None], LANES * block_of[:, None, None, None], total)
    chirp_phases = chirp_phases.reshape(points, holders * groups, chirp_slots, 4).transpose(0, 1, 3, 2)
    chirp_phases = jnp.asarray(chirp_phases[..., None].astype(np.float32))
    chirp_turns = chirp_turns.reshape(holders * groups, 2, chirp_slots, LANES)
    cos, sin = turn(rows[None, :] * np.arange(row_count)[:, None], row_count)
    cos[:, 0] = 0.5
    sin[:, 0] = np.where(np.arange(row_count) % 2 == 0, 0.5, -0.5)
    taps_table = np.stack([cos, sin], axis=1).reshape(row_count, 2, groups, holders, chirp_slots) / total
    taps_table = taps_table.transpose(0, 3, 2, 1, 4).reshape(row_count, 2 * half)
    taps_table = left_table(taps_table)
    own_block = jnp.minimum(position, points - 1)
    own_chirp_phases = lax.dynamic_index_in_dim(chirp_phases, own_block, 0, keepdims=False)
    own_row_phases = lax.dynamic_index_in_dim(row_phases(block_of * LANES), own_block, 0, keepdims=False)
    response_shape = (count, 4, 2, 2, own_rows, LANES)
    response = call(
        response_kernel,
        "response",
        4,
        [
            whole(chirp_parts.shape),
            whole(chirp_turns.shape),
            whole(own_chirp_phases.shape),
            pl.BlockSpec((quarter, taps_table.shape[1]), lambda i: (i, 0)),
            whole(row_table.shape),
            pl.BlockSpec((count, 2, own_rows, LANES), lambda i: (0, 0, 0, 0)),
            whole(own_row_phases.shape),
        ],
        pl.BlockSpec((count, 1, 2, 2, own_rows, LANES), lambda i: (0, i, 0, 0, 0, 0)),
        response_shape,
        [pltpu.VMEM((6 * half, 2 * LANES), jnp.bfloat16)],
        5e9,
        1e7,
    )(chirp_parts, chirp_turns, own_chirp_phases, taps_table, row_table, turns, own_row_phases)
    taps = exchange(response)[:points]

    spread_shape = (count, 2, 2, own_rows, width)
    spread = call(
        spread_kernel,
        "spread",
        width // tile,
        [
            pl.BlockSpec((1, 2, quarter, tile), lambda c: (0, 0, 0, c)),
            whole(row_table.shape),
            pl.BlockSpec((count, 2, own_rows, tile), lambda c: (0, 0, 0, c)),
            whole(phases.shape),
        ],
        pl.BlockSpec((count, 2, 2, own_rows, tile), lambda c: (0, 0, 0, 0, c)),
        spread_shape,
        [],
        2e9,
        1e7,
    )(voltage, row_table, turns, phases)
    spread = exchange(spread).reshape(segments, groups, 2, 2, own_rows, width)

    pair_scratch = pltpu.VMEM((2, 2) + cells, f32)
    spectrum = call(
        forward_kernel,
        "forward",
        segments // 2,
        [pl.BlockSpec((2, groups, 2, 2, own_rows, width), lambda s: (s, 0, 0, 0, 0, 0))] + column_specs,
        pl.BlockSpec((2, 2) + cells, lambda s: (s, 0, 0, 0)),
        (segments, 2) + cells,
        [pair_scratch],
        2e9,
        1e7,
    )(spread, *column_tables)

    def lagged(i):
        return jnp.maximum(i - 2, 0)

    packed = call(
        apply_kernel,
        "apply",
        segments // 2 + 2,
        [
            pl.BlockSpec((points, 2, 2, 2, own_rows, LANES), lambda i: (0, jnp.minimum(i, 1), 0, 0, 0, 0)),
            pl.BlockSpec((2, 2) + cells, lambda i: (lagged(i), 0, 0, 0)),
        ]
        + column_specs,
        pl.BlockSpec((2, groups, 2, 2, own_rows, width), lambda i: (lagged(i), 0, 0, 0, 0, 0)),
        (segments, groups, 2, 2, own_rows, width),
        [
            pltpu.VMEM((4, 2) + cells, f32),
            pltpu.VMEM((4, 2) + cells, f32),
            pltpu.VMEM((3, 2) + cells, f32),
            pair_scratch,
            pair_scratch,
        ],
        4e9,
        2e7,
    )(taps, spectrum, *column_tables)
    parts = exchange(packed.reshape(spread_shape))

    return call(
        gather_kernel,
        "gather",
        width // narrow,
        [
            pl.BlockSpec((count, 2, 2, own_rows, narrow), lambda c: (0, 0, 0, 0, c)),
            pl.BlockSpec((count, 2, own_rows, narrow), lambda c: (0, 0, 0, c)),
            whole(phases.shape),
            whole(back_table.shape),
        ],
        pl.BlockSpec((1, 2, quarter, narrow), lambda c: (0, 0, 0, c)),
        (1, 2, quarter, width),
        [],
        2e9,
        1e7,
    )(parts, turns, phases, back_table)


def solution(mesh):
    in_specs = (P("seg", None, None, "fft"), P(None, "fft", None))
    out_specs = P("seg", None, None, "fft")
    return jax.shard_map(per_device, mesh=mesh, in_specs=in_specs, out_specs=out_specs, check_vma=False)
```

```python
import math

import jax
import jax.numpy as jnp
import ml_dtypes
import numpy as np
from jax import lax
from jax.experimental import pallas as pl
from jax.experimental.pallas import tpu as pltpu
from jax.sharding import PartitionSpec as P

LANES = 128
SUB = 8
VMEM = 50 * 1024 * 1024


def turn(products, period):
    angles = np.mod(products, period).astype(np.float64) * (-2.0 * math.pi / period)
    return np.cos(angles), np.sin(angles)


def halves(table):
    high = table.astype(ml_dtypes.bfloat16)
    low = (table - high.astype(np.float64)).astype(ml_dtypes.bfloat16)
    return high, low


def split(values):
    high = values.astype(jnp.bfloat16)
    low = (values - high.astype(jnp.float32)).astype(jnp.bfloat16)
    return high, low


def thrice(values, axis):
    high, low = split(values)
    return jnp.concatenate([high, low, high] if axis == 0 else [high, high, low], axis=axis)


def right_table(table):
    high, low = halves(table)
    return np.concatenate([high, low, high], axis=-2)


def left_table(table):
    high, low = halves(table)
    return np.concatenate([high, high, low], axis=-1)


def dot(left, right):
    return jnp.dot(left, right, preferred_element_type=jnp.float32)


def scale_by(value, cos, sin):
    re, im = value
    near = 1e-12
    if abs(sin) < near:
        return value if cos > 0 else (-re, -im)
    if abs(cos) < near:
        return (-im, re) if sin > 0 else (im, -re)
    if abs(abs(cos) - abs(sin)) < near:
        size = abs(cos)
        first = re if cos > 0 else -re
        second = im if cos > 0 else -im
        third = im if sin > 0 else -im
        fourth = re if sin > 0 else -re
        return (first - third) * size, (second + fourth) * size
    return re * cos - im * sin, re * sin + im * cos


def plus(left, right):
    return left[0] + right[0], left[1] + right[1]


def minus(left, right):
    return left[0] - right[0], left[1] - right[1]


def small_dft(values, sign):
    count = len(values)
    if count == 1:
        return values
    if count == 2:
        return [plus(values[0], values[1]), minus(values[0], values[1])]
    if count == 4:
        even_sum, even_gap = plus(values[0], values[2]), minus(values[0], values[2])
        odd_sum, odd_gap = plus(values[1], values[3]), minus(values[1], values[3])
        turned = scale_by(odd_gap, 0.0, float(sign))
        return [plus(even_sum, odd_sum), plus(even_gap, turned), minus(even_sum, odd_sum), minus(even_gap, turned)]
    radix = 4 if count == 32 else 2
    part = count // radix
    pieces = [small_dft(values[i::radix], sign) for i in range(radix)]
    result = [None] * count
    for k in range(part):
        column = []
        for i in range(radix):
            angle = sign * 2.0 * math.pi * i * k / count
            column.append(scale_by(pieces[i][k], math.cos(angle), math.sin(angle)))
        for q, value in enumerate(small_dft(column, sign)):
            result[k + part * q] = value
    return result


def forward(value_at, twist, tables, grid):
    spectra = []
    for parity in range(2):
        values = [value_at(parity, j) for j in range(twist.shape[2])]
        for k, (re, im) in enumerate(small_dft(values, -1)):
            w_re, w_im = twist[parity, 0, pl.ds(k, 1)], twist[parity, 1, pl.ds(k, 1)]
            grid[parity, pl.ds(k * SUB, SUB), pl.ds(0, LANES)] = re * w_re - im * w_im
            grid[parity, pl.ds(k * SUB, SUB), pl.ds(LANES, LANES)] = re * w_im + im * w_re
        spectra.append(dot(thrice(grid[parity], 1), tables[parity]))
    even, odd = spectra
    return even + odd, even - odd


def backward(side, parity, twist, table, grid, put):
    grid[parity] = dot(thrice(side, 1), table)
    values = []
    for k in range(twist.shape[2]):
        re = grid[parity, pl.ds(k * SUB, SUB), pl.ds(0, LANES)]
        im = grid[parity, pl.ds(k * SUB, SUB), pl.ds(LANES, LANES)]
        w_re, w_im = twist[parity, 0, pl.ds(k, 1)], twist[parity, 1, pl.ds(k, 1)]
        values.append((re * w_re + im * w_im, im * w_re - re * w_im))
    for j, (re, im) in enumerate(small_dft(values, 1)):
        put(j, re, im)


def turned_by(angles):
    half = angles * 0.5
    square = half * half
    sin, cos = 0.0, 0.0
    for n in range(6, -1, -1):
        sin = sin * square + (-1.0) ** n / math.factorial(2 * n + 1)
        cos = cos * square + (-1.0) ** n / math.factorial(2 * n)
    sin = sin * half
    return 1.0 - 2.0 * sin * sin, 2.0 * sin * cos


def spread_kernel(x, table, turns, phases, out):
    count, slots, width = out.shape[0], out.shape[3], out.shape[4]
    sums = dot(table[...], thrice(jnp.concatenate([x[0, 0], x[0, 1]], axis=1), 0))
    sums = sums.reshape(count, 2, slots, 2 * width)
    turn_re, turn_im = turns[:, 0], turns[:, 1]
    for parity in range(2):
        lanes = slice(parity * width, (parity + 1) * width)
        ph_re, ph_im = phases[:, 2 * parity], phases[:, 2 * parity + 1]
        re, im = sums[:, 0, :, lanes], sums[:, 1, :, lanes]
        w_re = turn_re * ph_re - turn_im * ph_im
        w_im = turn_re * ph_im + turn_im * ph_re
        out[:, parity, 0] = re * w_re - im * w_im
        out[:, parity, 1] = re * w_im + im * w_re


def digits_swapped(tiles):
    lane = lax.broadcasted_iota(jnp.int32, tiles[0].shape, 1)
    step = 1
    while step < len(tiles):
        low_half = jnp.bitwise_and(lane, step) == 0
        swapped = list(tiles)
        for k in range(len(tiles)):
            if k & step == 0:
                first, second = tiles[k], tiles[k + step]
                swapped[k] = jnp.where(low_half, first, pltpu.roll(second, step, 1))
                swapped[k + step] = jnp.where(low_half, pltpu.roll(first, LANES - step, 1), second)
        tiles = swapped
        step *= 2
    return tiles


def chirp_kernel(place, angles, small, tables, out, sides, grid, held):
    twist, mirror, extra_turn = (small.at[n] for n in range(3))
    points = small.shape[3]
    blocks = angles.shape[1] // SUB
    for block in range(blocks):
        for side in range(2):
            rows = pl.ds(block * SUB, SUB)
            tiles = [angles[side, rows, pl.ds(k * LANES, LANES)] for k in range(points)]
            for k, value in enumerate(digits_swapped(tiles)):
                cos, sin = turned_by(value)
                sides[block, side, pl.ds(k * SUB, SUB), pl.ds(0, LANES)] = cos
                sides[block, side, pl.ds(k * SUB, SUB), pl.ds(LANES, LANES)] = sin

    @pl.when(place[0] == 0)
    def _():
        slot = lax.broadcasted_iota(jnp.int32, (SUB, LANES), 0)
        lane = lax.broadcasted_iota(jnp.int32, (SUB, LANES), 1)
        alive = jnp.logical_or(slot > 0, lane > 0)
        for part in range(2):
            lanes = pl.ds(part * LANES, LANES)
            sides[0, 0, pl.ds(0, SUB), lanes] = jnp.where(alive, sides[0, 0, pl.ds(0, SUB), lanes], 0.0)

    for block in range(blocks):
        rows = pl.ds(block * SUB, SUB)
        for parity in range(2):
            for side in range(2):

                def put(j, re, im, block=block, rows=rows, parity=parity, side=side):
                    held[block, parity, side, 0, j] = re
                    held[block, parity, side, 1, j] = im
                    if side == 1:
                        sign = 1.0 - 2.0 * parity
                        m_re, m_im = mirror[parity, 0, pl.ds(j, 1)], mirror[parity, 1, pl.ds(j, 1)]
                        out[j, parity, 0, rows] = held[block, parity, 0, 0, j] + sign * (re * m_re + im * m_im)
                        out[j, parity, 1, rows] = held[block, parity, 0, 1, j] + sign * (re * m_im - im * m_re)

                backward(sides[block, side], parity, twist, tables[parity], grid.at[block, side], put)

    @pl.when(place[0] == 0)
    def _():
        keep = lax.broadcasted_iota(jnp.int32, (SUB, LANES), 0) > 0
        rows = pl.ds(0, SUB)
        for parity in range(2):
            for j in range(points):
                w_re, w_im = extra_turn[parity, 0, pl.ds(j, 1)], extra_turn[parity, 1, pl.ds(j, 1)]
                near = 2.0 * held[0, parity, 0, 0, j]
                far = 2.0 * (held[0, parity, 1, 0, j] * w_re + held[0, parity, 1, 1, j] * w_im)
                out[j, parity, 0, rows] = jnp.where(keep, out[j, parity, 0, rows], near)
                out[j, parity, 1, rows] = jnp.where(keep, out[j, parity, 1, rows], far)


def response_kernel(parts, turns_in, phases_in, back_table, table, turns, phases, out, packed):
    sources, slots = parts.shape[0], parts.shape[3]
    count, out_slots = out.shape[0], out.shape[4]
    depth = 2 * sources * slots

    @pl.when(pl.program_id(0) == 0)
    def _():
        for source in range(sources):
            t_re, t_im = turns_in[source, 0], turns_in[source, 1]
            for parity in range(2):
                ph_re, ph_im = phases_in[source, 2 * parity], phases_in[source, 2 * parity + 1]
                w_re = t_re * ph_re - t_im * ph_im
                w_im = t_re * ph_im + t_im * ph_re
                re, im = parts[source, parity, 0], parts[source, parity, 1]
                lanes = pl.ds(parity * LANES, LANES)
                pair = jnp.concatenate([re * w_re + im * w_im, im * w_re - re * w_im], axis=0)
                high, low = split(pair)
                for n, value in enumerate((high, low, high)):
                    packed[pl.ds(n * depth + 2 * source * slots, 2 * slots), lanes] = value

    taps = dot(back_table[...], packed[...])
    sums = dot(table[...], thrice(taps, 0)).reshape(count, 2, out_slots, 2 * LANES)
    turn_re, turn_im = turns[:, 0], turns[:, 1]
    for parity in range(2):
        lanes = slice(parity * LANES, (parity + 1) * LANES)
        ph_re, ph_im = phases[:, 2 * parity], phases[:, 2 * parity + 1]
        re, im = sums[:, 0, :, lanes], sums[:, 1, :, lanes]
        w_re = turn_re * ph_re - turn_im * ph_im
        w_im = turn_re * ph_im + turn_im * ph_re
        out[:, 0, parity, 0] = re * w_re - im * w_im
        out[:, 0, parity, 1] = re * w_im + im * w_re


def forward_kernel(x, twist, tables, out, grid):
    tiles = x.shape[5] // LANES
    for n in range(x.shape[0]):

        def value_at(parity, j, n=n):
            group, tile = divmod(j, tiles)
            lanes = pl.ds(tile * LANES, LANES)
            return x[n, group, parity, 0, :, lanes], x[n, group, parity, 1, :, lanes]

        upper, lower = forward(value_at, twist, tables, grid.at[n])
        out[n, 0] = upper
        out[n, 1] = lower


def apply_kernel(taps, spectrum, twist, tables, out, raw, response, past, sides, grid):
    step = pl.program_id(0)
    points = twist.shape[2]
    tiles = out.shape[5] // LANES
    re_lanes, im_lanes = pl.ds(0, LANES), pl.ds(LANES, LANES)

    @pl.when(step == 0)
    def _():
        past[...] = jnp.zeros_like(past)

    @pl.when(step < 2)
    def _():
        for n in range(2):

            def value_at(parity, j, n=n):
                return taps[j, n, parity, 0], taps[j, n, parity, 1]

            upper, lower = forward(value_at, twist, tables, grid.at[n])
            raw[2 * step + n, 0] = upper
            raw[2 * step + n, 1] = lower

    @pl.when(step == 1)
    def _():
        sign = 1.0 - 2.0 * (lax.broadcasted_iota(jnp.int32, (SUB, LANES), 0) % 2).astype(jnp.float32)
        for side in range(2):
            for k in range(points):
                rows = pl.ds(k * SUB, SUB)
                res = [raw[j, side, rows, re_lanes] for j in range(4)]
                ims = [raw[j, side, rows, im_lanes] for j in range(4)]
                for j in range(4):
                    response[j, side, rows, re_lanes] = res[j] - sign * ims[j - 1]
                    response[j, side, rows, im_lanes] = ims[j] + sign * res[j - 1]

    @pl.when(step >= 2)
    def _():
        window = [past.at[n] for n in range(3)] + [spectrum.at[n] for n in range(2)]
        for k in range(points):
            rows = pl.ds(k * SUB, SUB)
            sums = [[], []]
            for side in range(2):
                xs = [(ref[side, rows, re_lanes], ref[side, rows, im_lanes]) for ref in window]
                totals = [None, None]
                for j in range(4):
                    h_re, h_im = response[j, side, rows, re_lanes], response[j, side, rows, im_lanes]
                    for n in range(2):
                        x_re, x_im = xs[3 + n - j]
                        term = h_re * x_re - h_im * x_im, h_re * x_im + h_im * x_re
                        totals[n] = term if j == 0 else plus(totals[n], term)
                for n in range(2):
                    sums[n].append(totals[n])
            for n in range(2):
                for parity, value in enumerate((plus(*sums[n]), minus(*sums[n]))):
                    sides[n, parity, rows, re_lanes] = value[0]
                    sides[n, parity, rows, im_lanes] = value[1]
        for n in range(2):
            for parity in range(2):

                def put(j, re, im, n=n, parity=parity):
                    group, tile = divmod(j, tiles)
                    lanes = pl.ds(tile * LANES, LANES)
                    out[n, group, parity, 0, :, lanes] = re
                    out[n, group, parity, 1, :, lanes] = im

                backward(sides[n, parity], parity, twist, tables[2 + parity], grid.at[n], put)
        past[0] = past[2]
        past[1] = spectrum[0]
        past[2] = spectrum[1]


def gather_kernel(parts, turns, phases, table, out):
    count, slots, width = parts.shape[0], parts.shape[3], parts.shape[4]
    turn_re, turn_im = turns[:, 0], turns[:, 1]
    columns = []
    for parity in range(2):
        ph_re, ph_im = phases[:, 2 * parity], phases[:, 2 * parity + 1]
        w_re = turn_re * ph_re - turn_im * ph_im
        w_im = turn_re * ph_im + turn_im * ph_re
        re, im = parts[:, parity, 0], parts[:, parity, 1]
        pair = jnp.stack([re * w_re + im * w_im, im * w_re - re * w_im], axis=1)
        columns.append(pair.reshape(count * 2 * slots, width))
    sums = dot(table[...], thrice(jnp.concatenate(columns, axis=1), 0))
    for parity in range(2):
        out[0, parity] = sums[:, parity * width : (parity + 1) * width]


def whole(shape):
    return pl.BlockSpec(shape, lambda i, *_: (0,) * len(shape))


def call(kernel, name, grid, in_specs, out_specs, out_shape, scratch, flops, size, scalars=0):
    return pl.pallas_call(
        kernel,
        grid_spec=pltpu.PrefetchScalarGridSpec(
            num_scalar_prefetch=scalars,
            grid=(grid,),
            in_specs=in_specs,
            out_specs=out_specs,
            scratch_shapes=scratch,
        ),
        out_shape=jax.ShapeDtypeStruct(out_shape, jnp.float32),
        compiler_params=pltpu.CompilerParams(vmem_limit_bytes=VMEM, dimension_semantics=("arbitrary",)),
        cost_estimate=pl.CostEstimate(flops=int(flops), bytes_accessed=int(size), transcendentals=0),
        name=name,
    )


def exchange(values):
    return lax.all_to_all(values, ("seg", "fft"), split_axis=0, concat_axis=0, tiled=True)


def phase_pair(odd_rows, column, period):
    even = np.stack(turn(odd_rows * column, period), axis=-1)
    odd = np.stack(turn(odd_rows * (2 * column + 1), 2 * period), axis=-1)
    return np.concatenate([even, odd], axis=-1)


def per_device(voltage, chirp_phase):
    groups, segments = lax.axis_size("fft"), lax.axis_size("seg")
    group, segment = lax.axis_index("fft"), lax.axis_index("seg")
    count = groups * segments
    position = segment * groups + group
    quarter, width = voltage.shape[2], voltage.shape[3]
    row_count, half = 4 * quarter, 2 * quarter
    columns = width * groups
    points = columns // LANES
    total = row_count * columns
    short = total // 2
    slots = half // groups
    tile, wide = min(2 * LANES, width // 4), width // 2
    f32 = jnp.float32

    keys, lanes = np.arange(points), np.arange(LANES)
    twist = np.stack(
        [
            np.stack(turn(keys[:, None] * lanes[None, :], columns)),
            np.stack(turn(keys[:, None] * (2 * lanes[None, :] + 1), 2 * columns)),
        ]
    ).astype(np.float32)
    tables = []
    for cos, sin in (
        turn(lanes[:, None] * lanes[None, :], LANES),
        turn((2 * lanes[:, None] + 1) * lanes[None, :], 2 * LANES),
    ):
        tables.append(np.block([[cos, sin], [-sin, cos]]))
    column_tables = [twist, right_table(np.stack(tables + [table.T for table in tables]))]
    digit_order = (LANES // points * (lanes % points) + lanes // points).astype(np.int64)
    digit_order = np.concatenate([digit_order, LANES + digit_order])
    swapped_tables = right_table(np.stack([table.T[digit_order] for table in tables]))
    column_specs = [whole(table.shape) for table in column_tables]

    own_rows = max(SUB, quarter // count)
    odd_rows = 2 * np.arange(own_rows * count) + 1
    live = (odd_rows < 2 * quarter).astype(np.float64)
    cos, sin = turn(odd_rows[:, None] * np.arange(quarter)[None, :], 2 * half)
    row_table = np.stack([cos, sin], axis=1) * live[:, None, None]
    row_table = row_table.reshape(count, own_rows, 2, quarter).transpose(0, 2, 1, 3).reshape(-1, quarter)
    back_table = left_table(row_table.T / short)
    row_table = left_table(row_table)
    turns = np.stack(turn(odd_rows[:, None] * np.arange(width)[None, :], 2 * short))
    turns = turns.reshape(2, count, own_rows, width).transpose(1, 0, 2, 3).astype(np.float32)

    def row_phases(column_starts):
        table = phase_pair(odd_rows[None, :], column_starts[:, None], 2 * short)
        table = table.reshape(-1, count, own_rows, 4).transpose(0, 1, 3, 2)
        return jnp.asarray(table[..., None].astype(np.float32))

    phases = lax.dynamic_index_in_dim(row_phases(np.arange(groups) * width), group, 0, keepdims=False)

    chirp_slots = max(SUB, slots // segments)
    holders = slots // chirp_slots
    blocks = chirp_slots // SUB
    start = jnp.minimum(segment, holders - 1)
    place = jnp.stack([position, start]).astype(jnp.int32)
    every = LANES * keys[:, None] + lanes[None, :]
    extra_turn = np.stack(
        [np.stack(turn(half * every, total)), np.stack(turn(half * (2 * every + 1), 2 * total))]
    ).astype(np.float32)
    mirror = np.stack(
        [np.stack(turn(every, columns)), np.stack(turn((1 - columns) * (2 * every + 1), 2 * columns))]
    ).astype(np.float32)
    small = np.stack([twist, mirror, extra_turn])
    cells = (points * SUB, 2 * LANES)
    chirp_columns = call(
        chirp_kernel,
        "chirp_columns",
        1,
        [
            pl.BlockSpec((2, chirp_slots, columns), lambda i, place: (0, place[1], 0)),
            whole(small.shape),
            whole(swapped_tables.shape),
        ],
        whole((points, 2, 2, chirp_slots, LANES)),
        (points, 2, 2, chirp_slots, LANES),
        [
            pltpu.VMEM((blocks, 2) + cells, f32),
            pltpu.VMEM((blocks, 2, 2) + cells, f32),
            pltpu.VMEM((blocks, 2, 2, 2, points, SUB, LANES), f32),
        ],
        4e8 * blocks,
        3e6,
        scalars=1,
    )(place, chirp_phase, small, swapped_tables)
    if holders < segments:
        chirp_columns = jnp.where(segment < holders, chirp_columns, 0.0)
    if count > points:
        chirp_columns = jnp.pad(chirp_columns, ((0, count - points),) + ((0, 0),) * 4)
    chirp_parts = exchange(chirp_columns)[: holders * groups]

    rows = np.arange(half)
    order = rows.reshape(groups, holders, chirp_slots).transpose(1, 0, 2)
    chirp_turns = np.stack(turn(order[..., None] * lanes, total), axis=2).astype(np.float32)
    block_of = np.arange(points)
    chirp_phases = phase_pair(order[None], LANES * block_of[:, None, None, None], total)
    chirp_phases = chirp_phases.reshape(points, holders * groups, chirp_slots, 4).transpose(0, 1, 3, 2)
    chirp_phases = jnp.asarray(chirp_phases[..., None].astype(np.float32))
    chirp_turns = chirp_turns.reshape(holders * groups, 2, chirp_slots, LANES)
    cos, sin = turn(rows[None, :] * np.arange(row_count)[:, None], row_count)
    cos[:, 0] = 0.5
    sin[:, 0] = np.where(np.arange(row_count) % 2 == 0, 0.5, -0.5)
    taps_table = np.stack([cos, sin], axis=1).reshape(row_count, 2, groups, holders, chirp_slots) / total
    taps_table = taps_table.transpose(0, 3, 2, 1, 4).reshape(row_count, 2 * half)
    taps_table = left_table(taps_table)
    own_block = jnp.minimum(position, points - 1)
    own_chirp_phases = lax.dynamic_index_in_dim(chirp_phases, own_block, 0, keepdims=False)
    own_row_phases = lax.dynamic_index_in_dim(row_phases(block_of * LANES), own_block, 0, keepdims=False)
    response_shape = (count, 4, 2, 2, own_rows, LANES)
    response = call(
        response_kernel,
        "response",
        4,
        [
            whole(chirp_parts.shape),
            whole(chirp_turns.shape),
            whole(own_chirp_phases.shape),
            pl.BlockSpec((quarter, taps_table.shape[1]), lambda i: (i, 0)),
            whole(row_table.shape),
            pl.BlockSpec((count, 2, own_rows, LANES), lambda i: (0, 0, 0, 0)),
            whole(own_row_phases.shape),
        ],
        pl.BlockSpec((count, 1, 2, 2, own_rows, LANES), lambda i: (0, i, 0, 0, 0, 0)),
        response_shape,
        [pltpu.VMEM((6 * half, 2 * LANES), jnp.bfloat16)],
        5e9,
        1e7,
    )(chirp_parts, chirp_turns, own_chirp_phases, taps_table, row_table, turns, own_row_phases)
    taps = exchange(response)[:points]

    spread_shape = (count, 2, 2, own_rows, width)
    spread = call(
        spread_kernel,
        "spread",
        width // tile,
        [
            pl.BlockSpec((1, 2, quarter, tile), lambda c: (0, 0, 0, c)),
            whole(row_table.shape),
            pl.BlockSpec((count, 2, own_rows, tile), lambda c: (0, 0, 0, c)),
            whole(phases.shape),
        ],
        pl.BlockSpec((count, 2, 2, own_rows, tile), lambda c: (0, 0, 0, 0, c)),
        spread_shape,
        [],
        2e9,
        1e7,
    )(voltage, row_table, turns, phases)
    spread = exchange(spread).reshape(segments, groups, 2, 2, own_rows, width)

    pair_scratch = pltpu.VMEM((2, 2) + cells, f32)
    spectrum = call(
        forward_kernel,
        "forward",
        segments // 2,
        [pl.BlockSpec((2, groups, 2, 2, own_rows, width), lambda s: (s, 0, 0, 0, 0, 0))] + column_specs,
        pl.BlockSpec((2, 2) + cells, lambda s: (s, 0, 0, 0)),
        (segments, 2) + cells,
        [pair_scratch],
        2e9,
        1e7,
    )(spread, *column_tables)

    def lagged(i):
        return jnp.maximum(i - 2, 0)

    packed = call(
        apply_kernel,
        "apply",
        segments // 2 + 2,
        [
            pl.BlockSpec((points, 2, 2, 2, own_rows, LANES), lambda i: (0, jnp.minimum(i, 1), 0, 0, 0, 0)),
            pl.BlockSpec((2, 2) + cells, lambda i: (lagged(i), 0, 0, 0)),
        ]
        + column_specs,
        pl.BlockSpec((2, groups, 2, 2, own_rows, width), lambda i: (lagged(i), 0, 0, 0, 0, 0)),
        (segments, groups, 2, 2, own_rows, width),
        [
            pltpu.VMEM((4, 2) + cells, f32),
            pltpu.VMEM((4, 2) + cells, f32),
            pltpu.VMEM((3, 2) + cells, f32),
            pair_scratch,
            pair_scratch,
        ],
        4e9,
        2e7,
    )(taps, spectrum, *column_tables)
    parts = exchange(packed.reshape(spread_shape))

    return call(
        gather_kernel,
        "gather",
        width // wide,
        [
            pl.BlockSpec((count, 2, 2, own_rows, wide), lambda c: (0, 0, 0, 0, c)),
            pl.BlockSpec((count, 2, own_rows, wide), lambda c: (0, 0, 0, c)),
            whole(phases.shape),
            whole(back_table.shape),
        ],
        pl.BlockSpec((1, 2, quarter, wide), lambda c: (0, 0, 0, c)),
        (1, 2, quarter, width),
        [],
        2e9,
        1e7,
    )(parts, turns, phases, back_table)


def solution(mesh):
    in_specs = (P("seg", None, None, "fft"), P(None, "fft", None))
    out_specs = P("seg", None, None, "fft")
    return jax.shard_map(per_device, mesh=mesh, in_specs=in_specs, out_specs=out_specs, check_vma=False)
```

```python
import math

import jax
import jax.numpy as jnp
import ml_dtypes
import numpy as np
from jax import lax
from jax.experimental import pallas as pl
from jax.experimental.pallas import tpu as pltpu
from jax.sharding import PartitionSpec as P

LANES = 128
SUB = 8
VMEM = 50 * 1024 * 1024


def turn(products, period):
    angles = np.mod(products, period).astype(np.float64) * (-2.0 * math.pi / period)
    return np.cos(angles), np.sin(angles)


def halves(table):
    high = table.astype(ml_dtypes.bfloat16)
    low = (table - high.astype(np.float64)).astype(ml_dtypes.bfloat16)
    return high, low


def split(values):
    high = values.astype(jnp.bfloat16)
    low = (values - high.astype(jnp.float32)).astype(jnp.bfloat16)
    return high, low


def thrice(values, axis):
    high, low = split(values)
    return jnp.concatenate([high, low, high] if axis == 0 else [high, high, low], axis=axis)


def right_table(table):
    high, low = halves(table)
    return np.concatenate([high, low, high], axis=-2)


def left_table(table):
    high, low = halves(table)
    return np.concatenate([high, high, low], axis=-1)


def dot(left, right):
    return jnp.dot(left, right, preferred_element_type=jnp.float32)


def scale_by(value, cos, sin):
    re, im = value
    near = 1e-12
    if abs(sin) < near:
        return value if cos > 0 else (-re, -im)
    if abs(cos) < near:
        return (-im, re) if sin > 0 else (im, -re)
    if abs(abs(cos) - abs(sin)) < near:
        size = abs(cos)
        first = re if cos > 0 else -re
        second = im if cos > 0 else -im
        third = im if sin > 0 else -im
        fourth = re if sin > 0 else -re
        return (first - third) * size, (second + fourth) * size
    return re * cos - im * sin, re * sin + im * cos


def plus(left, right):
    return left[0] + right[0], left[1] + right[1]


def minus(left, right):
    return left[0] - right[0], left[1] - right[1]


def small_dft(values, sign):
    count = len(values)
    if count == 1:
        return values
    if count == 2:
        return [plus(values[0], values[1]), minus(values[0], values[1])]
    if count == 4:
        even_sum, even_gap = plus(values[0], values[2]), minus(values[0], values[2])
        odd_sum, odd_gap = plus(values[1], values[3]), minus(values[1], values[3])
        turned = scale_by(odd_gap, 0.0, float(sign))
        return [plus(even_sum, odd_sum), plus(even_gap, turned), minus(even_sum, odd_sum), minus(even_gap, turned)]
    radix = 4 if count == 32 else 2
    part = count // radix
    pieces = [small_dft(values[i::radix], sign) for i in range(radix)]
    result = [None] * count
    for k in range(part):
        column = []
        for i in range(radix):
            angle = sign * 2.0 * math.pi * i * k / count
            column.append(scale_by(pieces[i][k], math.cos(angle), math.sin(angle)))
        for q, value in enumerate(small_dft(column, sign)):
            result[k + part * q] = value
    return result


def forward(value_ats, twist, tables, grid):
    points = twist.shape[2]
    spectra = []
    for parity in range(2):
        for n, value_at in enumerate(value_ats):
            values = [value_at(parity, j) for j in range(points)]
            for k, (re, im) in enumerate(small_dft(values, -1)):
                w_re, w_im = twist[parity, 0, pl.ds(k, 1)], twist[parity, 1, pl.ds(k, 1)]
                rows = pl.ds((n * points + k) * SUB, SUB)
                grid[parity, rows, pl.ds(0, LANES)] = re * w_re - im * w_im
                grid[parity, rows, pl.ds(LANES, LANES)] = re * w_im + im * w_re
        spectra.append(dot(thrice(grid[parity], 1), tables[parity]))
    even, odd = spectra
    return even + odd, even - odd


def backward(side, parity, twist, table, grid, puts):
    points = twist.shape[2]
    grid[parity] = dot(thrice(side, 1), table)
    for n, put in enumerate(puts):
        values = []
        for k in range(points):
            rows = pl.ds((n * points + k) * SUB, SUB)
            re, im = grid[parity, rows, pl.ds(0, LANES)], grid[parity, rows, pl.ds(LANES, LANES)]
            w_re, w_im = twist[parity, 0, pl.ds(k, 1)], twist[parity, 1, pl.ds(k, 1)]
            values.append((re * w_re + im * w_im, im * w_re - re * w_im))
        for j, (re, im) in enumerate(small_dft(values, 1)):
            put(j, re, im)


def turned_by(angles):
    half = angles * 0.5
    square = half * half
    sin, cos = 0.0, 0.0
    for n in range(6, -1, -1):
        sin = sin * square + (-1.0) ** n / math.factorial(2 * n + 1)
        cos = cos * square + (-1.0) ** n / math.factorial(2 * n)
    sin = sin * half
    return 1.0 - 2.0 * sin * sin, 2.0 * sin * cos


def spread_kernel(x, table, turns, phases, out):
    count, slots, width = out.shape[0], out.shape[3], out.shape[4]
    sums = dot(table[...], thrice(jnp.concatenate([x[0, 0], x[0, 1]], axis=1), 0))
    sums = sums.reshape(count, 2, slots, 2 * width)
    turn_re, turn_im = turns[:, 0], turns[:, 1]
    for parity in range(2):
        lanes = slice(parity * width, (parity + 1) * width)
        ph_re, ph_im = phases[:, 2 * parity], phases[:, 2 * parity + 1]
        re, im = sums[:, 0, :, lanes], sums[:, 1, :, lanes]
        w_re = turn_re * ph_re - turn_im * ph_im
        w_im = turn_re * ph_im + turn_im * ph_re
        out[:, parity, 0] = re * w_re - im * w_im
        out[:, parity, 1] = re * w_im + im * w_re


def digits_swapped(tiles):
    lane = lax.broadcasted_iota(jnp.int32, tiles[0].shape, 1)
    step = 1
    while step < len(tiles):
        low_half = jnp.bitwise_and(lane, step) == 0
        swapped = list(tiles)
        for k in range(len(tiles)):
            if k & step == 0:
                first, second = tiles[k], tiles[k + step]
                swapped[k] = jnp.where(low_half, first, pltpu.roll(second, step, 1))
                swapped[k + step] = jnp.where(low_half, pltpu.roll(first, LANES - step, 1), second)
        tiles = swapped
        step *= 2
    return tiles


def chirp_kernel(place, angles, small, tables, out, sides, grid, held):
    twist, mirror, extra_turn = (small.at[n] for n in range(3))
    points = small.shape[3]
    blocks = angles.shape[1] // SUB
    for block in range(blocks):
        for side in range(2):
            rows = pl.ds(block * SUB, SUB)
            tiles = [angles[side, rows, pl.ds(k * LANES, LANES)] for k in range(points)]
            for k, value in enumerate(digits_swapped(tiles)):
                cos, sin = turned_by(value)
                cell = pl.ds(((2 * block + side) * points + k) * SUB, SUB)
                sides[cell, pl.ds(0, LANES)] = cos
                sides[cell, pl.ds(LANES, LANES)] = sin

    @pl.when(place[0] == 0)
    def _():
        slot = lax.broadcasted_iota(jnp.int32, (SUB, LANES), 0)
        lane = lax.broadcasted_iota(jnp.int32, (SUB, LANES), 1)
        alive = jnp.logical_or(slot > 0, lane > 0)
        for part in range(2):
            lanes = pl.ds(part * LANES, LANES)
            sides[pl.ds(0, SUB), lanes] = jnp.where(alive, sides[pl.ds(0, SUB), lanes], 0.0)

    for parity in range(2):
        puts = []
        for block in range(blocks):
            rows = pl.ds(block * SUB, SUB)
            for side in range(2):

                def put(j, re, im, block=block, rows=rows, parity=parity, side=side):
                    held[block, parity, side, 0, j] = re
                    held[block, parity, side, 1, j] = im
                    if side == 1:
                        sign = 1.0 - 2.0 * parity
                        m_re, m_im = mirror[parity, 0, pl.ds(j, 1)], mirror[parity, 1, pl.ds(j, 1)]
                        out[j, parity, 0, rows] = held[block, parity, 0, 0, j] + sign * (re * m_re + im * m_im)
                        out[j, parity, 1, rows] = held[block, parity, 0, 1, j] + sign * (re * m_im - im * m_re)

                puts.append(put)
        backward(sides[...], parity, twist, tables[parity], grid, puts)

    @pl.when(place[0] == 0)
    def _():
        keep = lax.broadcasted_iota(jnp.int32, (SUB, LANES), 0) > 0
        rows = pl.ds(0, SUB)
        for parity in range(2):
            for j in range(points):
                w_re, w_im = extra_turn[parity, 0, pl.ds(j, 1)], extra_turn[parity, 1, pl.ds(j, 1)]
                near = 2.0 * held[0, parity, 0, 0, j]
                far = 2.0 * (held[0, parity, 1, 0, j] * w_re + held[0, parity, 1, 1, j] * w_im)
                out[j, parity, 0, rows] = jnp.where(keep, out[j, parity, 0, rows], near)
                out[j, parity, 1, rows] = jnp.where(keep, out[j, parity, 1, rows], far)


def response_kernel(parts, turns_in, phases_in, back_table, table, turns, phases, out, packed):
    sources, slots = parts.shape[0], parts.shape[3]
    count, out_slots = out.shape[0], out.shape[4]
    depth = 2 * sources * slots

    @pl.when(pl.program_id(0) == 0)
    def _():
        for source in range(sources):
            t_re, t_im = turns_in[source, 0], turns_in[source, 1]
            for parity in range(2):
                ph_re, ph_im = phases_in[source, 2 * parity], phases_in[source, 2 * parity + 1]
                w_re = t_re * ph_re - t_im * ph_im
                w_im = t_re * ph_im + t_im * ph_re
                re, im = parts[source, parity, 0], parts[source, parity, 1]
                lanes = pl.ds(parity * LANES, LANES)
                pair = jnp.concatenate([re * w_re + im * w_im, im * w_re - re * w_im], axis=0)
                high, low = split(pair)
                for n, value in enumerate((high, low, high)):
                    packed[pl.ds(n * depth + 2 * source * slots, 2 * slots), lanes] = value

    taps = dot(back_table[...], packed[...])
    sums = dot(table[...], thrice(taps, 0)).reshape(count, 2, out_slots, 2 * LANES)
    turn_re, turn_im = turns[:, 0], turns[:, 1]
    for parity in range(2):
        lanes = slice(parity * LANES, (parity + 1) * LANES)
        ph_re, ph_im = phases[:, 2 * parity], phases[:, 2 * parity + 1]
        re, im = sums[:, 0, :, lanes], sums[:, 1, :, lanes]
        w_re = turn_re * ph_re - turn_im * ph_im
        w_im = turn_re * ph_im + turn_im * ph_re
        out[:, 0, parity, 0] = re * w_re - im * w_im
        out[:, 0, parity, 1] = re * w_im + im * w_re


def forward_kernel(x, twist, tables, out, grid):
    tiles = x.shape[5] // LANES
    size = out.shape[2]
    value_ats = []
    for n in range(x.shape[0]):

        def value_at(parity, j, n=n):
            group, tile = divmod(j, tiles)
            lanes = pl.ds(tile * LANES, LANES)
            return x[n, group, parity, 0, :, lanes], x[n, group, parity, 1, :, lanes]

        value_ats.append(value_at)
    upper, lower = forward(value_ats, twist, tables, grid)
    for n in range(x.shape[0]):
        out[n, 0] = upper[n * size : (n + 1) * size]
        out[n, 1] = lower[n * size : (n + 1) * size]


def apply_kernel(taps, spectrum, twist, tables, out, raw, response, past, sides, grid):
    step = pl.program_id(0)
    points = twist.shape[2]
    tiles = out.shape[5] // LANES
    size = points * SUB
    re_lanes, im_lanes = pl.ds(0, LANES), pl.ds(LANES, LANES)

    @pl.when(step == 0)
    def _():
        past[...] = jnp.zeros_like(past)

    @pl.when(step < 2)
    def _():
        value_ats = []
        for n in range(2):

            def value_at(parity, j, n=n):
                return taps[j, n, parity, 0], taps[j, n, parity, 1]

            value_ats.append(value_at)
        upper, lower = forward(value_ats, twist, tables, grid)
        for n in range(2):
            raw[2 * step + n, 0] = upper[n * size : (n + 1) * size]
            raw[2 * step + n, 1] = lower[n * size : (n + 1) * size]

    @pl.when(step == 1)
    def _():
        sign = 1.0 - 2.0 * (lax.broadcasted_iota(jnp.int32, (SUB, LANES), 0) % 2).astype(jnp.float32)
        for side in range(2):
            for k in range(points):
                rows = pl.ds(k * SUB, SUB)
                res = [raw[j, side, rows, re_lanes] for j in range(4)]
                ims = [raw[j, side, rows, im_lanes] for j in range(4)]
                for j in range(4):
                    response[j, side, rows, re_lanes] = res[j] - sign * ims[j - 1]
                    response[j, side, rows, im_lanes] = ims[j] + sign * res[j - 1]

    @pl.when(step >= 2)
    def _():
        window = [past.at[n] for n in range(3)] + [spectrum.at[n] for n in range(2)]
        for k in range(points):
            rows = pl.ds(k * SUB, SUB)
            sums = [[], []]
            for side in range(2):
                xs = [(ref[side, rows, re_lanes], ref[side, rows, im_lanes]) for ref in window]
                totals = [None, None]
                for j in range(4):
                    h_re, h_im = response[j, side, rows, re_lanes], response[j, side, rows, im_lanes]
                    for n in range(2):
                        x_re, x_im = xs[3 + n - j]
                        term = h_re * x_re - h_im * x_im, h_re * x_im + h_im * x_re
                        totals[n] = term if j == 0 else plus(totals[n], term)
                for n in range(2):
                    sums[n].append(totals[n])
            for n in range(2):
                for parity, value in enumerate((plus(*sums[n]), minus(*sums[n]))):
                    cell = pl.ds(n * size + k * SUB, SUB)
                    sides[parity, cell, re_lanes] = value[0]
                    sides[parity, cell, im_lanes] = value[1]
        for parity in range(2):
            puts = []
            for n in range(2):

                def put(j, re, im, n=n, parity=parity):
                    group, tile = divmod(j, tiles)
                    lanes = pl.ds(tile * LANES, LANES)
                    out[n, group, parity, 0, :, lanes] = re
                    out[n, group, parity, 1, :, lanes] = im

                puts.append(put)
            backward(sides[parity], parity, twist, tables[2 + parity], grid, puts)
        past[0] = past[2]
        past[1] = spectrum[0]
        past[2] = spectrum[1]


def gather_kernel(parts, turns, phases, table, out):
    count, slots, width = parts.shape[0], parts.shape[3], parts.shape[4]
    turn_re, turn_im = turns[:, 0], turns[:, 1]
    columns = []
    for parity in range(2):
        ph_re, ph_im = phases[:, 2 * parity], phases[:, 2 * parity + 1]
        w_re = turn_re * ph_re - turn_im * ph_im
        w_im = turn_re * ph_im + turn_im * ph_re
        re, im = parts[:, parity, 0], parts[:, parity, 1]
        pair = jnp.stack([re * w_re + im * w_im, im * w_re - re * w_im], axis=1)
        columns.append(pair.reshape(count * 2 * slots, width))
    sums = dot(table[...], thrice(jnp.concatenate(columns, axis=1), 0))
    for parity in range(2):
        out[0, parity] = sums[:, parity * width : (parity + 1) * width]


def whole(shape):
    return pl.BlockSpec(shape, lambda i, *_: (0,) * len(shape))


def call(kernel, name, grid, in_specs, out_specs, out_shape, scratch, flops, size, scalars=0):
    return pl.pallas_call(
        kernel,
        grid_spec=pltpu.PrefetchScalarGridSpec(
            num_scalar_prefetch=scalars,
            grid=(grid,),
            in_specs=in_specs,
            out_specs=out_specs,
            scratch_shapes=scratch,
        ),
        out_shape=jax.ShapeDtypeStruct(out_shape, jnp.float32),
        compiler_params=pltpu.CompilerParams(vmem_limit_bytes=VMEM, dimension_semantics=("arbitrary",)),
        cost_estimate=pl.CostEstimate(flops=int(flops), bytes_accessed=int(size), transcendentals=0),
        name=name,
    )


def exchange(values):
    return lax.all_to_all(values, ("seg", "fft"), split_axis=0, concat_axis=0, tiled=True)


def phase_pair(odd_rows, column, period):
    even = np.stack(turn(odd_rows * column, period), axis=-1)
    odd = np.stack(turn(odd_rows * (2 * column + 1), 2 * period), axis=-1)
    return np.concatenate([even, odd], axis=-1)


def per_device(voltage, chirp_phase):
    groups, segments = lax.axis_size("fft"), lax.axis_size("seg")
    group, segment = lax.axis_index("fft"), lax.axis_index("seg")
    count = groups * segments
    position = segment * groups + group
    quarter, width = voltage.shape[2], voltage.shape[3]
    row_count, half = 4 * quarter, 2 * quarter
    columns = width * groups
    points = columns // LANES
    total = row_count * columns
    short = total // 2
    slots = half // groups
    tile, wide = min(2 * LANES, width // 4), width // 2
    f32 = jnp.float32

    keys, lanes = np.arange(points), np.arange(LANES)
    twist = np.stack(
        [
            np.stack(turn(keys[:, None] * lanes[None, :], columns)),
            np.stack(turn(keys[:, None] * (2 * lanes[None, :] + 1), 2 * columns)),
        ]
    ).astype(np.float32)
    tables = []
    for cos, sin in (
        turn(lanes[:, None] * lanes[None, :], LANES),
        turn((2 * lanes[:, None] + 1) * lanes[None, :], 2 * LANES),
    ):
        tables.append(np.block([[cos, sin], [-sin, cos]]))
    column_tables = [twist, right_table(np.stack(tables + [table.T for table in tables]))]
    digit_order = (LANES // points * (lanes % points) + lanes // points).astype(np.int64)
    digit_order = np.concatenate([digit_order, LANES + digit_order])
    swapped_tables = right_table(np.stack([table.T[digit_order] for table in tables]))
    column_specs = [whole(table.shape) for table in column_tables]

    own_rows = max(SUB, quarter // count)
    odd_rows = 2 * np.arange(own_rows * count) + 1
    live = (odd_rows < 2 * quarter).astype(np.float64)
    cos, sin = turn(odd_rows[:, None] * np.arange(quarter)[None, :], 2 * half)
    row_table = np.stack([cos, sin], axis=1) * live[:, None, None]
    row_table = row_table.reshape(count, own_rows, 2, quarter).transpose(0, 2, 1, 3).reshape(-1, quarter)
    back_table = left_table(row_table.T / short)
    row_table = left_table(row_table)
    turns = np.stack(turn(odd_rows[:, None] * np.arange(width)[None, :], 2 * short))
    turns = turns.reshape(2, count, own_rows, width).transpose(1, 0, 2, 3).astype(np.float32)

    def row_phases(column_starts):
        table = phase_pair(odd_rows[None, :], column_starts[:, None], 2 * short)
        table = table.reshape(-1, count, own_rows, 4).transpose(0, 1, 3, 2)
        return jnp.asarray(table[..., None].astype(np.float32))

    phases = lax.dynamic_index_in_dim(row_phases(np.arange(groups) * width), group, 0, keepdims=False)

    chirp_slots = max(SUB, slots // segments)
    holders = slots // chirp_slots
    blocks = chirp_slots // SUB
    start = jnp.minimum(segment, holders - 1)
    place = jnp.stack([position, start]).astype(jnp.int32)
    every = LANES * keys[:, None] + lanes[None, :]
    extra_turn = np.stack(
        [np.stack(turn(half * every, total)), np.stack(turn(half * (2 * every + 1), 2 * total))]
    ).astype(np.float32)
    mirror = np.stack(
        [np.stack(turn(every, columns)), np.stack(turn((1 - columns) * (2 * every + 1), 2 * columns))]
    ).astype(np.float32)
    small = np.stack([twist, mirror, extra_turn])
    cells = (points * SUB, 2 * LANES)
    chirp_columns = call(
        chirp_kernel,
        "chirp_columns",
        1,
        [
            pl.BlockSpec((2, chirp_slots, columns), lambda i, place: (0, place[1], 0)),
            whole(small.shape),
            whole(swapped_tables.shape),
        ],
        whole((points, 2, 2, chirp_slots, LANES)),
        (points, 2, 2, chirp_slots, LANES),
        [
            pltpu.VMEM((2 * blocks * points * SUB, 2 * LANES), f32),
            pltpu.VMEM((2, 2 * blocks * points * SUB, 2 * LANES), f32),
            pltpu.VMEM((blocks, 2, 2, 2, points, SUB, LANES), f32),
        ],
        4e8 * blocks,
        3e6,
        scalars=1,
    )(place, chirp_phase, small, swapped_tables)
    if holders < segments:
        chirp_columns = jnp.where(segment < holders, chirp_columns, 0.0)
    if count > points:
        chirp_columns = jnp.pad(chirp_columns, ((0, count - points),) + ((0, 0),) * 4)
    chirp_parts = exchange(chirp_columns)[: holders * groups]

    rows = np.arange(half)
    order = rows.reshape(groups, holders, chirp_slots).transpose(1, 0, 2)
    chirp_turns = np.stack(turn(order[..., None] * lanes, total), axis=2).astype(np.float32)
    block_of = np.arange(points)
    chirp_phases = phase_pair(order[None], LANES * block_of[:, None, None, None], total)
    chirp_phases = chirp_phases.reshape(points, holders * groups, chirp_slots, 4).transpose(0, 1, 3, 2)
    chirp_phases = jnp.asarray(chirp_phases[..., None].astype(np.float32))
    chirp_turns = chirp_turns.reshape(holders * groups, 2, chirp_slots, LANES)
    cos, sin = turn(rows[None, :] * np.arange(row_count)[:, None], row_count)
    cos[:, 0] = 0.5
    sin[:, 0] = np.where(np.arange(row_count) % 2 == 0, 0.5, -0.5)
    taps_table = np.stack([cos, sin], axis=1).reshape(row_count, 2, groups, holders, chirp_slots) / total
    taps_table = taps_table.transpose(0, 3, 2, 1, 4).reshape(row_count, 2 * half)
    taps_table = left_table(taps_table)
    own_block = jnp.minimum(position, points - 1)
    own_chirp_phases = lax.dynamic_index_in_dim(chirp_phases, own_block, 0, keepdims=False)
    own_row_phases = lax.dynamic_index_in_dim(row_phases(block_of * LANES), own_block, 0, keepdims=False)
    response_shape = (count, 4, 2, 2, own_rows, LANES)
    response = call(
        response_kernel,
        "response",
        4,
        [
            whole(chirp_parts.shape),
            whole(chirp_turns.shape),
            whole(own_chirp_phases.shape),
            pl.BlockSpec((quarter, taps_table.shape[1]), lambda i: (i, 0)),
            whole(row_table.shape),
            pl.BlockSpec((count, 2, own_rows, LANES), lambda i: (0, 0, 0, 0)),
            whole(own_row_phases.shape),
        ],
        pl.BlockSpec((count, 1, 2, 2, own_rows, LANES), lambda i: (0, i, 0, 0, 0, 0)),
        response_shape,
        [pltpu.VMEM((6 * half, 2 * LANES), jnp.bfloat16)],
        5e9,
        1e7,
    )(chirp_parts, chirp_turns, own_chirp_phases, taps_table, row_table, turns, own_row_phases)
    taps = exchange(response)[:points]

    spread_shape = (count, 2, 2, own_rows, width)
    spread = call(
        spread_kernel,
        "spread",
        width // tile,
        [
            pl.BlockSpec((1, 2, quarter, tile), lambda c: (0, 0, 0, c)),
            whole(row_table.shape),
            pl.BlockSpec((count, 2, own_rows, tile), lambda c: (0, 0, 0, c)),
            whole(phases.shape),
        ],
        pl.BlockSpec((count, 2, 2, own_rows, tile), lambda c: (0, 0, 0, 0, c)),
        spread_shape,
        [],
        2e9,
        1e7,
    )(voltage, row_table, turns, phases)
    spread = exchange(spread).reshape(segments, groups, 2, 2, own_rows, width)

    pair_scratch = pltpu.VMEM((2, 2 * points * SUB, 2 * LANES), f32)
    spectrum = call(
        forward_kernel,
        "forward",
        segments // 2,
        [pl.BlockSpec((2, groups, 2, 2, own_rows, width), lambda s: (s, 0, 0, 0, 0, 0))] + column_specs,
        pl.BlockSpec((2, 2) + cells, lambda s: (s, 0, 0, 0)),
        (segments, 2) + cells,
        [pair_scratch],
        2e9,
        1e7,
    )(spread, *column_tables)

    def lagged(i):
        return jnp.maximum(i - 2, 0)

    packed = call(
        apply_kernel,
        "apply",
        segments // 2 + 2,
        [
            pl.BlockSpec((points, 2, 2, 2, own_rows, LANES), lambda i: (0, jnp.minimum(i, 1), 0, 0, 0, 0)),
            pl.BlockSpec((2, 2) + cells, lambda i: (lagged(i), 0, 0, 0)),
        ]
        + column_specs,
        pl.BlockSpec((2, groups, 2, 2, own_rows, width), lambda i: (lagged(i), 0, 0, 0, 0, 0)),
        (segments, groups, 2, 2, own_rows, width),
        [
            pltpu.VMEM((4, 2) + cells, f32),
            pltpu.VMEM((4, 2) + cells, f32),
            pltpu.VMEM((3, 2) + cells, f32),
            pair_scratch,
            pair_scratch,
        ],
        4e9,
        2e7,
    )(taps, spectrum, *column_tables)
    parts = exchange(packed.reshape(spread_shape))

    return call(
        gather_kernel,
        "gather",
        width // wide,
        [
            pl.BlockSpec((count, 2, 2, own_rows, wide), lambda c: (0, 0, 0, 0, c)),
            pl.BlockSpec((count, 2, own_rows, wide), lambda c: (0, 0, 0, c)),
            whole(phases.shape),
            whole(back_table.shape),
        ],
        pl.BlockSpec((1, 2, quarter, wide), lambda c: (0, 0, 0, c)),
        (1, 2, quarter, width),
        [],
        2e9,
        1e7,
    )(parts, turns, phases, back_table)


def solution(mesh):
    in_specs = (P("seg", None, None, "fft"), P(None, "fft", None))
    out_specs = P("seg", None, None, "fft")
    return jax.shard_map(per_device, mesh=mesh, in_specs=in_specs, out_specs=out_specs, check_vma=False)
```

```python
import math

import jax
import jax.numpy as jnp
import ml_dtypes
import numpy as np
from jax import lax
from jax.experimental import pallas as pl
from jax.experimental.pallas import tpu as pltpu
from jax.sharding import PartitionSpec as P

LANES = 128
SUB = 8
VMEM = 40 * 1024 * 1024


def turn(products, period):
    angles = np.mod(products, period).astype(np.float64) * (-2.0 * math.pi / period)
    return np.cos(angles), np.sin(angles)


def halves(table):
    high = table.astype(ml_dtypes.bfloat16)
    low = (table - high.astype(np.float64)).astype(ml_dtypes.bfloat16)
    return high, low


def split(values):
    high = values.astype(jnp.bfloat16)
    low = (values - high.astype(jnp.float32)).astype(jnp.bfloat16)
    return high, low


def thrice(values, axis):
    high, low = split(values)
    return jnp.concatenate([high, low, high] if axis == 0 else [high, high, low], axis=axis)


def right_table(table):
    high, low = halves(table)
    return np.concatenate([high, low, high], axis=-2)


def left_table(table):
    high, low = halves(table)
    return np.concatenate([high, high, low], axis=-1)


def dot(left, right):
    return jnp.dot(left, right, preferred_element_type=jnp.float32)


def scale_by(value, cos, sin):
    re, im = value
    near = 1e-12
    if abs(sin) < near:
        return value if cos > 0 else (-re, -im)
    if abs(cos) < near:
        return (-im, re) if sin > 0 else (im, -re)
    if abs(abs(cos) - abs(sin)) < near:
        size = abs(cos)
        first = re if cos > 0 else -re
        second = im if cos > 0 else -im
        third = im if sin > 0 else -im
        fourth = re if sin > 0 else -re
        return (first - third) * size, (second + fourth) * size
    return re * cos - im * sin, re * sin + im * cos


def plus(left, right):
    return left[0] + right[0], left[1] + right[1]


def minus(left, right):
    return left[0] - right[0], left[1] - right[1]


def small_dft(values, sign):
    count = len(values)
    if count == 1:
        return values
    if count == 2:
        return [plus(values[0], values[1]), minus(values[0], values[1])]
    if count == 4:
        even_sum, even_gap = plus(values[0], values[2]), minus(values[0], values[2])
        odd_sum, odd_gap = plus(values[1], values[3]), minus(values[1], values[3])
        turned = scale_by(odd_gap, 0.0, float(sign))
        return [plus(even_sum, odd_sum), plus(even_gap, turned), minus(even_sum, odd_sum), minus(even_gap, turned)]
    radix = 4 if count == 32 else 2
    part = count // radix
    pieces = [small_dft(values[i::radix], sign) for i in range(radix)]
    result = [None] * count
    for k in range(part):
        column = []
        for i in range(radix):
            angle = sign * 2.0 * math.pi * i * k / count
            column.append(scale_by(pieces[i][k], math.cos(angle), math.sin(angle)))
        for q, value in enumerate(small_dft(column, sign)):
            result[k + part * q] = value
    return result


def forward(value_ats, twist, tables, grid):
    points = twist.shape[2]
    spectra = []
    for parity in range(2):
        for n, value_at in enumerate(value_ats):
            values = [value_at(parity, j) for j in range(points)]
            for k, (re, im) in enumerate(small_dft(values, -1)):
                w_re, w_im = twist[parity, 0, pl.ds(k, 1)], twist[parity, 1, pl.ds(k, 1)]
                rows = pl.ds((n * points + k) * SUB, SUB)
                grid[parity, rows, pl.ds(0, LANES)] = re * w_re - im * w_im
                grid[parity, rows, pl.ds(LANES, LANES)] = re * w_im + im * w_re
        spectra.append(dot(thrice(grid[parity], 1), tables[parity]))
    even, odd = spectra
    return even + odd, even - odd


def backward(side, parity, twist, table, grid, puts):
    points = twist.shape[2]
    grid[parity] = dot(thrice(side, 1), table)
    for n, put in enumerate(puts):
        values = []
        for k in range(points):
            rows = pl.ds((n * points + k) * SUB, SUB)
            re, im = grid[parity, rows, pl.ds(0, LANES)], grid[parity, rows, pl.ds(LANES, LANES)]
            w_re, w_im = twist[parity, 0, pl.ds(k, 1)], twist[parity, 1, pl.ds(k, 1)]
            values.append((re * w_re + im * w_im, im * w_re - re * w_im))
        for j, (re, im) in enumerate(small_dft(values, 1)):
            put(j, re, im)


def turned_by(angles):
    half = angles * 0.5
    square = half * half
    sin, cos = 0.0, 0.0
    for n in range(6, -1, -1):
        sin = sin * square + (-1.0) ** n / math.factorial(2 * n + 1)
        cos = cos * square + (-1.0) ** n / math.factorial(2 * n)
    sin = sin * half
    return 1.0 - 2.0 * sin * sin, 2.0 * sin * cos


def spread_kernel(x, table, turns, phases, out):
    count, slots, width = out.shape[0], out.shape[3], out.shape[4]
    sums = dot(table[...], thrice(jnp.concatenate([x[0, 0], x[0, 1]], axis=1), 0))
    sums = sums.reshape(count, 2, slots, 2 * width)
    turn_re, turn_im = turns[:, 0], turns[:, 1]
    for parity in range(2):
        lanes = slice(parity * width, (parity + 1) * width)
        ph_re, ph_im = phases[:, 2 * parity], phases[:, 2 * parity + 1]
        re, im = sums[:, 0, :, lanes], sums[:, 1, :, lanes]
        w_re = turn_re * ph_re - turn_im * ph_im
        w_im = turn_re * ph_im + turn_im * ph_re
        out[:, parity, 0] = re * w_re - im * w_im
        out[:, parity, 1] = re * w_im + im * w_re


def digits_swapped(tiles):
    lane = lax.broadcasted_iota(jnp.int32, tiles[0].shape, 1)
    step = 1
    while step < len(tiles):
        low_half = jnp.bitwise_and(lane, step) == 0
        swapped = list(tiles)
        for k in range(len(tiles)):
            if k & step == 0:
                first, second = tiles[k], tiles[k + step]
                swapped[k] = jnp.where(low_half, first, pltpu.roll(second, step, 1))
                swapped[k + step] = jnp.where(low_half, pltpu.roll(first, LANES - step, 1), second)
        tiles = swapped
        step *= 2
    return tiles


def chirp_kernel(place, angles, small, tables, out, sides, grid, held):
    twist, mirror, extra_turn = (small.at[n] for n in range(3))
    points = small.shape[3]
    blocks = angles.shape[1] // SUB
    for block in range(blocks):
        for side in range(2):
            rows = pl.ds(block * SUB, SUB)
            tiles = [angles[side, rows, pl.ds(k * LANES, LANES)] for k in range(points)]
            for k, value in enumerate(digits_swapped(tiles)):
                cos, sin = turned_by(value)
                cell = pl.ds(((2 * block + side) * points + k) * SUB, SUB)
                sides[cell, pl.ds(0, LANES)] = cos
                sides[cell, pl.ds(LANES, LANES)] = sin

    @pl.when(place[0] == 0)
    def _():
        slot = lax.broadcasted_iota(jnp.int32, (SUB, LANES), 0)
        lane = lax.broadcasted_iota(jnp.int32, (SUB, LANES), 1)
        alive = jnp.logical_or(slot > 0, lane > 0)
        for part in range(2):
            lanes = pl.ds(part * LANES, LANES)
            sides[pl.ds(0, SUB), lanes] = jnp.where(alive, sides[pl.ds(0, SUB), lanes], 0.0)

    for parity in range(2):
        puts = []
        for block in range(blocks):
            rows = pl.ds(block * SUB, SUB)
            for side in range(2):

                def put(j, re, im, block=block, rows=rows, parity=parity, side=side):
                    held[block, parity, side, 0, j] = re
                    held[block, parity, side, 1, j] = im
                    if side == 1:
                        sign = 1.0 - 2.0 * parity
                        m_re, m_im = mirror[parity, 0, pl.ds(j, 1)], mirror[parity, 1, pl.ds(j, 1)]
                        out[j, parity, 0, rows] = held[block, parity, 0, 0, j] + sign * (re * m_re + im * m_im)
                        out[j, parity, 1, rows] = held[block, parity, 0, 1, j] + sign * (re * m_im - im * m_re)

                puts.append(put)
        backward(sides[...], parity, twist, tables[parity], grid, puts)

    @pl.when(place[0] == 0)
    def _():
        keep = lax.broadcasted_iota(jnp.int32, (SUB, LANES), 0) > 0
        rows = pl.ds(0, SUB)
        for parity in range(2):
            for j in range(points):
                w_re, w_im = extra_turn[parity, 0, pl.ds(j, 1)], extra_turn[parity, 1, pl.ds(j, 1)]
                near = 2.0 * held[0, parity, 0, 0, j]
                far = 2.0 * (held[0, parity, 1, 0, j] * w_re + held[0, parity, 1, 1, j] * w_im)
                out[j, parity, 0, rows] = jnp.where(keep, out[j, parity, 0, rows], near)
                out[j, parity, 1, rows] = jnp.where(keep, out[j, parity, 1, rows], far)


def response_kernel(parts, turns_in, phases_in, back_table, table, turns, phases, out, packed):
    sources, slots = parts.shape[0], parts.shape[3]
    count, out_slots = out.shape[0], out.shape[4]
    depth = 2 * sources * slots

    @pl.when(pl.program_id(0) == 0)
    def _():
        for source in range(sources):
            t_re, t_im = turns_in[source, 0], turns_in[source, 1]
            for parity in range(2):
                ph_re, ph_im = phases_in[source, 2 * parity], phases_in[source, 2 * parity + 1]
                w_re = t_re * ph_re - t_im * ph_im
                w_im = t_re * ph_im + t_im * ph_re
                re, im = parts[source, parity, 0], parts[source, parity, 1]
                lanes = pl.ds(parity * LANES, LANES)
                pair = jnp.concatenate([re * w_re + im * w_im, im * w_re - re * w_im], axis=0)
                high, low = split(pair)
                for n, value in enumerate((high, low, high)):
                    packed[pl.ds(n * depth + 2 * source * slots, 2 * slots), lanes] = value

    taps = dot(back_table[...], packed[...])
    sums = dot(table[...], thrice(taps, 0)).reshape(count, 2, out_slots, 2 * LANES)
    turn_re, turn_im = turns[:, 0], turns[:, 1]
    for parity in range(2):
        lanes = slice(parity * LANES, (parity + 1) * LANES)
        ph_re, ph_im = phases[:, 2 * parity], phases[:, 2 * parity + 1]
        re, im = sums[:, 0, :, lanes], sums[:, 1, :, lanes]
        w_re = turn_re * ph_re - turn_im * ph_im
        w_im = turn_re * ph_im + turn_im * ph_re
        out[:, 0, parity, 0] = re * w_re - im * w_im
        out[:, 0, parity, 1] = re * w_im + im * w_re


def forward_kernel(x, twist, tables, out, grid):
    tiles = x.shape[5] // LANES
    size = out.shape[2]
    value_ats = []
    for n in range(x.shape[0]):

        def value_at(parity, j, n=n):
            group, tile = divmod(j, tiles)
            lanes = pl.ds(tile * LANES, LANES)
            return x[n, group, parity, 0, :, lanes], x[n, group, parity, 1, :, lanes]

        value_ats.append(value_at)
    upper, lower = forward(value_ats, twist, tables, grid)
    for n in range(x.shape[0]):
        out[n, 0] = upper[n * size : (n + 1) * size]
        out[n, 1] = lower[n * size : (n + 1) * size]


def apply_kernel(taps, spectrum, twist, tables, out, raw, response, past, sides, grid):
    step = pl.program_id(0)
    points = twist.shape[2]
    tiles = out.shape[5] // LANES
    size = points * SUB
    re_lanes, im_lanes = pl.ds(0, LANES), pl.ds(LANES, LANES)

    @pl.when(step == 0)
    def _():
        past[...] = jnp.zeros_like(past)

    @pl.when(step < 2)
    def _():
        value_ats = []
        for n in range(2):

            def value_at(parity, j, n=n):
                return taps[j, n, parity, 0], taps[j, n, parity, 1]

            value_ats.append(value_at)
        upper, lower = forward(value_ats, twist, tables, grid)
        for n in range(2):
            raw[2 * step + n, 0] = upper[n * size : (n + 1) * size]
            raw[2 * step + n, 1] = lower[n * size : (n + 1) * size]

    @pl.when(step == 1)
    def _():
        sign = 1.0 - 2.0 * (lax.broadcasted_iota(jnp.int32, (SUB, LANES), 0) % 2).astype(jnp.float32)
        for side in range(2):
            for k in range(points):
                rows = pl.ds(k * SUB, SUB)
                res = [raw[j, side, rows, re_lanes] for j in range(4)]
                ims = [raw[j, side, rows, im_lanes] for j in range(4)]
                for j in range(4):
                    response[j, side, rows, re_lanes] = res[j] - sign * ims[j - 1]
                    response[j, side, rows, im_lanes] = ims[j] + sign * res[j - 1]

    @pl.when(step >= 2)
    def _():
        window = [past.at[n] for n in range(3)] + [spectrum.at[n] for n in range(2)]
        for k in range(points):
            rows = pl.ds(k * SUB, SUB)
            sums = [[], []]
            for side in range(2):
                xs = [(ref[side, rows, re_lanes], ref[side, rows, im_lanes]) for ref in window]
                totals = [None, None]
                for j in range(4):
                    h_re, h_im = response[j, side, rows, re_lanes], response[j, side, rows, im_lanes]
                    for n in range(2):
                        x_re, x_im = xs[3 + n - j]
                        term = h_re * x_re - h_im * x_im, h_re * x_im + h_im * x_re
                        totals[n] = term if j == 0 else plus(totals[n], term)
                for n in range(2):
                    sums[n].append(totals[n])
            for n in range(2):
                for parity, value in enumerate((plus(*sums[n]), minus(*sums[n]))):
                    cell = pl.ds(n * size + k * SUB, SUB)
                    sides[parity, cell, re_lanes] = value[0]
                    sides[parity, cell, im_lanes] = value[1]
        for parity in range(2):
            puts = []
            for n in range(2):

                def put(j, re, im, n=n, parity=parity):
                    group, tile = divmod(j, tiles)
                    lanes = pl.ds(tile * LANES, LANES)
                    out[n, group, parity, 0, :, lanes] = re
                    out[n, group, parity, 1, :, lanes] = im

                puts.append(put)
            backward(sides[parity], parity, twist, tables[2 + parity], grid, puts)
        past[0] = past[2]
        past[1] = spectrum[0]
        past[2] = spectrum[1]


def gather_kernel(parts, turns, phases, table, out):
    count, slots, width = parts.shape[0], parts.shape[3], parts.shape[4]
    turn_re, turn_im = turns[:, 0], turns[:, 1]
    columns = []
    for parity in range(2):
        ph_re, ph_im = phases[:, 2 * parity], phases[:, 2 * parity + 1]
        w_re = turn_re * ph_re - turn_im * ph_im
        w_im = turn_re * ph_im + turn_im * ph_re
        re, im = parts[:, parity, 0], parts[:, parity, 1]
        pair = jnp.stack([re * w_re + im * w_im, im * w_re - re * w_im], axis=1)
        columns.append(pair.reshape(count * 2 * slots, width))
    sums = dot(table[...], thrice(jnp.concatenate(columns, axis=1), 0))
    for parity in range(2):
        out[0, parity] = sums[:, parity * width : (parity + 1) * width]


def whole(shape):
    return pl.BlockSpec(shape, lambda i, *_: (0,) * len(shape))


def call(kernel, name, grid, in_specs, out_specs, out_shape, scratch, flops, size, scalars=0):
    return pl.pallas_call(
        kernel,
        grid_spec=pltpu.PrefetchScalarGridSpec(
            num_scalar_prefetch=scalars,
            grid=(grid,),
            in_specs=in_specs,
            out_specs=out_specs,
            scratch_shapes=scratch,
        ),
        out_shape=jax.ShapeDtypeStruct(out_shape, jnp.float32),
        compiler_params=pltpu.CompilerParams(vmem_limit_bytes=VMEM, dimension_semantics=("arbitrary",)),
        cost_estimate=pl.CostEstimate(flops=int(flops), bytes_accessed=int(size), transcendentals=0),
        name=name,
    )


def exchange(values):
    return lax.all_to_all(values, ("seg", "fft"), split_axis=0, concat_axis=0, tiled=True)


def phase_pair(odd_rows, column, period):
    even = np.stack(turn(odd_rows * column, period), axis=-1)
    odd = np.stack(turn(odd_rows * (2 * column + 1), 2 * period), axis=-1)
    return np.concatenate([even, odd], axis=-1)


def per_device(voltage, chirp_phase):
    groups, segments = lax.axis_size("fft"), lax.axis_size("seg")
    group, segment = lax.axis_index("fft"), lax.axis_index("seg")
    count = groups * segments
    position = segment * groups + group
    quarter, width = voltage.shape[2], voltage.shape[3]
    row_count, half = 4 * quarter, 2 * quarter
    columns = width * groups
    points = columns // LANES
    total = row_count * columns
    short = total // 2
    slots = half // groups
    tile, wide = min(2 * LANES, width // 4), width // 2
    f32 = jnp.float32

    keys, lanes = np.arange(points), np.arange(LANES)
    twist = np.stack(
        [
            np.stack(turn(keys[:, None] * lanes[None, :], columns)),
            np.stack(turn(keys[:, None] * (2 * lanes[None, :] + 1), 2 * columns)),
        ]
    ).astype(np.float32)
    tables = []
    for cos, sin in (
        turn(lanes[:, None] * lanes[None, :], LANES),
        turn((2 * lanes[:, None] + 1) * lanes[None, :], 2 * LANES),
    ):
        tables.append(np.block([[cos, sin], [-sin, cos]]))
    column_tables = [twist, right_table(np.stack(tables + [table.T for table in tables]))]
    digit_order = (LANES // points * (lanes % points) + lanes // points).astype(np.int64)
    digit_order = np.concatenate([digit_order, LANES + digit_order])
    swapped_tables = right_table(np.stack([table.T[digit_order] for table in tables]))
    column_specs = [whole(table.shape) for table in column_tables]

    own_rows = max(SUB, quarter // count)
    odd_rows = 2 * np.arange(own_rows * count) + 1
    live = (odd_rows < 2 * quarter).astype(np.float64)
    cos, sin = turn(odd_rows[:, None] * np.arange(quarter)[None, :], 2 * half)
    row_table = np.stack([cos, sin], axis=1) * live[:, None, None]
    row_table = row_table.reshape(count, own_rows, 2, quarter).transpose(0, 2, 1, 3).reshape(-1, quarter)
    back_table = left_table(row_table.T / short)
    row_table = left_table(row_table)
    turns = np.stack(turn(odd_rows[:, None] * np.arange(width)[None, :], 2 * short))
    turns = turns.reshape(2, count, own_rows, width).transpose(1, 0, 2, 3).astype(np.float32)

    def row_phases(column_starts):
        table = phase_pair(odd_rows[None, :], column_starts[:, None], 2 * short)
        table = table.reshape(-1, count, own_rows, 4).transpose(0, 1, 3, 2)
        return jnp.asarray(table[..., None].astype(np.float32))

    phases = lax.dynamic_index_in_dim(row_phases(np.arange(groups) * width), group, 0, keepdims=False)

    chirp_slots = max(SUB, slots // segments)
    holders = slots // chirp_slots
    blocks = chirp_slots // SUB
    start = jnp.minimum(segment, holders - 1)
    place = jnp.stack([position, start]).astype(jnp.int32)
    every = LANES * keys[:, None] + lanes[None, :]
    extra_turn = np.stack(
        [np.stack(turn(half * every, total)), np.stack(turn(half * (2 * every + 1), 2 * total))]
    ).astype(np.float32)
    mirror = np.stack(
        [np.stack(turn(every, columns)), np.stack(turn((1 - columns) * (2 * every + 1), 2 * columns))]
    ).astype(np.float32)
    small = np.stack([twist, mirror, extra_turn])
    cells = (points * SUB, 2 * LANES)
    chirp_columns = call(
        chirp_kernel,
        "chirp_columns",
        1,
        [
            pl.BlockSpec((2, chirp_slots, columns), lambda i, place: (0, place[1], 0)),
            whole(small.shape),
            whole(swapped_tables.shape),
        ],
        whole((points, 2, 2, chirp_slots, LANES)),
        (points, 2, 2, chirp_slots, LANES),
        [
            pltpu.VMEM((2 * blocks * points * SUB, 2 * LANES), f32),
            pltpu.VMEM((2, 2 * blocks * points * SUB, 2 * LANES), f32),
            pltpu.VMEM((blocks, 2, 2, 2, points, SUB, LANES), f32),
        ],
        4e8 * blocks,
        3e6,
        scalars=1,
    )(place, chirp_phase, small, swapped_tables)
    if holders < segments:
        chirp_columns = jnp.where(segment < holders, chirp_columns, 0.0)
    if count > points:
        chirp_columns = jnp.pad(chirp_columns, ((0, count - points),) + ((0, 0),) * 4)
    chirp_parts = exchange(chirp_columns)[: holders * groups]

    rows = np.arange(half)
    order = rows.reshape(groups, holders, chirp_slots).transpose(1, 0, 2)
    chirp_turns = np.stack(turn(order[..., None] * lanes, total), axis=2).astype(np.float32)
    block_of = np.arange(points)
    chirp_phases = phase_pair(order[None], LANES * block_of[:, None, None, None], total)
    chirp_phases = chirp_phases.reshape(points, holders * groups, chirp_slots, 4).transpose(0, 1, 3, 2)
    chirp_phases = jnp.asarray(chirp_phases[..., None].astype(np.float32))
    chirp_turns = chirp_turns.reshape(holders * groups, 2, chirp_slots, LANES)
    cos, sin = turn(rows[None, :] * np.arange(row_count)[:, None], row_count)
    cos[:, 0] = 0.5
    sin[:, 0] = np.where(np.arange(row_count) % 2 == 0, 0.5, -0.5)
    taps_table = np.stack([cos, sin], axis=1).reshape(row_count, 2, groups, holders, chirp_slots) / total
    taps_table = taps_table.transpose(0, 3, 2, 1, 4).reshape(row_count, 2 * half)
    taps_table = left_table(taps_table)
    own_block = jnp.minimum(position, points - 1)
    own_chirp_phases = lax.dynamic_index_in_dim(chirp_phases, own_block, 0, keepdims=False)
    own_row_phases = lax.dynamic_index_in_dim(row_phases(block_of * LANES), own_block, 0, keepdims=False)
    response_shape = (count, 4, 2, 2, own_rows, LANES)
    response = call(
        response_kernel,
        "response",
        4,
        [
            whole(chirp_parts.shape),
            whole(chirp_turns.shape),
            whole(own_chirp_phases.shape),
            pl.BlockSpec((quarter, taps_table.shape[1]), lambda i: (i, 0)),
            whole(row_table.shape),
            pl.BlockSpec((count, 2, own_rows, LANES), lambda i: (0, 0, 0, 0)),
            whole(own_row_phases.shape),
        ],
        pl.BlockSpec((count, 1, 2, 2, own_rows, LANES), lambda i: (0, i, 0, 0, 0, 0)),
        response_shape,
        [pltpu.VMEM((6 * half, 2 * LANES), jnp.bfloat16)],
        5e9,
        1e7,
    )(chirp_parts, chirp_turns, own_chirp_phases, taps_table, row_table, turns, own_row_phases)
    taps = exchange(response)[:points]

    spread_shape = (count, 2, 2, own_rows, width)
    spread = call(
        spread_kernel,
        "spread",
        width // tile,
        [
            pl.BlockSpec((1, 2, quarter, tile), lambda c: (0, 0, 0, c)),
            whole(row_table.shape),
            pl.BlockSpec((count, 2, own_rows, tile), lambda c: (0, 0, 0, c)),
            whole(phases.shape),
        ],
        pl.BlockSpec((count, 2, 2, own_rows, tile), lambda c: (0, 0, 0, 0, c)),
        spread_shape,
        [],
        2e9,
        1e7,
    )(voltage, row_table, turns, phases)
    spread = exchange(spread).reshape(segments, groups, 2, 2, own_rows, width)

    pair_scratch = pltpu.VMEM((2, 2 * points * SUB, 2 * LANES), f32)
    spectrum = call(
        forward_kernel,
        "forward",
        segments // 2,
        [pl.BlockSpec((2, groups, 2, 2, own_rows, width), lambda s: (s, 0, 0, 0, 0, 0))] + column_specs,
        pl.BlockSpec((2, 2) + cells, lambda s: (s, 0, 0, 0)),
        (segments, 2) + cells,
        [pair_scratch],
        2e9,
        1e7,
    )(spread, *column_tables)

    def lagged(i):
        return jnp.maximum(i - 2, 0)

    packed = call(
        apply_kernel,
        "apply",
        segments // 2 + 2,
        [
            pl.BlockSpec((points, 2, 2, 2, own_rows, LANES), lambda i: (0, jnp.minimum(i, 1), 0, 0, 0, 0)),
            pl.BlockSpec((2, 2) + cells, lambda i: (lagged(i), 0, 0, 0)),
        ]
        + column_specs,
        pl.BlockSpec((2, groups, 2, 2, own_rows, width), lambda i: (lagged(i), 0, 0, 0, 0, 0)),
        (segments, groups, 2, 2, own_rows, width),
        [
            pltpu.VMEM((4, 2) + cells, f32),
            pltpu.VMEM((4, 2) + cells, f32),
            pltpu.VMEM((3, 2) + cells, f32),
            pair_scratch,
            pair_scratch,
        ],
        4e9,
        2e7,
    )(taps, spectrum, *column_tables)
    parts = exchange(packed.reshape(spread_shape))

    return call(
        gather_kernel,
        "gather",
        width // wide,
        [
            pl.BlockSpec((count, 2, 2, own_rows, wide), lambda c: (0, 0, 0, 0, c)),
            pl.BlockSpec((count, 2, own_rows, wide), lambda c: (0, 0, 0, c)),
            whole(phases.shape),
            whole(back_table.shape),
        ],
        pl.BlockSpec((1, 2, quarter, wide), lambda c: (0, 0, 0, c)),
        (1, 2, quarter, width),
        [],
        2e9,
        1e7,
    )(parts, turns, phases, back_table)


def solution(mesh):
    in_specs = (P("seg", None, None, "fft"), P(None, "fft", None))
    out_specs = P("seg", None, None, "fft")
    return jax.shard_map(per_device, mesh=mesh, in_specs=in_specs, out_specs=out_specs, check_vma=False)
```
